32 devices in a mesh: dp: 16 (over z, x, core), tensor: 2 (over y).
Axes of the slice: x: 2, y: 2, z: 4, core: 2. Of those that a mesh axis runs over, the one named last changes fastest.
Arguments:
- tokens: bfloat16 [16, 1024, 1152], P('dp', 'tensor'), may hold values from -6 to 6
- segments: int32 [16, 1024], P('dp'), may hold values from 0 to 3, as said below
- labels: int32 [16, 4], P('dp'), may hold values from 0 to 1000
- timesteps: int32 [16, 4], P('dp'), may hold values from 0 to 999
- class_table: float32 [1001, 1152], replicated, may hold values from -6 to 6
- time_weight: float32 [256, 1152], replicated, may hold values from -0.5 to 0.5
- ada_weight: bfloat16 [1152, 6912], P(None, 'tensor'), may hold values from -0.1875 to 0.1875
- qkv_weight: bfloat16 [1152, 3, 1152], P(None, None, 'tensor'), may hold values from -0.1875 to 0.1875
- proj_weight: bfloat16 [1152, 1152], P('tensor'), may hold values from -0.75 to 0.75
- up_weight: bfloat16 [1152, 4608], P(None, 'tensor'), may hold values from -0.1875 to 0.1875
- down_weight: bfloat16 [4608, 1152], P('tensor'), may hold values from -0.09375 to 0.09375
- cotangent: bfloat16 [16, 1024, 1152], P('dp', 'tensor'), may hold values from -6 to 6
Outputs:
- output: bfloat16 [16, 1024, 1152], P('dp', 'tensor')
- grad_tokens: bfloat16 [16, 1024, 1152], P('dp', 'tensor')
- grad_class_table: float32 [1001, 1152], replicated
- grad_time_weight: float32 [256, 1152], replicated
- grad_ada_weight: float32 [1152, 6912], P(None, 'tensor')
- grad_qkv_weight: float32 [1152, 3, 1152], P(None, None, 'tensor')
- grad_proj_weight: float32 [1152, 1152], P('tensor')
- grad_up_weight: float32 [1152, 4608], P(None, 'tensor')
- grad_down_weight: float32 [4608, 1152], P('tensor')
The draws below stay inside these ranges and needn't reach their ends.
Inputs may be any that keep to these rules, and one draw needn't show every extreme that they name: `segments`: slots of a pack are numbered from 0 by the samples present; each sample has 1024 or 256 tokens, the same number on each of the pack's blocks of 512 positions, where its tokens are consecutive and ids never fall within a block; the samples fill the pack; some pack holds only samples of 256 tokens and some only samples of 1024.
All inputs are finite; a program needn't handle non-finite values.
Results may differ from the reference program's by a relative error of at most 0.025.
The reference program's roundings to bfloat16 on the way count: a program that leaves them out, or rounds other values in their place, can miss the bound.
Values may be sent and summed in bfloat16 or wider, within the bound.
No kernel may reach another device: no remote copies, remote signals or barrier semaphores. Data moves between devices by JAX's collectives and lax.ppermute only.
A program may use at most 256 MiB of HBM per device.

```python
import math
import jax
import jax.numpy as jnp
from jax import lax

D = 1152
HEADS = 16
HEAD_DIM = 72
FF = 4608
CLASSES = 1001
FREQ = 256
STEPS = 1000
LONG = 1024
SHORT = 256
PACK = 1024
SHARD = 512
SLOTS = 4
PACKS = 16
ADA = 6912


def draw_segments(key, part):
    key = jax.random.fold_in(key, 11)
    units = PACK // SHORT
    ratio = LONG // SHORT
    most_long = PACK // LONG
    count_key, order_key, pick_key = jax.random.split(key, 3)
    long_counts = jax.random.randint(count_key, (PACKS,), 0, most_long + 1)
    chosen = jax.random.permutation(pick_key, PACKS)
    long_counts = long_counts.at[chosen[0]].set(most_long).at[chosen[1]].set(0)
    sample_counts = long_counts + units - long_counts * ratio
    priority = jax.vmap(lambda subkey: jax.random.permutation(subkey, units))(jax.random.split(order_key, PACKS))
    slot_index = jnp.arange(units, dtype=jnp.int32)
    alive_slots = slot_index[None, :] < sample_counts[:, None]
    beneath = (priority[:, None, :] < priority[:, :, None]) & alive_slots[:, None, :]
    standing = jnp.sum(beneath.astype(jnp.int32), axis=2)
    is_long = standing < long_counts[:, None]
    slot_units = jnp.where(alive_slots, jnp.where(is_long, ratio, 1), 0)
    slot_ends = jnp.cumsum(slot_units, axis=1)
    unit_slot = jnp.sum((slot_ends[:, None, :] <= slot_index[None, :, None]).astype(jnp.int32), axis=2)
    positions = jnp.arange(PACK, dtype=jnp.int32) % SHARD
    unit_of_pos = positions // (SHARD // units)
    return jnp.take(unit_slot, unit_of_pos, axis=1).astype(jnp.int32)


def with_ends(array, own_key, low, high):
    longest = array.shape.index(max(array.shape))
    spots = []
    for shift in (0, 1):
        where = [jax.random.randint(jax.random.fold_in(own_key, axis), (), 0, length) for axis, length in enumerate(array.shape)]
        where[longest] = (where[longest] + shift) % array.shape[longest]
        spots.append(tuple(where))
    return array.at[spots[0]].set(low).at[spots[1]].set(high)


def block_levels(stream_key, extent, shards, least, top_value):
    gain, own = 1.0, jax.random.fold_in(stream_key, 6)
    for position, parts in shards:
        draws = jnp.exp(jax.random.uniform(jax.random.fold_in(own, position), (parts,), jnp.float32, least / len(shards), top_value / len(shards)))
        gain = gain * jnp.repeat(draws, extent[position] // parts).reshape([-1 if axis == position else 1 for axis in range(len(extent))])
    return gain


def noise(own_key, shape, width, limit, cuts=(), kind=jnp.bfloat16):
    values = jax.random.normal(own_key, shape, jnp.float32) * width
    if len(cuts) > 0:
        values = block_levels(own_key, shape, cuts, -0.22, 0.18) * values
    return jnp.clip(values, min=-limit, max=limit).astype(kind)


def setup_inputs(seed: int = 0) -> dict:
    streams_of = jax.random.split(jax.random.key(seed), 13)
    tokens = noise(streams_of[0], (PACKS, PACK, D), 1.0, 6.0, ((0, 16), (1, 2)))
    segments = draw_segments(jax.random.fold_in(streams_of[12], 71), 0)
    labels = with_ends(jax.random.randint(streams_of[2], (PACKS, SLOTS), 0, CLASSES), jax.random.fold_in(streams_of[2], 1), 0, CLASSES - 1).astype(jnp.int32)
    timesteps = with_ends(jax.random.randint(streams_of[3], (PACKS, SLOTS), 0, STEPS), jax.random.fold_in(streams_of[3], 1), 0, STEPS - 1).astype(jnp.int32)
    class_table = noise(streams_of[4], (CLASSES, D), 1.0, 6.0, (), jnp.float32)
    time_weight = noise(streams_of[5], (FREQ, D), (FREQ // 2) ** -0.5, 0.5, (), jnp.float32)
    ada_weight = noise(streams_of[6], (D, ADA), D ** -0.5, 0.1875, ((1, 2),))
    qkv_weight = noise(streams_of[7], (D, 3, D), D ** -0.5, 0.1875, ((2, 2),))
    proj_weight = noise(streams_of[8], (D, D), (D // 16) ** -0.5, 0.75, ((0, 2),))
    up_weight = noise(streams_of[9], (D, FF), D ** -0.5, 0.1875, ((1, 2),))
    down_weight = noise(streams_of[10], (FF, D), FF ** -0.5, 0.09375, ((0, 2),))
    cotangent = noise(streams_of[11], (PACKS, PACK, D), 1.0, 6.0, ((0, 16), (1, 2)))
    return dict(tokens=tokens, segments=segments, labels=labels, timesteps=timesteps, class_table=class_table, time_weight=time_weight, ada_weight=ada_weight, qkv_weight=qkv_weight, proj_weight=proj_weight, up_weight=up_weight, down_weight=down_weight, cotangent=cotangent)


HIGH = lax.Precision.HIGHEST

@jax.custom_vjp
def low(v):
    return lax.optimization_barrier(v.astype(jnp.bfloat16)).astype(jnp.float32)

@jax.custom_vjp
def low_back(v):
    return v

def low_keep(v):
    return (low(v), None)

def low_pass(kept, grad):
    return (grad,)

def back_keep(v):
    return (v, None)

def back_low(kept, grad):
    return (low(grad),)
low.defvjp(low_keep, low_pass)
low_back.defvjp(back_keep, back_low)

def features(steps_f):
    half = FREQ // 2
    freqs = jnp.exp(-math.log(10000.0) * jnp.arange(half, dtype=jnp.float32) / half)
    angles = steps_f[:, None] * freqs[None, :]
    return jnp.concatenate([jnp.cos(angles), jnp.sin(angles)], axis=1)

def normalize(values):
    average = lax.optimization_barrier(jnp.mean(values, axis=-1, keepdims=True))
    centred = values - average
    return centred * lax.rsqrt(lax.optimization_barrier(jnp.mean(centred * centred, axis=-1, keepdims=True)) + 1e-06)

def pack_forward(tokens_f, seg_ids, label_ids, step_ids, class_table, time_weight, ada_weight, qkv_weight, proj_weight, up_weight, down_weight):
    label_hot = (label_ids[:, None] == jnp.arange(CLASSES, dtype=jnp.int32)[None, :]).astype(jnp.float32)
    condition = jnp.dot(label_hot, class_table, precision=HIGH) + jnp.dot(features(step_ids.astype(jnp.float32)), time_weight, precision=HIGH)
    modulation = low_back(jnp.dot(low(jax.nn.silu(condition)), ada_weight, precision=HIGH))
    slot_hot = (seg_ids[:, None] == jnp.arange(SLOTS, dtype=jnp.int32)[None, :]).astype(jnp.float32)
    per_token = jnp.dot(slot_hot, modulation, precision=HIGH)
    shift_one, scale_one, gate_one, shift_two, scale_two, gate_two = jnp.split(per_token, 6, axis=1)
    modulated_one = low(normalize(tokens_f) * (1.0 + scale_one) + shift_one)
    qkv = low(low_back(jnp.dot(modulated_one, qkv_weight.reshape(D, 3 * D), precision=HIGH)))
    qkv = qkv.reshape(PACK, 3, HEADS, HEAD_DIM)
    queries = jnp.transpose(qkv[:, 0], (1, 0, 2))
    keys = jnp.transpose(qkv[:, 1], (1, 0, 2))
    values = jnp.transpose(qkv[:, 2], (1, 0, 2))
    block = min(512, PACK)
    query_blocks = queries.reshape(HEADS, PACK // block, block, HEAD_DIM).transpose(1, 0, 2, 3)
    seg_blocks = seg_ids.reshape(PACK // block, block)
    scale_factor = 1.0 / math.sqrt(HEAD_DIM)

    def attend(pair):
        query_block, seg_block = pair
        scores = low_back(jnp.einsum('hqd,hkd->hqk', query_block, keys, precision=HIGH) * scale_factor)
        same = (seg_block[:, None] == seg_ids[None, :])[None]
        scores = jnp.where(same, scores, -1e+30)
        shifted = scores - lax.optimization_barrier(jnp.max(scores, axis=-1, keepdims=True))
        exps = jnp.exp(shifted)
        weights = low(exps / lax.optimization_barrier(jnp.sum(exps, axis=-1, keepdims=True)))
        return jnp.einsum('hqk,hkd->hqd', weights, values, precision=HIGH)
    outputs = lax.map(jax.checkpoint(attend), (query_blocks, seg_blocks))
    attended = low(low_back(outputs.transpose(0, 2, 1, 3).reshape(PACK, D)))
    branch_one = low_back(jnp.dot(attended, proj_weight, precision=HIGH))
    halfway = tokens_f + gate_one * branch_one
    modulated_two = low(normalize(halfway) * (1.0 + scale_two) + shift_two)
    hidden = low_back(jnp.dot(modulated_two, up_weight, precision=HIGH))
    active = low(jax.nn.gelu(hidden, approximate=True))
    branch_two = low_back(jnp.dot(active, down_weight, precision=HIGH))
    return halfway + gate_two * branch_two

def reference(tokens, segments, labels, timesteps, class_table, time_weight, ada_weight, qkv_weight, proj_weight, up_weight, down_weight, cotangent):
    tokens_f = tokens.astype(jnp.float32)
    weights = (class_table.astype(jnp.float32), time_weight.astype(jnp.float32), ada_weight.astype(jnp.float32), qkv_weight.astype(jnp.float32), proj_weight.astype(jnp.float32), up_weight.astype(jnp.float32), down_weight.astype(jnp.float32))

    def forward(tokens_in, weight_set):

        def one_pack(item):
            return pack_forward(item[0], item[1], item[2], item[3], *weight_set)
        return lax.map(jax.checkpoint(one_pack), (tokens_in, segments, labels, timesteps))
    result, pullback = jax.vjp(forward, tokens_f, weights)
    grad_input, grad_weights = pullback(cotangent.astype(jnp.float32))
    return (result.astype(jnp.bfloat16), grad_input.astype(jnp.bfloat16), grad_weights[0], grad_weights[1], grad_weights[2], grad_weights[3], grad_weights[4], grad_weights[5], grad_weights[6])
```

```python
import functools
import math

import jax
import jax.numpy as jnp
from jax import lax
from jax.experimental import pallas as pl
from jax.experimental.pallas import tpu as pltpu
from jax.sharding import PartitionSpec as P

HEAD_DIM = 72
SHORT = 256
HIGH = lax.Precision.HIGHEST
F32 = jnp.float32
BF16 = jnp.bfloat16
SCALE = 1.0 / math.sqrt(HEAD_DIM)
SCALE_LOG2 = SCALE * math.log2(math.e)


def dot(left, right, left_dim, right_dim, precision=None):
    return lax.dot_general(
        left,
        right,
        (((left_dim,), (right_dim,)), ((), ())),
        precision=precision,
        preferred_element_type=F32,
    )


def features(steps_f, width_total):
    half = width_total // 2
    freqs = jnp.exp(-math.log(10000.0) * jnp.arange(half, dtype=F32) / half)
    angles = steps_f[:, None] * freqs[None, :]
    return jnp.concatenate([jnp.cos(angles), jnp.sin(angles)], axis=1)


def normalize(values):
    average = jnp.mean(values, axis=-1, keepdims=True)
    centred = values - average
    inverse = lax.rsqrt(jnp.mean(centred * centred, axis=-1, keepdims=True) + 1e-06)
    return centred * inverse, inverse


def norm_back(grad_normed, normed, inverse):
    first = jnp.mean(grad_normed, axis=-1, keepdims=True)
    second = jnp.mean(grad_normed * normed, axis=-1, keepdims=True)
    return inverse * (grad_normed - first - normed * second)


def gelu_parts(x):
    root = math.sqrt(2.0 / math.pi)
    square = x * x
    bent = jnp.tanh(root * x * (1.0 + 0.044715 * square))
    half = 0.5 * (1.0 + bent)
    slope = half + 0.5 * x * (1.0 - bent * bent) * root * (1.0 + 3 * 0.044715 * square)
    return x * half, slope


def attend_kernel(block, q_ref, k_ref, v_ref, bias_ref, hot_ref, o_ref, lse_ref):
    tokens = q_ref.shape[2]
    query = jnp.concatenate([q_ref[0], bias_ref[...]], axis=0)
    key = jnp.concatenate([k_ref[0], hot_ref[...]], axis=0).T
    value = v_ref[0]
    for start in range(0, tokens, block):
        part = slice(start, start + block)
        scores = dot(key, query[:, part], 1, 0)
        top = jnp.max(scores, axis=0, keepdims=True) * SCALE_LOG2
        exps = jnp.exp2(scores * SCALE_LOG2 - top)
        total = jnp.sum(exps, axis=0, keepdims=True)
        out = dot(value, exps.astype(BF16), 1, 0)
        o_ref[0, :, part] = (out / total).astype(BF16)
        lse_ref[0, :, part] = top + jnp.log2(total)


def attend_back_kernel(
    block, q_ref, k_ref, v_ref, bias_ref, hot_ref, o_ref, do_ref, lse_ref, grad_ref
):
    tokens = q_ref.shape[2]
    query = jnp.concatenate([q_ref[0], bias_ref[...]], axis=0)
    key = jnp.concatenate([k_ref[0], hot_ref[...]], axis=0).T
    value = v_ref[0].T
    query_rows = q_ref[0].T
    grad_out = do_ref[0]
    grad_rows = grad_out.T
    delta = jnp.sum(grad_out.astype(F32) * o_ref[0].astype(F32), axis=0, keepdims=True)
    lse = lse_ref[0]
    grad_key = grad_value = None
    for start in range(0, tokens, block):
        part = slice(start, start + block)
        scores = dot(key, query[:, part], 1, 0)
        probs = jnp.exp2(scores * SCALE_LOG2 - lse[:, part])
        grad_probs = dot(value, grad_out[:, part], 1, 0)
        grad_scores = (probs * (grad_probs - delta[:, part])).astype(BF16)
        value_term = dot(probs.astype(BF16), grad_rows[part], 1, 0)
        key_term = dot(grad_scores, query_rows[part], 1, 0)
        grad_value = value_term if grad_value is None else grad_value + value_term
        grad_key = key_term if grad_key is None else grad_key + key_term
        grad_ref[0, 0, :, part] = (dot(k_ref[0], grad_scores, 1, 0) * SCALE).astype(BF16)
    grad_ref[1, 0] = (grad_key * SCALE).astype(BF16).T
    grad_ref[2, 0] = grad_value.astype(BF16).T


def head_spec(tokens, offset):
    return pl.BlockSpec((1, HEAD_DIM, tokens), lambda head: (head + offset, 0, 0))


def whole_spec(shape):
    return pl.BlockSpec(shape, lambda head: (0,) * len(shape))


def row_spec(tokens):
    return pl.BlockSpec((1, 1, tokens), lambda head: (head, 0, 0))


def attend(qkv, bias, hot, first, count):
    heads = qkv.shape[0] // 3
    tokens = qkv.shape[2]
    block = min(tokens, (1 << 20) // tokens)
    work = count * tokens * tokens
    return pl.pallas_call(
        functools.partial(attend_kernel, block),
        grid=(count,),
        in_specs=[
            head_spec(tokens, first),
            head_spec(tokens, heads + first),
            head_spec(tokens, 2 * heads + first),
            whole_spec(bias.shape),
            whole_spec(hot.shape),
        ],
        out_specs=[head_spec(tokens, 0), row_spec(tokens)],
        out_shape=[
            jax.ShapeDtypeStruct((count, HEAD_DIM, tokens), BF16),
            jax.ShapeDtypeStruct((count, 1, tokens), F32),
        ],
        compiler_params=pltpu.CompilerParams(vmem_limit_bytes=48 << 20),
        cost_estimate=pl.CostEstimate(
            flops=2400 * work, bytes_accessed=8 * count * HEAD_DIM * tokens, transcendentals=work
        ),
    )(qkv, qkv, qkv, bias, hot)


def attend_back(qkv, bias, hot, out, grad_out, lse, first, count):
    heads = qkv.shape[0] // 3
    tokens = qkv.shape[2]
    block = min(tokens, (1 << 19) // tokens)
    work = count * tokens * tokens
    return pl.pallas_call(
        functools.partial(attend_back_kernel, block),
        grid=(count,),
        in_specs=[
            head_spec(tokens, first),
            head_spec(tokens, heads + first),
            head_spec(tokens, 2 * heads + first),
            whole_spec(bias.shape),
            whole_spec(hot.shape),
            head_spec(tokens, first),
            head_spec(tokens, first),
            row_spec(tokens),
        ],
        out_specs=pl.BlockSpec((3, 1, HEAD_DIM, tokens), lambda head: (0, head, 0, 0)),
        out_shape=jax.ShapeDtypeStruct((3, count, HEAD_DIM, tokens), BF16),
        compiler_params=pltpu.CompilerParams(vmem_limit_bytes=56 << 20),
        cost_estimate=pl.CostEstimate(
            flops=3200 * work, bytes_accessed=16 * count * HEAD_DIM * tokens, transcendentals=work
        ),
    )(qkv, qkv, qkv, bias, hot, out, grad_out, lse)


def block_step(
    dp_size,
    tensor_size,
    tokens,
    segments,
    labels,
    timesteps,
    class_table,
    time_weight,
    ada_weight,
    qkv_weight,
    proj_weight,
    up_weight,
    down_weight,
    cotangent,
):
    pair = tensor_size == 2
    position = lax.axis_index("tensor")
    own_low = tokens[0]
    shard, width = own_low.shape
    pack = segments.shape[1]
    slot_count = labels.shape[1]
    class_count = class_table.shape[0]
    freq_width = time_weight.shape[0]
    local_width = qkv_weight.shape[2]
    heads = local_width // HEAD_DIM
    chunk = shard * SHORT // pack

    def swap(x):
        return lax.ppermute(x, "tensor", [(0, 1), (1, 0)])

    def gather(x, axis):
        if pair:
            return jnp.concatenate([x, swap(x)], axis=axis)
        return lax.all_gather(x, "tensor", axis=axis, tiled=True)

    def own_rows(x):
        if pair:
            return x[:shard]
        return lax.dynamic_slice_in_dim(x, position * shard, shard, 0)

    def summed_rows(make):
        if pair:
            away = make(shard, pack).astype(BF16)
            return make(0, shard) + swap(away).astype(F32)
        whole = make(0, pack).astype(BF16)
        return lax.psum_scatter(whole, "tensor", scatter_dimension=0, tiled=True).astype(F32)

    def across(x):
        if pair:
            return jnp.concatenate([swap(x[:, shard:]), swap(x[:, :shard])], axis=1)
        return lax.all_gather(x, "tensor", axis=0, tiled=True)

    def sum_dp(parts):
        return [lax.psum(p.astype(BF16), "dp").astype(F32) for p in parts]

    tokens_low = gather(own_low, 0)
    proj_all = gather(proj_weight, 0)
    grad_low = gather(cotangent[0], 0)
    labels_all = lax.all_gather(labels[0], "dp", axis=0, tiled=True)
    steps_all = lax.all_gather(timesteps[0], "dp", axis=0, tiled=True)

    seg = segments[0]
    if pair:
        seg = jnp.where(position == 0, seg, jnp.roll(seg, shard))
    chunk_seg = seg[::chunk]
    slots = jnp.arange(slot_count, dtype=jnp.int32)
    chunk_hot = (chunk_seg[:, None] == slots[None, :]).astype(F32)
    mask_rows = -(-slot_count // 8) * 8
    same = jnp.arange(mask_rows, dtype=jnp.int32)[:, None] == seg[None, :]
    hot = same.astype(BF16)
    bias = jnp.where(same, 0.0, -1e30).astype(BF16)

    rows = [lax.dynamic_slice_in_dim(class_table, labels[0, i], 1, 0) for i in range(slot_count)]
    condition = jnp.concatenate(rows, axis=0) + dot(
        features(timesteps[0].astype(F32), freq_width), time_weight, 1, 0, HIGH
    )
    act_low = jax.nn.silu(condition).astype(BF16)
    mod_part = dot(act_low, ada_weight, 1, 0)
    if pair:
        mod_away = swap(mod_part)
        modulation = jnp.where(
            position == 0,
            jnp.concatenate([mod_part, mod_away], axis=1),
            jnp.concatenate([mod_away, mod_part], axis=1),
        )
    else:
        modulation = lax.all_gather(mod_part, "tensor", axis=1, tiled=True)
    condition_all = lax.all_gather(condition, "dp", axis=0, tiled=True)
    per_chunk = dot(chunk_hot, modulation, 1, 0, HIGH)
    mods = [m[:, None, :] for m in jnp.split(per_chunk, 6, axis=1)]
    shift_one, scale_one, gate_one, shift_two, scale_two, gate_two = mods
    own_chunks = shard // chunk

    def chunked(x):
        return x.reshape(x.shape[0] // chunk, chunk, x.shape[1])

    def flat(x):
        return x.reshape(x.shape[0] * chunk, x.shape[2])

    def own_chunk(m):
        if pair:
            return m[:own_chunks]
        return lax.dynamic_slice_in_dim(m, position * own_chunks, own_chunks, 0)

    tokens_f = chunked(tokens_low.astype(F32))
    normed_one, _ = normalize(tokens_f)
    inputs_one = flat((normed_one * (1.0 + scale_one) + shift_one).astype(BF16))
    qkv_flat = qkv_weight.reshape(width, 3 * local_width)
    qkv = dot(qkv_flat, inputs_one, 0, 1).astype(BF16).reshape(3 * heads, HEAD_DIM, pack)
    out, lse = attend(qkv, bias, hot, 0, heads)
    out_flat = out.reshape(local_width, pack)
    out_other = across(out_flat)
    if pair:
        branch_one = dot(out_flat, proj_all[:local_width], 0, 0) + dot(
            out_other, proj_all[local_width:], 0, 0
        )
    else:
        branch_one = dot(out_other, proj_all, 0, 0)
    branch_one = chunked(branch_one)
    halfway = tokens_f + gate_one * branch_one
    normed_two, inverse_two = normalize(halfway)
    inputs_two = flat((normed_two * (1.0 + scale_two) + shift_two).astype(BF16))

    hidden = dot(inputs_two, up_weight, 1, 0)
    active, slope = gelu_parts(hidden)
    active = active.astype(BF16)
    slope = slope.astype(BF16)
    grad_branch_two = flat((chunked(grad_low.astype(F32)) * gate_two).astype(BF16))
    grad_down = dot(active, grad_branch_two, 0, 0)
    grad_active = dot(grad_branch_two, down_weight, 1, 1)
    grad_hidden = (grad_active * slope.astype(F32)).astype(BF16)
    grad_up = dot(inputs_two, grad_hidden, 0, 0)
    grad_mod_two = chunked(summed_rows(lambda a, b: dot(grad_hidden[a:b], up_weight, 1, 1)))
    branch_two = chunked(summed_rows(lambda a, b: dot(active[a:b], down_weight, 1, 0)))
    own_halfway = chunked(own_rows(flat(halfway)))
    own_branch_one = chunked(own_rows(flat(branch_one)))
    own_normed_two, own_inverse_two = normalize(own_halfway)
    grad_out = chunked(cotangent[0].astype(F32))
    result = own_halfway + own_chunk(gate_two) * branch_two
    grad_gate_two = grad_out * branch_two
    grad_halfway = grad_out + norm_back(
        grad_mod_two * (1.0 + own_chunk(scale_two)), own_normed_two, own_inverse_two
    )
    grad_gate_one = grad_halfway * own_branch_one
    grad_branch_one = flat((grad_halfway * own_chunk(gate_one)).astype(BF16))

    if pair:
        grad_att_own = dot(proj_all[:local_width], grad_branch_one, 1, 1).astype(BF16)
        grad_att_away = dot(proj_all[local_width:], grad_branch_one, 1, 1).astype(BF16)
        grad_att = jnp.concatenate([grad_att_own, swap(grad_att_away)], axis=1)
        grads_one = gather(grad_branch_one, 0)
    else:
        grads_one = gather(grad_branch_one, 0)
        grad_att = dot(proj_weight, grads_one, 1, 1).astype(BF16)
    grad_proj = dot(out_flat, grads_one, 1, 0)
    grad_qkv = attend_back(
        qkv, bias, hot, out, grad_att.reshape(heads, HEAD_DIM, pack), lse, 0, heads
    ).reshape(3 * local_width, pack)
    grad_qkv_weight = dot(inputs_one, grad_qkv, 0, 1).reshape(width, 3, local_width)
    grad_mod_one = chunked(summed_rows(lambda a, b: dot(grad_qkv[:, a:b], qkv_flat, 0, 1)))
    own_normed_one, own_inverse_one = normalize(chunked(own_low.astype(F32)))
    grad_input = grad_halfway + norm_back(
        grad_mod_one * (1.0 + own_chunk(scale_one)), own_normed_one, own_inverse_one
    )

    terms = [
        grad_mod_one,
        grad_mod_one * own_normed_one,
        grad_gate_one,
        grad_mod_two,
        grad_mod_two * own_normed_two,
        grad_gate_two,
    ]
    chunk_terms = jnp.concatenate([jnp.sum(t, axis=1) for t in terms], axis=1)
    slot_terms = dot(own_chunk(chunk_hot), chunk_terms, 0, 0, HIGH).astype(BF16)
    if pair:
        half = slot_terms.shape[1] // 2
        low, high = slot_terms[:, :half], slot_terms[:, half:]
        keep = jnp.where(position == 0, low, high)
        away = jnp.where(position == 0, high, low)
        grad_modulation = (keep.astype(F32) + swap(away).astype(F32)).astype(BF16)
    else:
        grad_modulation = lax.psum_scatter(
            slot_terms, "tensor", scatter_dimension=1, tiled=True
        )
    grad_mod_all = lax.all_gather(grad_modulation, "dp", axis=0, tiled=True)
    act_all = jax.nn.silu(condition_all).astype(BF16)
    grad_ada = dot(act_all, grad_mod_all, 0, 0)
    cond_part = dot(grad_mod_all, ada_weight, 1, 1).astype(BF16)
    if pair:
        grad_act = cond_part.astype(F32) + swap(cond_part).astype(F32)
    else:
        grad_act = lax.psum(cond_part, "tensor").astype(F32)
    grad_condition = jax.vjp(jax.nn.silu, condition_all)[1](grad_act)[0]
    classes = jnp.arange(class_count, dtype=jnp.int32)
    label_hot = (labels_all[:, None] == classes[None, :]).astype(F32)
    grad_class = dot(label_hot, grad_condition, 0, 0, HIGH)
    grad_time = dot(features(steps_all.astype(F32), freq_width), grad_condition, 0, 0, HIGH)

    grad_up, grad_down = sum_dp([grad_up, grad_down])
    last, grad_qkv_weight, _ = lax.optimization_barrier((grad_proj, grad_qkv_weight, grad_up[0, 0]))
    grad_proj, grad_qkv_weight = sum_dp([last, grad_qkv_weight])
    return (
        flat(result).astype(BF16)[None],
        flat(grad_input).astype(BF16)[None],
        grad_class,
        grad_time,
        grad_ada,
        grad_qkv_weight,
        grad_proj,
        grad_up,
        grad_down,
    )


def solution(mesh):
    return jax.shard_map(
        functools.partial(block_step, mesh.shape["dp"], mesh.shape["tensor"]),
        mesh=mesh,
        in_specs=(
            P("dp", "tensor", None),
            P("dp", None),
            P("dp", None),
            P("dp", None),
            P(),
            P(),
            P(None, "tensor"),
            P(None, None, "tensor"),
            P("tensor", None),
            P(None, "tensor"),
            P("tensor", None),
            P("dp", "tensor", None),
        ),
        out_specs=(
            P("dp", "tensor", None),
            P("dp", "tensor", None),
            P(),
            P(),
            P(None, "tensor"),
            P(None, None, "tensor"),
            P("tensor", None),
            P(None, "tensor"),
            P("tensor", None),
        ),
        check_vma=False,
    )
```

```python
import functools
import math

import jax
import jax.numpy as jnp
from jax import lax
from jax.experimental import pallas as pl
from jax.experimental.pallas import tpu as pltpu
from jax.sharding import PartitionSpec as P

HEAD_DIM = 72
SHORT = 256
HIGH = lax.Precision.HIGHEST
F32 = jnp.float32
BF16 = jnp.bfloat16
SCALE = 1.0 / math.sqrt(HEAD_DIM)
SCALE_LOG2 = SCALE * math.log2(math.e)


def dot(left, right, left_dim, right_dim, precision=None):
    return lax.dot_general(
        left,
        right,
        (((left_dim,), (right_dim,)), ((), ())),
        precision=precision,
        preferred_element_type=F32,
    )


def features(steps_f, width_total):
    half = width_total // 2
    freqs = jnp.exp(-math.log(10000.0) * jnp.arange(half, dtype=F32) / half)
    angles = steps_f[:, None] * freqs[None, :]
    return jnp.concatenate([jnp.cos(angles), jnp.sin(angles)], axis=1)


def contract_rows(left, right):
    return dot(left, right, 0, 0)


def contract_exact(left, right):
    return dot(left, right, 0, 0, HIGH)


def times_transposed(left, right):
    return dot(left, right, 1, 1)


def normalize(values):
    average = jnp.mean(values, axis=-1, keepdims=True)
    centred = values - average
    inverse = lax.rsqrt(jnp.mean(centred * centred, axis=-1, keepdims=True) + 1e-06)
    return centred * inverse, inverse


def norm_back(grad_normed, normed, inverse):
    first = jnp.mean(grad_normed, axis=-1, keepdims=True)
    second = jnp.mean(grad_normed * normed, axis=-1, keepdims=True)
    return inverse * (grad_normed - first - normed * second)


def gelu_parts(x):
    root = math.sqrt(2.0 / math.pi)
    square = x * x
    bent = jnp.tanh(root * x * (1.0 + 0.044715 * square))
    half = 0.5 * (1.0 + bent)
    slope = half + 0.5 * x * (1.0 - bent * bent) * root * (1.0 + 3 * 0.044715 * square)
    return x * half, slope


def joined(own, other):
    return jnp.concatenate([own[0], other[0]], axis=1)


def attend_kernel(block, q0, q1, k0, k1, v0, v1, bias_ref, hot_ref, o_ref, lse_ref):
    tokens = o_ref.shape[2]
    query = jnp.concatenate([joined(q0, q1), bias_ref[...]], axis=0)
    key = jnp.concatenate([joined(k0, k1), hot_ref[...]], axis=0).T
    value = joined(v0, v1)
    for start in range(0, tokens, block):
        part = slice(start, start + block)
        scores = dot(key, query[:, part], 1, 0)
        top = jnp.max(scores, axis=0, keepdims=True) * SCALE_LOG2
        exps = jnp.exp2(scores * SCALE_LOG2 - top)
        total = jnp.sum(exps, axis=0, keepdims=True)
        out = dot(value, exps.astype(BF16), 1, 0)
        o_ref[0, :, part] = (out / total).astype(BF16)
        lse_ref[0, :, part] = top + jnp.log2(total)


def attend_back_kernel(
    block, q0, q1, k0, k1, v0, v1, bias_ref, hot_ref, o_ref, do0, do1, lse_ref, grad_ref
):
    tokens = o_ref.shape[2]
    query_all, key_all = joined(q0, q1), joined(k0, k1)
    query = jnp.concatenate([query_all, bias_ref[...]], axis=0)
    key = jnp.concatenate([key_all, hot_ref[...]], axis=0).T
    value = joined(v0, v1).T
    query_rows = query_all.T
    grad_out = joined(do0, do1)
    grad_rows = grad_out.T
    delta = jnp.sum(grad_out.astype(F32) * o_ref[0].astype(F32), axis=0, keepdims=True)
    lse = lse_ref[0]
    grad_key = grad_value = None
    for start in range(0, tokens, block):
        part = slice(start, start + block)
        scores = dot(key, query[:, part], 1, 0)
        probs = jnp.exp2(scores * SCALE_LOG2 - lse[:, part])
        grad_probs = dot(value, grad_out[:, part], 1, 0)
        grad_scores = (probs * (grad_probs - delta[:, part])).astype(BF16)
        value_term = dot(probs.astype(BF16), grad_rows[part], 1, 0)
        key_term = dot(grad_scores, query_rows[part], 1, 0)
        grad_value = value_term if grad_value is None else grad_value + value_term
        grad_key = key_term if grad_key is None else grad_key + key_term
        grad_ref[0, 0, :, part] = (dot(key_all, grad_scores, 1, 0) * SCALE).astype(BF16)
    grad_ref[1, 0] = (grad_key * SCALE).astype(BF16).T
    grad_ref[2, 0] = grad_value.astype(BF16).T


def head_spec(tokens, offset):
    return pl.BlockSpec((1, HEAD_DIM, tokens), lambda head: (head + offset, 0, 0))


def whole_spec(shape):
    return pl.BlockSpec(shape, lambda head: (0,) * len(shape))


def row_spec(tokens):
    return pl.BlockSpec((1, 1, tokens), lambda head: (head, 0, 0))


SMALL = pl.CostEstimate(flops=1 << 20, bytes_accessed=1 << 20, transcendentals=0)


def attend(own, other, bias, hot, first, count):
    heads = own.shape[0] // 3
    part = own.shape[2]
    tokens = part + other.shape[2]
    in_specs = [
        head_spec(part, component * heads + first) for component in range(3) for _ in range(2)
    ]
    return pl.pallas_call(
        functools.partial(attend_kernel, min(tokens, (1 << 20) // tokens)),
        grid=(count,),
        in_specs=in_specs + [whole_spec(bias.shape), whole_spec(hot.shape)],
        out_specs=[head_spec(tokens, 0), row_spec(tokens)],
        out_shape=[
            jax.ShapeDtypeStruct((count, HEAD_DIM, tokens), BF16),
            jax.ShapeDtypeStruct((count, 1, tokens), F32),
        ],
        compiler_params=pltpu.CompilerParams(vmem_limit_bytes=48 << 20),
        cost_estimate=SMALL,
    )(own, other, own, other, own, other, bias, hot)


def attend_back(own, other, bias, hot, out, grad_own, grad_other, lse, first, count):
    heads = own.shape[0] // 3
    part = own.shape[2]
    tokens = part + other.shape[2]
    in_specs = [
        head_spec(part, component * heads + first) for component in range(3) for _ in range(2)
    ]
    return pl.pallas_call(
        functools.partial(attend_back_kernel, min(tokens, (1 << 19) // tokens)),
        grid=(count,),
        in_specs=in_specs
        + [
            whole_spec(bias.shape),
            whole_spec(hot.shape),
            head_spec(tokens, 0),
            head_spec(part, first),
            head_spec(part, first),
            row_spec(tokens),
        ],
        out_specs=pl.BlockSpec((3, 1, HEAD_DIM, tokens), lambda head: (0, head, 0, 0)),
        out_shape=jax.ShapeDtypeStruct((3, count, HEAD_DIM, tokens), BF16),
        compiler_params=pltpu.CompilerParams(vmem_limit_bytes=56 << 20),
        cost_estimate=SMALL,
    )(own, other, own, other, own, other, bias, hot, out, grad_own, grad_other, lse)


def write_kernel(place, blocks, aliased, *refs):
    me = lax.axis_index("dp")
    sources = refs[: len(refs) - 3 - aliased]
    out_ref, wide, sems = refs[-3:]
    copies = []
    for group, source in enumerate(sources):
        for block in range(blocks):
            slot = group * blocks + block
            wide[slot] = source[block].astype(F32)
            copies.append(
                pltpu.make_async_copy(
                    wide.at[slot], place(out_ref, me, group, block), sems.at[slot]
                )
            )
            copies[-1].start()
    for copy in copies:
        copy.wait()


def write_out(groups, place, shape, onto=None):
    blocks, rows, columns = groups[0].shape
    count = len(groups) * blocks
    anywhere = pl.BlockSpec(memory_space=pl.ANY)
    extra = [] if onto is None else [onto]
    return pl.pallas_call(
        functools.partial(write_kernel, place, blocks, len(extra)),
        in_specs=[pl.BlockSpec(memory_space=pltpu.VMEM)] * len(groups) + [anywhere] * len(extra),
        out_specs=anywhere,
        scratch_shapes=[
            pltpu.VMEM((count, rows, columns), F32),
            pltpu.SemaphoreType.DMA((count,)),
        ],
        out_shape=jax.ShapeDtypeStruct(shape, F32),
        input_output_aliases={} if onto is None else {len(groups): 0},
        compiler_params=pltpu.CompilerParams(vmem_limit_bytes=32 << 20),
        cost_estimate=SMALL,
    )(*groups, *extra)


def pair_body(
    tokens,
    segments,
    labels,
    timesteps,
    class_table,
    time_weight,
    ada_weight,
    qkv_weight,
    proj_weight,
    up_weight,
    down_weight,
    cotangent,
):
    position = lax.axis_index("tensor")
    rank = lax.axis_index("dp")
    dp_size = 16
    core, line, deep = rank % 2, rank // 2 % 2, rank // 4 % 2
    own_low = tokens[0]
    cot_low = cotangent[0]
    shard, width = own_low.shape
    pack = segments.shape[1]
    slot_count = labels.shape[1]
    class_count = class_table.shape[0]
    freq_width = time_weight.shape[0]
    local_width = qkv_weight.shape[2]
    heads = local_width // HEAD_DIM
    half_heads = heads // 2
    half_width = local_width // 2
    hidden_width = up_weight.shape[1]
    chunk = shard * SHORT // pack
    own_chunks = shard // chunk
    CORE, LINE, DEEP, FAR = 1, 2, 4, 8

    def fence(*values):
        return lax.optimization_barrier(values)

    def swap(x):
        return lax.ppermute(x, "tensor", [(0, 1), (1, 0)])

    def trade(x, bits):
        return lax.ppermute(x, "dp", [(i, i ^ bits) for i in range(dp_size)])

    def rows_of(x, index, count):
        size = x.shape[0] // count
        return lax.dynamic_slice_in_dim(x, index * size, size, 0)

    def columns_of(x, index, count):
        size = x.shape[1] // count
        return lax.dynamic_slice_in_dim(x, index * size, size, 1)

    def plus(a, b):
        return (a.astype(F32) + b.astype(F32)).astype(BF16)

    def halve(x, digit, bits):
        return plus(rows_of(x, digit, 2), trade(rows_of(x, 1 - digit, 2), bits))

    def gather_dp(x):
        y = x[None]
        y = jnp.concatenate([y, trade(y, CORE)], axis=0)
        y = jnp.concatenate([y, trade(y, LINE)], axis=0)
        y = jnp.concatenate([y, trade(y, DEEP), trade(y, FAR), trade(y, DEEP + FAR)], axis=0)
        return y.reshape((dp_size * x.shape[0],) + x.shape[1:])

    def chunked(x):
        return x.reshape(x.shape[0] // chunk, chunk, x.shape[1])

    def flat(x):
        return x.reshape(x.shape[0] * chunk, x.shape[2])

    quarter = shard // 2
    cuts = (0, shard // 4, shard * 5 // 8, shard)
    pieces = [own_low[a:b] for a, b in zip(cuts[:-1], cuts[1:], strict=True)]
    arrived = [swap(pieces[0])]
    ids = jnp.stack([labels[0], timesteps[0]], axis=1)

    seg = segments[0]
    seg = jnp.where(position == 0, seg, jnp.roll(seg, shard))
    slots = jnp.arange(slot_count, dtype=jnp.int32)
    chunk_hot = (seg[::chunk][:, None] == slots[None, :]).astype(F32)
    mask_rows = -(-slot_count // 8) * 8
    same = jnp.arange(mask_rows, dtype=jnp.int32)[:, None] == seg[None, :]
    hot = same.astype(BF16)
    bias = jnp.where(same, 0.0, -1e30).astype(BF16)

    classes = jnp.arange(class_count, dtype=jnp.int32)

    def condition_of(ids):
        label_hot = (ids[:, 0][:, None] == classes[None, :]).astype(F32)
        feats = features(ids[:, 1].astype(F32), freq_width)
        values = dot(label_hot, class_table, 1, 0, HIGH) + dot(feats, time_weight, 1, 0, HIGH)
        return label_hot, feats, values

    condition, arrived[0], pieces[1] = fence(condition_of(ids)[2], arrived[0], pieces[1])
    arrived.append(swap(pieces[1]))
    act_low = jax.nn.silu(condition).astype(BF16)
    mod_part, arrived[1], pieces[2] = fence(
        dot(act_low, ada_weight, 1, 0), arrived[1], pieces[2]
    )
    arrived.append(swap(pieces[2]))
    mod_away = swap(mod_part)
    modulation = jnp.where(
        position == 0,
        jnp.concatenate([mod_part, mod_away], axis=1),
        jnp.concatenate([mod_away, mod_part], axis=1),
    )
    per_chunk = dot(chunk_hot, modulation, 1, 0, HIGH)
    mods_own = [m[:, None, :] for m in jnp.split(per_chunk[:own_chunks], 6, axis=1)]
    mods_other = [m[:, None, :] for m in jnp.split(per_chunk[own_chunks:], 6, axis=1)]

    weight_t = qkv_weight.transpose(1, 2, 0).reshape(3 * local_width, width)

    def enter(low, mods):
        values = chunked(low.astype(F32))
        normed, inverse = normalize(values)
        inputs = flat((normed * (1.0 + mods[1]) + mods[0]).astype(BF16))
        return values, normed, inverse, inputs

    def project(inputs):
        return dot(weight_t, inputs, 1, 1).astype(BF16).reshape(3 * heads, HEAD_DIM, shard)

    tokens_own, normed_one, inverse_one, inputs_one_own = enter(own_low, mods_own)
    qkv_own = project(inputs_one_own)
    arrived[2], proj_half, qkv_own = fence(arrived[2], rows_of(proj_weight, core, 2), qkv_own)
    tokens_away = jnp.concatenate(arrived, axis=0)
    proj_half = swap(proj_half)
    tokens_other, normed_one_other, _, inputs_one_other = enter(tokens_away, mods_other)
    qkv_other = project(inputs_one_other)
    out_a, lse_a = attend(qkv_own, qkv_other, bias, hot, 0, half_heads)
    out_a, qkv_own = fence(out_a, qkv_own)
    away_a = swap(out_a.reshape(half_width, pack))
    out_b, lse_b = attend(qkv_own, qkv_other, bias, hot, half_heads, half_heads)
    out_b, proj_half, ids = fence(out_b, proj_half, ids)
    away_b = swap(out_b.reshape(half_width, pack))
    ids_all = gather_dp(ids)
    proj_rest = trade(proj_half, CORE)
    proj_other = jnp.where(
        core == 0,
        jnp.concatenate([proj_half, proj_rest], axis=0),
        jnp.concatenate([proj_rest, proj_half], axis=0),
    )
    out_flat = jnp.concatenate([out_a, out_b], axis=0).reshape(local_width, pack)
    own_part, other_part = slice(0, shard), slice(shard, pack)

    def reordered(away):
        return jnp.concatenate([away[:, other_part], away[:, own_part]], axis=1)

    away_a, ids_all, proj_other = fence(away_a, ids_all, proj_other)
    label_hot, features_all, condition_all = condition_of(ids_all)
    first = dot(
        jnp.concatenate([out_flat, reordered(away_a)], axis=0),
        jnp.concatenate([proj_weight, proj_other[:half_width]], axis=0),
        0,
        0,
    )
    away_b, cot_a, cot_b, condition_all, first = fence(
        away_b, cot_low[:quarter], cot_low[quarter:], condition_all, first
    )
    cot_away_a = swap(cot_a)
    branch_one = first + dot(reordered(away_b), proj_other[half_width:], 0, 0)
    branch_own, branch_other = branch_one[own_part], branch_one[other_part]

    def middle(values, branch, mods):
        halfway = values + mods[2] * chunked(branch)
        normed, inverse = normalize(halfway)
        inputs = flat((normed * (1.0 + mods[4]) + mods[3]).astype(BF16))
        return halfway, normed, inverse, inputs

    halfway, normed_two, inverse_two, inputs_two_own = middle(tokens_own, branch_own, mods_own)
    _, normed_two_other, _, inputs_two_other = middle(tokens_other, branch_other, mods_other)
    inputs_two = jnp.concatenate([inputs_two_own, inputs_two_other], axis=0)
    inputs_two, cot_away_a, cot_b = fence(inputs_two, cot_away_a, cot_b)
    cot_away_b = swap(cot_b)

    hidden = dot(inputs_two, up_weight, 1, 0)
    active, slope = gelu_parts(hidden)
    active = active.astype(BF16)
    slope = slope.astype(BF16)
    active, slope, cot_away_b = fence(active, slope, cot_away_b)
    cot_away = jnp.concatenate([cot_away_a, cot_away_b], axis=0)
    grad_branch_two = jnp.concatenate(
        [
            flat((chunked(cot_low.astype(F32)) * mods_own[5]).astype(BF16)),
            flat((chunked(cot_away.astype(F32)) * mods_other[5]).astype(BF16)),
        ],
        axis=0,
    )

    def down_half(half):
        return dot(columns_of(active, half, 2), grad_branch_two, 0, 0)

    down_away = trade(down_half(1 - core).astype(BF16), CORE)
    grad_active = dot(grad_branch_two, down_weight, 1, 1)
    grad_hidden = (grad_active * slope.astype(F32)).astype(BF16)
    down_sum = plus(down_half(core), down_away)
    down_sum, grad_hidden = fence(down_sum, grad_hidden)
    down_x = trade(rows_of(down_sum, 1 - line, 2), LINE)
    mod_two_other = dot(grad_hidden[other_part], up_weight, 1, 1)
    mod_two_away = mod_two_other.astype(BF16)
    mod_two_away, grad_hidden = fence(mod_two_away, grad_hidden)

    def up_half(half):
        return dot(inputs_two, columns_of(grad_hidden, half, 2), 0, 0)

    arrived_a = swap(mod_two_away[:quarter])
    up_away = trade(up_half(1 - core).astype(BF16), CORE)
    up_sum = plus(up_half(core), up_away)
    arrived_a, up_sum, mod_two_next, grad_hidden, active = fence(
        arrived_a, up_sum, mod_two_away[quarter:], grad_hidden, active
    )
    arrived_b = swap(mod_two_next)
    up_x = trade(rows_of(up_sum, 1 - line, 2), LINE)
    mod_two = dot(grad_hidden[own_part], up_weight, 1, 1)
    branch_two_away = dot(active[other_part], down_weight, 1, 0)
    branch_two = dot(active[own_part], down_weight, 1, 0)
    arrived_b, mod_two, branch_two_away, branch_two, down_x = fence(
        arrived_b, mod_two, branch_two_away, branch_two, down_x
    )
    down_sum = plus(rows_of(down_sum, line, 2), down_x)
    down_z = trade(rows_of(down_sum, 1 - deep, 2), DEEP)
    grad_mod_two = chunked(
        mod_two + jnp.concatenate([arrived_a, arrived_b], axis=0).astype(F32)
    )
    grad_out = chunked(cot_low.astype(F32))
    grad_halfway = grad_out + norm_back(
        grad_mod_two * (1.0 + mods_own[4]), normed_two, inverse_two
    )
    grad_branch_one = flat((grad_halfway * mods_own[2]).astype(BF16))
    grad_att_away = dot(proj_other, grad_branch_one, 1, 1).astype(BF16)
    grad_att_away, grad_branch_one = fence(grad_att_away, grad_branch_one)

    grad_att_other = swap(grad_att_away)
    grad_att_own = dot(proj_weight, grad_branch_one, 1, 1).astype(BF16)
    inputs_one = jnp.concatenate([inputs_one_own, inputs_one_other], axis=0)
    grad_att_other, grad_att_own, down_z, branch_one_next, inputs_one = fence(
        grad_att_other, grad_att_own, down_z, grad_branch_one, inputs_one
    )
    down_sum = plus(rows_of(down_sum, deep, 2), down_z)
    down_far = trade(down_sum, FAR)

    def back(out, lse, first):
        return attend_back(
            qkv_own,
            qkv_other,
            bias,
            hot,
            out,
            grad_att_own.reshape(heads, HEAD_DIM, shard),
            grad_att_other.reshape(heads, HEAD_DIM, shard),
            lse,
            first,
            half_heads,
        ).reshape(3 * half_width, pack)

    def qkv_half(grad):
        return lambda half: dot(rows_of(grad, half, 2), inputs_one, 1, 0)

    grads_one_other = swap(branch_one_next)
    grad_qkv_a = back(out_a, lse_a, 0)
    grad_qkv_a, up_x = fence(grad_qkv_a, up_x)
    up_sum = plus(rows_of(up_sum, line, 2), up_x)
    up_z = trade(rows_of(up_sum, 1 - deep, 2), DEEP)
    qkv_make = qkv_half(grad_qkv_a)
    qkv_a_away = trade(qkv_make(1 - core).astype(BF16), CORE)
    qkv_a = plus(qkv_make(core), qkv_a_away)
    qkv_a, grad_att_own = fence(qkv_a, grad_att_own)
    qkv_a_x = trade(rows_of(qkv_a, 1 - line, 2), LINE)
    grad_qkv_b = back(out_b, lse_b, half_heads)
    grad_qkv_b, qkv_a_x, up_z, down_far, grads_one_other = fence(
        grad_qkv_b, qkv_a_x, up_z, down_far, grads_one_other
    )
    qkv_a = plus(rows_of(qkv_a, line, 2), qkv_a_x)
    up_sum = plus(rows_of(up_sum, deep, 2), up_z)
    up_far = trade(up_sum, FAR)
    down_sum = plus(down_sum, down_far)
    down_z = trade(down_sum, DEEP)
    down_x = trade(down_sum, LINE)
    weight_parts = weight_t.reshape(3, 2, half_width, width)
    weight_a = weight_parts[:, 0].reshape(3 * half_width, width)
    weight_b = weight_parts[:, 1].reshape(3 * half_width, width)
    mod_one = dot(grad_qkv_a, weight_a, 0, 0) + dot(grad_qkv_b, weight_b, 0, 0)
    mod_one_own, mod_one_away = chunked(mod_one[own_part]), chunked(mod_one[other_part])

    def chunk_sums(own, other):
        return jnp.concatenate([jnp.sum(own, axis=1), jnp.sum(other, axis=1)], axis=0)

    gate_one_sums = jnp.sum(grad_halfway * chunked(branch_own), axis=1)
    chunk_terms = jnp.concatenate(
        [
            chunk_sums(mod_one_own, mod_one_away),
            chunk_sums(mod_one_own * normed_one, mod_one_away * normed_one_other),
            jnp.concatenate([gate_one_sums, jnp.zeros_like(gate_one_sums)], axis=0),
            chunk_sums(chunked(mod_two), chunked(mod_two_other)),
            chunk_sums(
                chunked(mod_two) * normed_two, chunked(mod_two_other) * normed_two_other
            ),
            chunk_sums(
                chunked(branch_two) * grad_out,
                chunked(branch_two_away) * chunked(cot_away.astype(F32)),
            ),
        ],
        axis=1,
    )
    slot_terms = dot(chunk_hot, chunk_terms, 0, 0, HIGH).astype(BF16)
    half = slot_terms.shape[1] // 2
    low, high = slot_terms[:, :half], slot_terms[:, half:]
    keep = jnp.where(position == 0, low, high)
    away = jnp.where(position == 0, high, low)
    qkv_make_b = qkv_half(grad_qkv_b)
    qkv_b_away = trade(qkv_make_b(1 - core).astype(BF16), CORE)
    qkv_b = plus(qkv_make_b(core), qkv_b_away)

    def proj_half_of(half):
        rows = rows_of(out_flat, half, 2)
        return dot(rows[:, own_part], grad_branch_one, 1, 0) + dot(
            rows[:, other_part], grads_one_other, 1, 0
        )

    proj_away = trade(proj_half_of(1 - core).astype(BF16), CORE)
    proj_sum = plus(proj_half_of(core), proj_away)
    away, keep, mod_one_next, qkv_b, proj_sum, down_z, down_x = fence(
        away, keep, flat(mod_one_away).astype(BF16), qkv_b, proj_sum, down_z, down_x
    )

    grad_modulation = plus(keep, swap(away))[None]
    mod_one_other = swap(mod_one_next)
    gathered = jnp.concatenate([grad_modulation, trade(grad_modulation, CORE)], axis=0)
    down_zx = trade(down_z, LINE)
    proj_x = trade(rows_of(proj_sum, 1 - line, 2), LINE)
    qkv_a_z = trade(rows_of(qkv_a, 1 - deep, 2), DEEP)
    qkv_b_z = trade(rows_of(qkv_b, 1 - deep, 2), DEEP)
    gathered, up_far, qkv_a_z, qkv_b_z, down_zx, proj_x = fence(
        gathered, up_far, qkv_a_z, qkv_b_z, down_zx, proj_x
    )
    gathered = jnp.concatenate([gathered, trade(gathered, LINE)], axis=0)
    up_sum = plus(up_sum, up_far)
    up_x = trade(up_sum, LINE)
    up_z = trade(up_sum, DEEP)
    qkv_a = plus(rows_of(qkv_a, deep, 2), qkv_a_z)
    qkv_a_far = trade(qkv_a, FAR)
    qkv_b = plus(rows_of(qkv_b, deep, 2), qkv_b_z)
    qkv_b_x = trade(rows_of(qkv_b, 1 - line, 2), LINE)
    proj_sum = plus(rows_of(proj_sum, line, 2), proj_x)
    gathered, up_x, up_z, qkv_a_far, qkv_b_x, mod_one_other, proj_sum = fence(
        gathered, up_x, up_z, qkv_a_far, qkv_b_x, mod_one_other, proj_sum
    )
    gathered = jnp.concatenate(
        [gathered, trade(gathered, DEEP), trade(gathered, FAR), trade(gathered, DEEP + FAR)], axis=0
    )
    up_zx = trade(up_z, LINE)
    qkv_a = plus(qkv_a, qkv_a_far)
    qkv_a_z = trade(qkv_a, DEEP)
    qkv_b = plus(rows_of(qkv_b, line, 2), qkv_b_x)
    qkv_b_far = trade(qkv_b, FAR)
    proj_z = trade(rows_of(proj_sum, 1 - deep, 2), DEEP)
    grad_mod_one = mod_one_own + chunked(mod_one_other.astype(F32))
    grad_input = grad_halfway + norm_back(
        grad_mod_one * (1.0 + mods_own[1]), normed_one, inverse_one
    )
    grad_input = flat(grad_input).astype(BF16)
    gathered, up_zx, qkv_a_z, qkv_b_far, proj_z, grad_input, branch_two_next = fence(
        gathered,
        up_zx,
        qkv_a_z,
        qkv_b_far,
        proj_z,
        grad_input,
        branch_two_away.astype(BF16),
    )

    def in_order(digit, own, other):
        return jnp.where(
            digit == 0,
            jnp.concatenate([own, other], axis=0),
            jnp.concatenate([other, own], axis=0),
        ).reshape(3, HEAD_DIM, width)

    qkv_a = in_order(deep, qkv_a, qkv_a_z)
    qkv_a_x = trade(qkv_a, LINE)
    qkv_b = plus(qkv_b, qkv_b_far)
    qkv_b_x = trade(qkv_b, LINE)
    proj_sum = plus(rows_of(proj_sum, deep, 2), proj_z)
    proj_far = trade(proj_sum, FAR)
    grad_mod_all = gathered.reshape(dp_size * slot_count, half)
    grad_ada = dot(jax.nn.silu(condition_all).astype(BF16), grad_mod_all, 0, 0)
    cond_part = dot(grad_mod_all, ada_weight, 1, 1).astype(BF16)
    cond_part, qkv_b_x, proj_far, qkv_a_x, grad_ada = fence(
        cond_part, qkv_b_x, proj_far, qkv_a_x, grad_ada
    )
    qkv_b = in_order(line, qkv_b, qkv_b_x)
    qkv_b_z = trade(qkv_b, DEEP)
    proj_sum = plus(proj_sum, proj_far)
    proj_z = trade(proj_sum, DEEP)
    grad_act = cond_part.astype(F32) + swap(cond_part).astype(F32)
    grad_condition = jax.vjp(jax.nn.silu, condition_all)[1](grad_act)[0]
    grad_class = dot(label_hot.astype(BF16), grad_condition.astype(BF16), 0, 0)
    grad_time = dot(features_all, grad_condition, 0, 0, HIGH)
    branch_two = chunked(branch_two) + chunked(swap(branch_two_next).astype(F32))
    result = halfway + mods_own[5] * branch_two
    proj_near = jnp.stack([proj_sum, proj_z])

    def cores(near, far):
        return [near, far, trade(near, CORE), trade(far, CORE)]

    def digit(me, bits):
        return me // bits % 2

    def down_place(ref, me, group, block):
        index = (
            (digit(me, CORE) + group // 2) % 2 * 4
            + (digit(me, LINE) + group % 2) % 2 * 2
            + (digit(me, DEEP) + block) % 2
        )
        return ref.at[index]

    def up_place(ref, me, group, block):
        index = (digit(me, LINE) + group % 2) % 2 * 2 + (digit(me, DEEP) + block) % 2
        column = (digit(me, CORE) + group // 2) % 2 * (hidden_width // 2)
        return ref.at[index, :, pl.ds(pl.multiple_of(column, 128), hidden_width // 2)]

    def qkv_place(offset, bits):
        def place(ref, me, group, block):
            unit = (
                (digit(me, CORE) + group // 2) % 2 * 2 + (digit(me, bits) + group % 2) % 2
            ) * 3 + block
            return ref.at[unit // half_heads * heads + unit % half_heads + offset]

        return place

    grad_down = write_out(
        cores(jnp.stack([down_sum, down_z]), jnp.stack([down_x, down_zx])),
        down_place,
        (8, hidden_width // 8, width),
    )
    grad_up = write_out(
        cores(jnp.stack([up_sum, up_z]), jnp.stack([up_x, up_zx])),
        up_place,
        (4, width // 4, hidden_width),
    )
    grad_proj = write_out(
        cores(proj_near, trade(proj_near, LINE)), down_place, (8, local_width // 8, width)
    )
    qkv_shape = (3 * heads, HEAD_DIM, width)
    grad_qkv = write_out(cores(qkv_a, qkv_a_x), qkv_place(0, LINE), qkv_shape)
    grad_qkv = write_out(cores(qkv_b, qkv_b_z), qkv_place(half_heads, DEEP), qkv_shape, grad_qkv)
    return (
        flat(result).astype(BF16)[None],
        grad_input[None],
        grad_class,
        grad_time,
        grad_ada,
        grad_qkv.reshape(3, local_width, width).transpose(2, 0, 1),
        grad_proj.reshape(local_width, width),
        grad_up.reshape(width, hidden_width),
        grad_down.reshape(hidden_width, width),
    )


def any_body(
    tokens,
    segments,
    labels,
    timesteps,
    class_table,
    time_weight,
    ada_weight,
    qkv_weight,
    proj_weight,
    up_weight,
    down_weight,
    cotangent,
):
    own_tokens = tokens[0].astype(jnp.float32)
    shard_rows = own_tokens.shape[0]
    model_width = own_tokens.shape[1]
    seg_all = segments[0]
    pack_rows = seg_all.shape[0]
    slot_count = labels.shape[1]
    class_count = class_table.shape[0]
    freq_width = time_weight.shape[0]
    local_width = qkv_weight.shape[2]
    head_count = local_width // HEAD_DIM
    scale_factor = 1.0 / math.sqrt(HEAD_DIM)
    position = lax.axis_index("tensor")
    seg_own = lax.dynamic_slice_in_dim(seg_all, position * shard_rows, shard_rows)
    own_hot = (seg_own[:, None] == jnp.arange(slot_count, dtype=jnp.int32)[None, :]).astype(
        jnp.float32
    )
    label_hot = (labels[0][:, None] == jnp.arange(class_count, dtype=jnp.int32)[None, :]).astype(
        jnp.float32
    )
    step_feats = features(timesteps[0].astype(jnp.float32), freq_width)
    condition = jnp.dot(label_hot, class_table, precision=HIGH) + jnp.dot(
        step_feats, time_weight, precision=HIGH
    )
    act_low = jax.nn.silu(condition).astype(jnp.bfloat16)
    mod_part = jnp.dot(act_low, ada_weight, preferred_element_type=jnp.float32)
    modulation = lax.all_gather(mod_part, "tensor", axis=1, tiled=True)
    per_token = jnp.dot(own_hot, modulation, precision=HIGH)
    shift_one, scale_one, gate_one, shift_two, scale_two, gate_two = jnp.split(per_token, 6, axis=1)
    normed_one, inverse_one = normalize(own_tokens)
    modulated_one = (normed_one * (1.0 + scale_one) + shift_one).astype(jnp.bfloat16)
    inputs_one = lax.all_gather(modulated_one, "tensor", axis=0, tiled=True)
    qkv_flat = qkv_weight.reshape(model_width, 3 * local_width)
    qkv = jnp.dot(inputs_one, qkv_flat, preferred_element_type=jnp.float32).astype(jnp.bfloat16)
    qkv_heads = qkv.reshape(pack_rows, 3, head_count, HEAD_DIM).transpose(1, 2, 0, 3)
    queries = qkv_heads[0]
    keys = qkv_heads[1]
    values = qkv_heads[2]
    block = min(512, pack_rows)
    block_count = pack_rows // block
    starts = jnp.arange(block_count, dtype=jnp.int32) * block

    def scores_of(start):
        query_block = lax.dynamic_slice_in_dim(queries, start, block, 1)
        seg_block = lax.dynamic_slice_in_dim(seg_all, start, block)
        raw = (
            jnp.einsum("hqd,hkd->hqk", query_block, keys, preferred_element_type=jnp.float32)
            * scale_factor
        )
        same = (seg_block[:, None] == seg_all[None, :])[None]
        return (jnp.where(same, raw, -1e30), query_block)

    def attend(start):
        scores = scores_of(start)[0]
        top = jnp.max(scores, axis=-1, keepdims=True)
        exps = jnp.exp(scores - top)
        total = jnp.sum(exps, axis=-1, keepdims=True)
        weights = (exps / total).astype(jnp.bfloat16)
        out_block = jnp.einsum("hqk,hkd->hqd", weights, values, preferred_element_type=jnp.float32)
        return (out_block, (top + jnp.log(total))[..., 0])

    out_blocks, lse_blocks = lax.map(attend, starts)
    attended = out_blocks.transpose(0, 2, 1, 3).reshape(pack_rows, local_width).astype(jnp.bfloat16)
    lse_all = lse_blocks.transpose(1, 0, 2).reshape(head_count, pack_rows)
    branch_one = lax.psum_scatter(
        jnp.dot(attended, proj_weight, preferred_element_type=jnp.float32),
        "tensor",
        scatter_dimension=0,
        tiled=True,
    )
    halfway = own_tokens + gate_one * branch_one
    normed_two, inverse_two = normalize(halfway)
    modulated_two = (normed_two * (1.0 + scale_two) + shift_two).astype(jnp.bfloat16)
    inputs_two = lax.all_gather(modulated_two, "tensor", axis=0, tiled=True)
    hidden = jnp.dot(inputs_two, up_weight, preferred_element_type=jnp.float32)
    active = jax.nn.gelu(hidden, approximate=True).astype(jnp.bfloat16)
    branch_two = lax.psum_scatter(
        jnp.dot(active, down_weight, preferred_element_type=jnp.float32).astype(jnp.bfloat16),
        "tensor",
        scatter_dimension=0,
        tiled=True,
    ).astype(jnp.float32)
    result = halfway + gate_two * branch_two
    grad_out = cotangent[0].astype(jnp.float32)
    grad_gate_two = grad_out * branch_two
    grad_branch_two = (grad_out * gate_two).astype(jnp.bfloat16)
    grads_two = lax.all_gather(grad_branch_two, "tensor", axis=0, tiled=True)
    grad_down = contract_rows(active, grads_two)
    grad_active = times_transposed(grads_two, down_weight)
    gelu_back = jax.vjp(lambda inner: jax.nn.gelu(inner, approximate=True), hidden)[1]
    grad_hidden = gelu_back(grad_active)[0].astype(jnp.bfloat16)
    grad_up = contract_rows(inputs_two, grad_hidden)
    grad_mod_two = lax.psum_scatter(
        times_transposed(grad_hidden, up_weight), "tensor", scatter_dimension=0, tiled=True
    )
    grad_halfway = grad_out + norm_back(grad_mod_two * (1.0 + scale_two), normed_two, inverse_two)
    grad_gate_one = grad_halfway * branch_one
    grad_branch_one = (grad_halfway * gate_one).astype(jnp.bfloat16)
    grads_one = lax.all_gather(grad_branch_one, "tensor", axis=0, tiled=True)
    grad_proj = contract_rows(attended, grads_one)
    grad_attended = times_transposed(grads_one, proj_weight).astype(jnp.bfloat16)
    grad_heads = grad_attended.reshape(pack_rows, head_count, HEAD_DIM).transpose(1, 0, 2)

    def attend_back(carry, start):
        grad_keys, grad_values = carry
        scores, query_block = scores_of(start)
        lse_block = lax.dynamic_slice_in_dim(lse_all, start, block, 1)
        probs = jnp.exp(scores - lse_block[..., None])
        grad_block = lax.dynamic_slice_in_dim(grad_heads, start, block, 1)
        grad_probs = jnp.einsum(
            "hqd,hkd->hqk", grad_block, values, preferred_element_type=jnp.float32
        )
        grad_scores = (
            probs * (grad_probs - jnp.sum(probs * grad_probs, axis=-1, keepdims=True))
        ).astype(jnp.bfloat16)
        grad_query = (
            jnp.einsum("hqk,hkd->hqd", grad_scores, keys, preferred_element_type=jnp.float32)
            * scale_factor
        )
        grad_keys = (
            grad_keys
            + jnp.einsum(
                "hqk,hqd->hkd", grad_scores, query_block, preferred_element_type=jnp.float32
            )
            * scale_factor
        )
        grad_values = grad_values + jnp.einsum(
            "hqk,hqd->hkd",
            probs.astype(jnp.bfloat16),
            grad_block,
            preferred_element_type=jnp.float32,
        )
        return ((grad_keys, grad_values), grad_query)

    empty = jnp.zeros((head_count, pack_rows, HEAD_DIM), jnp.float32)
    key_grads, grad_queries = lax.scan(attend_back, (empty, empty), starts)
    query_grads = grad_queries.transpose(1, 0, 2, 3).reshape(head_count, pack_rows, HEAD_DIM)
    grad_stack = jnp.stack([query_grads, key_grads[0], key_grads[1]], axis=0)
    grad_qkv = (
        grad_stack.transpose(2, 0, 1, 3).reshape(pack_rows, 3 * local_width).astype(jnp.bfloat16)
    )
    grad_qkv_weight = contract_rows(inputs_one, grad_qkv).reshape(model_width, 3, local_width)
    grad_mod_one = lax.psum_scatter(
        times_transposed(grad_qkv, qkv_flat).astype(jnp.bfloat16),
        "tensor",
        scatter_dimension=0,
        tiled=True,
    ).astype(jnp.float32)
    grad_input = grad_halfway + norm_back(grad_mod_one * (1.0 + scale_one), normed_one, inverse_one)
    grad_per_token = jnp.concatenate(
        [
            grad_mod_one,
            grad_mod_one * normed_one,
            grad_gate_one,
            grad_mod_two,
            grad_mod_two * normed_two,
            grad_gate_two,
        ],
        axis=1,
    )
    slot_terms = contract_exact(own_hot, grad_per_token)
    grad_modulation = lax.psum_scatter(
        slot_terms.astype(jnp.bfloat16), "tensor", scatter_dimension=1, tiled=True
    )
    grad_ada = contract_rows(act_low, grad_modulation)
    cond_part = times_transposed(grad_modulation, ada_weight)
    grad_activated = lax.psum(cond_part.astype(jnp.bfloat16), "tensor").astype(jnp.float32)
    grad_condition = jax.vjp(jax.nn.silu, condition)[1](grad_activated)[0]
    grad_class = contract_exact(label_hot, grad_condition)
    grad_time = contract_exact(step_feats, grad_condition)
    summed = (
        lax.psum(grad_class.astype(jnp.bfloat16), "dp").astype(jnp.float32),
        lax.psum(grad_time.astype(jnp.bfloat16), "dp").astype(jnp.float32),
        lax.psum(grad_ada.astype(jnp.bfloat16), "dp").astype(jnp.float32),
        lax.psum(grad_qkv_weight.astype(jnp.bfloat16), "dp").astype(jnp.float32),
        lax.psum(grad_proj.astype(jnp.bfloat16), "dp").astype(jnp.float32),
        lax.psum(grad_up.astype(jnp.bfloat16), "dp").astype(jnp.float32),
        lax.psum(grad_down.astype(jnp.bfloat16), "dp").astype(jnp.float32),
    )
    grad_class, grad_time, grad_ada, grad_qkv_weight, grad_proj, grad_up, grad_down = summed
    return (
        result.astype(jnp.bfloat16)[None],
        grad_input.astype(jnp.bfloat16)[None],
        grad_class,
        grad_time,
        grad_ada,
        grad_qkv_weight,
        grad_proj,
        grad_up,
        grad_down,
    )


def solution(mesh):
    pairs = mesh.shape["dp"] == 16 and mesh.shape["tensor"] == 2
    return jax.shard_map(
        pair_body if pairs else any_body,
        mesh=mesh,
        in_specs=(
            P("dp", "tensor", None),
            P("dp", None),
            P("dp", None),
            P("dp", None),
            P(),
            P(),
            P(None, "tensor"),
            P(None, None, "tensor"),
            P("tensor", None),
            P(None, "tensor"),
            P("tensor", None),
            P("dp", "tensor", None),
        ),
        out_specs=(
            P("dp", "tensor", None),
            P("dp", "tensor", None),
            P(),
            P(),
            P(None, "tensor"),
            P(None, None, "tensor"),
            P("tensor", None),
            P(None, "tensor"),
            P("tensor", None),
        ),
        check_vma=False,
    )
```

```python
import functools
import math

import jax
import jax.numpy as jnp
from jax import lax
from jax.experimental import pallas as pl
from jax.experimental.pallas import tpu as pltpu
from jax.sharding import PartitionSpec as P

HEAD_DIM = 72
SHORT = 256
HIGH = lax.Precision.HIGHEST
F32 = jnp.float32
BF16 = jnp.bfloat16
SCALE = 1.0 / math.sqrt(HEAD_DIM)
SCALE_LOG2 = SCALE * math.log2(math.e)


def dot(left, right, left_dim, right_dim, precision=None):
    return lax.dot_general(
        left,
        right,
        (((left_dim,), (right_dim,)), ((), ())),
        precision=precision,
        preferred_element_type=F32,
    )


def features(steps_f, width_total):
    half = width_total // 2
    freqs = jnp.exp(-math.log(10000.0) * jnp.arange(half, dtype=F32) / half)
    angles = steps_f[:, None] * freqs[None, :]
    return jnp.concatenate([jnp.cos(angles), jnp.sin(angles)], axis=1)


def contract_rows(left, right):
    return dot(left, right, 0, 0)


def contract_exact(left, right):
    return dot(left, right, 0, 0, HIGH)


def times_transposed(left, right):
    return dot(left, right, 1, 1)


def normalize(values):
    average = jnp.mean(values, axis=-1, keepdims=True)
    centred = values - average
    inverse = lax.rsqrt(jnp.mean(centred * centred, axis=-1, keepdims=True) + 1e-06)
    return centred * inverse, inverse


def norm_back(grad_normed, normed, inverse):
    first = jnp.mean(grad_normed, axis=-1, keepdims=True)
    second = jnp.mean(grad_normed * normed, axis=-1, keepdims=True)
    return inverse * (grad_normed - first - normed * second)


def gelu_parts(x):
    root = math.sqrt(2.0 / math.pi)
    square = x * x
    bent = jnp.tanh(root * x * (1.0 + 0.044715 * square))
    half = 0.5 * (1.0 + bent)
    slope = half + 0.5 * x * (1.0 - bent * bent) * root * (1.0 + 3 * 0.044715 * square)
    return x * half, slope


def joined(own, other):
    return jnp.concatenate([own[0], other[0]], axis=1)


def attend_kernel(block, q0, q1, k0, k1, v0, v1, bias_ref, hot_ref, o_ref, lse_ref):
    tokens = o_ref.shape[2]
    query = jnp.concatenate([joined(q0, q1), bias_ref[...]], axis=0)
    key = jnp.concatenate([joined(k0, k1), hot_ref[...]], axis=0).T
    value = joined(v0, v1)
    for start in range(0, tokens, block):
        part = slice(start, start + block)
        scores = dot(key, query[:, part], 1, 0)
        top = jnp.max(scores, axis=0, keepdims=True) * SCALE_LOG2
        exps = jnp.exp2(scores * SCALE_LOG2 - top)
        total = jnp.sum(exps, axis=0, keepdims=True)
        out = dot(value, exps.astype(BF16), 1, 0)
        o_ref[0, :, part] = (out / total).astype(BF16)
        lse_ref[0, :, part] = top + jnp.log2(total)


def attend_back_kernel(
    block, q0, q1, k0, k1, v0, v1, bias_ref, hot_ref, o_ref, do0, do1, lse_ref, grad_ref
):
    tokens = o_ref.shape[2]
    query_all, key_all = joined(q0, q1), joined(k0, k1)
    query = jnp.concatenate([query_all, bias_ref[...]], axis=0)
    key = jnp.concatenate([key_all, hot_ref[...]], axis=0).T
    value = joined(v0, v1).T
    query_rows = query_all.T
    grad_out = joined(do0, do1)
    grad_rows = grad_out.T
    delta = jnp.sum(grad_out.astype(F32) * o_ref[0].astype(F32), axis=0, keepdims=True)
    lse = lse_ref[0]
    grad_key = grad_value = None
    for start in range(0, tokens, block):
        part = slice(start, start + block)
        scores = dot(key, query[:, part], 1, 0)
        probs = jnp.exp2(scores * SCALE_LOG2 - lse[:, part])
        grad_probs = dot(value, grad_out[:, part], 1, 0)
        grad_scores = (probs * (grad_probs - delta[:, part])).astype(BF16)
        value_term = dot(probs.astype(BF16), grad_rows[part], 1, 0)
        key_term = dot(grad_scores, query_rows[part], 1, 0)
        grad_value = value_term if grad_value is None else grad_value + value_term
        grad_key = key_term if grad_key is None else grad_key + key_term
        grad_ref[0, 0, :, part] = (dot(key_all, grad_scores, 1, 0) * SCALE).astype(BF16)
    grad_ref[1, 0] = (grad_key * SCALE).astype(BF16).T
    grad_ref[2, 0] = grad_value.astype(BF16).T


def head_spec(tokens, offset):
    return pl.BlockSpec((1, HEAD_DIM, tokens), lambda head: (head + offset, 0, 0))


def whole_spec(shape):
    return pl.BlockSpec(shape, lambda head: (0,) * len(shape))


def row_spec(tokens):
    return pl.BlockSpec((1, 1, tokens), lambda head: (head, 0, 0))


SMALL = pl.CostEstimate(flops=1 << 20, bytes_accessed=1 << 20, transcendentals=0)


def attend(own, other, bias, hot, first, count):
    heads = own.shape[0] // 3
    part = own.shape[2]
    tokens = part + other.shape[2]
    in_specs = [
        head_spec(part, component * heads + first) for component in range(3) for _ in range(2)
    ]
    return pl.pallas_call(
        functools.partial(attend_kernel, min(tokens, (1 << 20) // tokens)),
        grid=(count,),
        in_specs=in_specs + [whole_spec(bias.shape), whole_spec(hot.shape)],
        out_specs=[head_spec(tokens, 0), row_spec(tokens)],
        out_shape=[
            jax.ShapeDtypeStruct((count, HEAD_DIM, tokens), BF16),
            jax.ShapeDtypeStruct((count, 1, tokens), F32),
        ],
        compiler_params=pltpu.CompilerParams(vmem_limit_bytes=24 << 20),
        cost_estimate=SMALL,
    )(own, other, own, other, own, other, bias, hot)


def attend_back(own, other, bias, hot, out, grad_own, grad_other, lse, first, count):
    heads = own.shape[0] // 3
    part = own.shape[2]
    tokens = part + other.shape[2]
    in_specs = [
        head_spec(part, component * heads + first) for component in range(3) for _ in range(2)
    ]
    return pl.pallas_call(
        functools.partial(attend_back_kernel, min(tokens, (1 << 19) // tokens)),
        grid=(count,),
        in_specs=in_specs
        + [
            whole_spec(bias.shape),
            whole_spec(hot.shape),
            head_spec(tokens, 0),
            head_spec(part, first),
            head_spec(part, first),
            row_spec(tokens),
        ],
        out_specs=pl.BlockSpec((3, 1, HEAD_DIM, tokens), lambda head: (0, head, 0, 0)),
        out_shape=jax.ShapeDtypeStruct((3, count, HEAD_DIM, tokens), BF16),
        compiler_params=pltpu.CompilerParams(vmem_limit_bytes=24 << 20),
        cost_estimate=SMALL,
    )(own, other, own, other, own, other, bias, hot, out, grad_own, grad_other, lse)


def write_kernel(place, first, last, aliased, *refs):
    me = lax.axis_index("dp")
    sources = refs[: len(refs) - 3 - aliased]
    out_ref, wide, sems = refs[-3:]
    copies = []
    for group, source in enumerate(sources):
        for block in range(first, last):
            slot = group * (last - first) + block - first
            wide[slot] = source[block].astype(F32)
            copies.append(
                pltpu.make_async_copy(
                    wide.at[slot], place(out_ref, me, group, block), sems.at[slot]
                )
            )
            copies[-1].start()
    for copy in copies:
        copy.wait()


def write_out(groups, place, shape, onto=None, part=None):
    blocks, rows, columns = groups[0].shape
    first, last = (0, blocks) if part is None else part
    count = len(groups) * (last - first)
    anywhere = pl.BlockSpec(memory_space=pl.ANY)
    extra = [] if onto is None else [onto]
    return pl.pallas_call(
        functools.partial(write_kernel, place, first, last, len(extra)),
        in_specs=[pl.BlockSpec(memory_space=pltpu.VMEM)] * len(groups) + [anywhere] * len(extra),
        out_specs=anywhere,
        scratch_shapes=[
            pltpu.VMEM((count, rows, columns), F32),
            pltpu.SemaphoreType.DMA((count,)),
        ],
        out_shape=jax.ShapeDtypeStruct(shape, F32),
        input_output_aliases={} if onto is None else {len(groups): 0},
        compiler_params=pltpu.CompilerParams(vmem_limit_bytes=20 << 20),
        cost_estimate=SMALL,
    )(*groups, *extra)


def hidden_kernel(inputs_ref, weight_ref, active_ref, slope_ref):
    rows = inputs_ref.shape[0] // 4
    for start in range(0, 4 * rows, rows):
        part = slice(start, start + rows)
        active, slope = gelu_parts(dot(inputs_ref[part], weight_ref[...], 1, 0))
        active_ref[part] = active.astype(BF16)
        slope_ref[part] = slope.astype(BF16)


def hidden_units(inputs, weight):
    rows, width = inputs.shape
    units = weight.shape[1]
    block = units // 6
    out_block = pl.BlockSpec((rows, block), lambda i: (0, i))
    return pl.pallas_call(
        hidden_kernel,
        grid=(6,),
        in_specs=[
            pl.BlockSpec((rows, width), lambda i: (0, 0)),
            pl.BlockSpec((width, block), lambda i: (0, i)),
        ],
        out_specs=[out_block] * 2,
        out_shape=[jax.ShapeDtypeStruct((rows, units), BF16)] * 2,
        compiler_params=pltpu.CompilerParams(vmem_limit_bytes=20 << 20),
        cost_estimate=SMALL,
    )(inputs, weight)


def hidden_back_kernel(grad_ref, weight_ref, slope_ref, out_ref):
    rows = grad_ref.shape[0] // 4
    for start in range(0, 4 * rows, rows):
        part = slice(start, start + rows)
        grads = dot(grad_ref[part], weight_ref[...], 1, 1)
        out_ref[part] = (grads * slope_ref[part].astype(F32)).astype(BF16)


def hidden_back(grads, weight, slope):
    rows, width = grads.shape
    units = weight.shape[0]
    block = units // 6
    out_block = pl.BlockSpec((rows, block), lambda i: (0, i))
    return pl.pallas_call(
        hidden_back_kernel,
        grid=(6,),
        in_specs=[
            pl.BlockSpec((rows, width), lambda i: (0, 0)),
            pl.BlockSpec((block, width), lambda i: (i, 0)),
            out_block,
        ],
        out_specs=out_block,
        out_shape=jax.ShapeDtypeStruct((rows, units), BF16),
        compiler_params=pltpu.CompilerParams(vmem_limit_bytes=20 << 20),
        cost_estimate=SMALL,
    )(grads, weight, slope)


def gradient_kernel(left_is_blocked, half_ref, left_ref, right_ref, *refs):
    total = dot(left_ref[...], right_ref[...], 0, 0)
    if len(refs) == 2:
        total = total + refs[0][...].astype(F32)
    refs[-1][...] = total.astype(BF16)


def half_gradient(left, right, half, away, left_is_blocked):
    rows = left.shape[0]
    blocked = left if left_is_blocked else right
    whole = right if left_is_blocked else left
    units = blocked.shape[1] // 2
    block = units // 3
    half_spec = pl.BlockSpec((rows, block), lambda i, half_ref: (0, half_ref[0] * 3 + i))
    whole_block = pl.BlockSpec(whole.shape, lambda i, half_ref: (0, 0))
    if left_is_blocked:
        shape = (units, whole.shape[1])
        out_spec = pl.BlockSpec((block, shape[1]), lambda i, half_ref: (i, 0))
        in_specs = [half_spec, whole_block]
    else:
        shape = (whole.shape[1], units)
        out_spec = pl.BlockSpec((shape[0], block), lambda i, half_ref: (0, i))
        in_specs = [whole_block, half_spec]
    extra = [] if away is None else [away]
    return pl.pallas_call(
        functools.partial(gradient_kernel, left_is_blocked),
        grid_spec=pltpu.PrefetchScalarGridSpec(
            num_scalar_prefetch=1,
            grid=(3,),
            in_specs=in_specs + [out_spec] * len(extra),
            out_specs=out_spec,
        ),
        out_shape=jax.ShapeDtypeStruct(shape, BF16),
        compiler_params=pltpu.CompilerParams(vmem_limit_bytes=22 << 20),
        cost_estimate=SMALL,
    )(half.astype(jnp.int32)[None], left, right, *extra)


def down_gradient(active, grads, half, away=None):
    return half_gradient(active, grads, half, away, True)


def up_gradient(inputs, grads, half, away=None):
    return half_gradient(inputs, grads, half, away, False)


def rows_back_kernel(grad_ref, weight_ref, wide_ref, low_ref):
    total = dot(grad_ref[...], weight_ref[...], 1, 1)
    wide_ref[...] = total
    low_ref[...] = total.astype(BF16)


def rows_back(grads, weight, which):
    rows = grads.shape[0] // 2
    units = grads.shape[1]
    width = weight.shape[0]
    block = width // 3
    out_block = pl.BlockSpec((rows, block), lambda i: (0, i))
    return pl.pallas_call(
        rows_back_kernel,
        grid=(3,),
        in_specs=[
            pl.BlockSpec((rows, units), lambda i: (which, 0)),
            pl.BlockSpec((block, units), lambda i: (i, 0)),
        ],
        out_specs=[out_block] * 2,
        out_shape=[
            jax.ShapeDtypeStruct((rows, width), F32),
            jax.ShapeDtypeStruct((rows, width), BF16),
        ],
        compiler_params=pltpu.CompilerParams(vmem_limit_bytes=20 << 20),
        cost_estimate=SMALL,
    )(grads, weight)


def finish_kernel(
    halfway_ref,
    own_ref,
    away_ref,
    branch_ref,
    two_ref,
    two_away_ref,
    tokens_ref,
    mods_ref,
    result_ref,
    grad_ref,
):
    values = tokens_ref[...].astype(F32)
    two = two_ref[...] + two_away_ref[...].astype(F32)
    halfway = values + mods_ref[0, 2:3] * branch_ref[...]
    result_ref[...] = (halfway + mods_ref[0, 5:6] * two).astype(BF16)
    normed, inverse = normalize(values)
    grad_mod = own_ref[...] + away_ref[...].astype(F32)
    back = norm_back(grad_mod * (1.0 + mods_ref[0, 1:2]), normed, inverse)
    grad_ref[...] = (halfway_ref[...] + back).astype(BF16)


def finish(grad_halfway, own, away, branch, two, two_away, tokens, mods):
    rows, width = tokens.shape
    chunk = own.shape[0] // mods.shape[0]
    steps = rows // chunk
    row_block = pl.BlockSpec((chunk, width), lambda i: (i, 0))
    return pl.pallas_call(
        finish_kernel,
        grid=(steps,),
        in_specs=[
            row_block,
            row_block,
            row_block,
            row_block,
            row_block,
            row_block,
            row_block,
            pl.BlockSpec((1, 6, width), lambda i: (i, 0, 0)),
        ],
        out_specs=[row_block, row_block],
        out_shape=[jax.ShapeDtypeStruct((rows, width), BF16)] * 2,
        compiler_params=pltpu.CompilerParams(vmem_limit_bytes=16 << 20),
        cost_estimate=SMALL,
    )(grad_halfway, own, away, branch, two, two_away, tokens, mods)


def condition_kernel(grad_ref, weight_ref, out_ref):
    out_ref[...] = dot(grad_ref[...], weight_ref[...], 1, 1).astype(BF16)


def condition_part(grads, weight):
    rows, depth = weight.shape
    block = rows // 3
    return pl.pallas_call(
        condition_kernel,
        grid=(3,),
        in_specs=[
            pl.BlockSpec((grads.shape[0], depth), lambda i: (0, 0)),
            pl.BlockSpec((block, depth), lambda i: (i, 0)),
        ],
        out_specs=pl.BlockSpec((grads.shape[0], block), lambda i: (0, i)),
        out_shape=jax.ShapeDtypeStruct((grads.shape[0], rows), BF16),
        compiler_params=pltpu.CompilerParams(vmem_limit_bytes=14 << 20),
        cost_estimate=SMALL,
    )(grads, weight)


def ada_kernel(act_ref, grad_ref, out_ref):
    out_ref[...] = dot(act_ref[...], grad_ref[...], 0, 0)


def ada_gradient(act, grads, columns):
    block = columns // 9
    return pl.pallas_call(
        ada_kernel,
        grid=(9,),
        in_specs=[
            pl.BlockSpec(act.shape, lambda i: (0, 0)),
            pl.BlockSpec((act.shape[0], block), lambda i: (0, i)),
        ],
        out_specs=pl.BlockSpec((act.shape[1], block), lambda i: (0, i)),
        out_shape=jax.ShapeDtypeStruct((act.shape[1], columns), F32),
        compiler_params=pltpu.CompilerParams(vmem_limit_bytes=14 << 20),
        cost_estimate=SMALL,
    )(act, grads)


def middle_kernel(own_steps, first_ref, heads_ref, weight_ref, own_ref, away_ref, mods_ref, *outs):
    branch_ref, inputs_ref, normed_ref = outs
    branch = first_ref[...] + dot(heads_ref[...], weight_ref[...], 0, 0)
    is_own = pl.program_id(0) < own_steps
    values = jnp.where(is_own, own_ref[...].astype(F32), away_ref[...].astype(F32))
    normed, _ = normalize(values + mods_ref[0, 2:3] * branch)
    branch_ref[...] = branch
    inputs_ref[...] = (normed * (1.0 + mods_ref[0, 4:5]) + mods_ref[0, 3:4]).astype(BF16)
    normed_ref[...] = normed.astype(BF16)


def middle(first, heads_away, weight, own, away, mods):
    rows, width = first.shape
    steps = mods.shape[0]
    chunk = rows // steps
    own_steps = own.shape[0] // chunk
    row_block = pl.BlockSpec((chunk, width), lambda i: (i, 0))
    return pl.pallas_call(
        functools.partial(middle_kernel, own_steps),
        grid=(steps,),
        in_specs=[
            row_block,
            pl.BlockSpec((heads_away.shape[0], chunk), lambda i: (0, i)),
            pl.BlockSpec(weight.shape, lambda i: (0, 0)),
            pl.BlockSpec((chunk, width), lambda i: (jnp.minimum(i, own_steps - 1), 0)),
            pl.BlockSpec((chunk, width), lambda i: (jnp.maximum(i - own_steps, 0), 0)),
            pl.BlockSpec((1, 6, width), lambda i: (i, 0, 0)),
        ],
        out_specs=[row_block] * 3,
        out_shape=[
            jax.ShapeDtypeStruct((rows, width), F32),
            jax.ShapeDtypeStruct((rows, width), BF16),
            jax.ShapeDtypeStruct((rows, width), BF16),
        ],
        compiler_params=pltpu.CompilerParams(vmem_limit_bytes=14 << 20),
        cost_estimate=SMALL,
    )(first, heads_away, weight, own, away, mods)


def middle_back_kernel(
    half_steps, own_ref, first_ref, second_ref, branch_ref, tokens_ref, cot_ref, mods_ref, *outs
):
    grad_ref, low_ref, sums_ref = outs
    arrived = jnp.where(
        pl.program_id(0) < half_steps, first_ref[...].astype(F32), second_ref[...].astype(F32)
    )
    branch = branch_ref[...]
    gate = mods_ref[0, 2:3]
    normed, inverse = normalize(tokens_ref[...].astype(F32) + gate * branch)
    grad_mod = own_ref[...] + arrived
    grad = cot_ref[...].astype(F32) + norm_back(
        grad_mod * (1.0 + mods_ref[0, 4:5]), normed, inverse
    )
    grad_ref[...] = grad
    low_ref[...] = (grad * gate).astype(BF16)
    sums_ref[0] = jnp.sum(grad * branch, axis=0, keepdims=True)


def middle_back(own, first, second, branch, tokens, cot, mods):
    rows, width = own.shape
    chunk = branch.shape[0] // mods.shape[0]
    steps = rows // chunk
    half_steps = steps // 2
    row_block = pl.BlockSpec((chunk, width), lambda i: (i, 0))
    return pl.pallas_call(
        functools.partial(middle_back_kernel, half_steps),
        grid=(steps,),
        in_specs=[
            row_block,
            pl.BlockSpec((chunk, width), lambda i: (jnp.minimum(i, half_steps - 1), 0)),
            pl.BlockSpec((chunk, width), lambda i: (jnp.maximum(i - half_steps, 0), 0)),
            row_block,
            row_block,
            row_block,
            pl.BlockSpec((1, 6, width), lambda i: (i, 0, 0)),
        ],
        out_specs=[row_block, row_block, pl.BlockSpec((1, 1, width), lambda i: (i, 0, 0))],
        out_shape=[
            jax.ShapeDtypeStruct((rows, width), F32),
            jax.ShapeDtypeStruct((rows, width), BF16),
            jax.ShapeDtypeStruct((steps, 1, width), F32),
        ],
        compiler_params=pltpu.CompilerParams(vmem_limit_bytes=14 << 20),
        cost_estimate=SMALL,
    )(own, first, second, branch, tokens, cot, mods)


def pair_body(
    tokens,
    segments,
    labels,
    timesteps,
    class_table,
    time_weight,
    ada_weight,
    qkv_weight,
    proj_weight,
    up_weight,
    down_weight,
    cotangent,
):
    position = lax.axis_index("tensor")
    rank = lax.axis_index("dp")
    dp_size = 16
    core, line, deep = rank % 2, rank // 2 % 2, rank // 4 % 2
    own_low = tokens[0]
    cot_low = cotangent[0]
    shard, width = own_low.shape
    pack = segments.shape[1]
    slot_count = labels.shape[1]
    class_count = class_table.shape[0]
    freq_width = time_weight.shape[0]
    local_width = qkv_weight.shape[2]
    heads = local_width // HEAD_DIM
    half_heads = heads // 2
    half_width = local_width // 2
    hidden_width = up_weight.shape[1]
    chunk = shard * SHORT // pack
    own_chunks = shard // chunk
    CORE, LINE, DEEP, FAR = 1, 2, 4, 8

    def fence(*values):
        return lax.optimization_barrier(values)

    def swap(x):
        return lax.ppermute(x, "tensor", [(0, 1), (1, 0)])

    def trade(x, bits):
        return lax.ppermute(x, "dp", [(i, i ^ bits) for i in range(dp_size)])

    def rows_of(x, index, count):
        size = x.shape[0] // count
        return lax.dynamic_slice_in_dim(x, index * size, size, 0)

    def columns_of(x, index, count):
        size = x.shape[1] // count
        return lax.dynamic_slice_in_dim(x, index * size, size, 1)

    def plus(a, b):
        return (a.astype(F32) + b.astype(F32)).astype(BF16)

    def halve(x, digit, bits):
        return plus(rows_of(x, digit, 2), trade(rows_of(x, 1 - digit, 2), bits))

    def digit(me, bits):
        return me // bits % 2

    def down_place(ref, me, group, block):
        index = (
            (digit(me, CORE) + group // 2) % 2 * 4
            + (digit(me, LINE) + group) % 2 * 2
            + (digit(me, DEEP) + block) % 2
        )
        return ref.at[index]

    def proj_place(ref, me, group, block):
        index = (digit(me, CORE) + group // 2) % 2 * 4 + (digit(me, LINE) + group % 2) % 2 * 2
        return ref.at[index + block - 3]

    def up_place(ref, me, group, block):
        index = (digit(me, LINE) + group) % 2 * 2 + (digit(me, DEEP) + block) % 2
        column = (digit(me, CORE) + group // 2) % 2 * (hidden_width // 2)
        return ref.at[index, :, pl.ds(pl.multiple_of(column, 128), hidden_width // 2)]

    def qkv_place(offset, bits):
        def place(ref, me, group, block):
            unit = (
                (digit(me, CORE) + group // 2) % 2 * 2 + (digit(me, bits) + group % 2) % 2
            ) * 3 + block
            return ref.at[unit // half_heads * heads + unit % half_heads + offset]

        return place

    def chunked(x):
        return x.reshape(x.shape[0] // chunk, chunk, x.shape[1])

    def flat(x):
        return x.reshape(x.shape[0] * chunk, x.shape[2])

    quarter = shard // 2
    tokens_away = swap(own_low)
    ids = jnp.stack([labels[0], timesteps[0]], axis=1)

    seg = segments[0]
    seg = jnp.where(position == 0, seg, jnp.roll(seg, shard))
    slots = jnp.arange(slot_count, dtype=jnp.int32)
    chunk_hot = (seg[::chunk][:, None] == slots[None, :]).astype(F32)
    mask_rows = -(-slot_count // 8) * 8
    same = jnp.arange(mask_rows, dtype=jnp.int32)[:, None] == seg[None, :]
    hot = same.astype(BF16)
    bias = jnp.where(same, 0.0, -1e30).astype(BF16)

    classes = jnp.arange(class_count, dtype=jnp.int32)

    def condition_of(ids):
        label_hot = (ids[:, 0][:, None] == classes[None, :]).astype(F32)
        feats = features(ids[:, 1].astype(F32), freq_width)
        values = dot(label_hot, class_table, 1, 0, HIGH) + dot(feats, time_weight, 1, 0, HIGH)
        return label_hot, feats, values

    def hop(y, bits):
        return jnp.concatenate([y, trade(y, bits)], axis=0)

    condition = condition_of(ids)[2]
    ids = hop(hop(ids[None], LINE), FAR)
    act_low = jax.nn.silu(condition).astype(BF16)
    mod_part, tokens_away, proj_half, ids = fence(
        dot(act_low, ada_weight, 1, 0), tokens_away, rows_of(proj_weight, core, 2), ids
    )
    ids = hop(ids, DEEP)
    mod_away = swap(mod_part)
    modulation = jnp.where(
        position == 0,
        jnp.concatenate([mod_part, mod_away], axis=1),
        jnp.concatenate([mod_away, mod_part], axis=1),
    )
    proj_half = swap(proj_half)
    per_chunk = dot(chunk_hot, modulation, 1, 0, HIGH)
    mods_own = [m[:, None, :] for m in jnp.split(per_chunk[:own_chunks], 6, axis=1)]
    mods_other = [m[:, None, :] for m in jnp.split(per_chunk[own_chunks:], 6, axis=1)]

    weight_t = qkv_weight.transpose(1, 2, 0).reshape(3 * local_width, width)

    def enter(low, mods):
        values = chunked(low.astype(F32))
        normed, inverse = normalize(values)
        inputs = flat((normed * (1.0 + mods[1]) + mods[0]).astype(BF16))
        return values, normed, inverse, inputs

    def project(inputs):
        return dot(weight_t, inputs, 1, 1).astype(BF16).reshape(3 * heads, HEAD_DIM, shard)

    tokens_own, normed_one, inverse_one, inputs_one_own = enter(own_low, mods_own)
    qkv_own = project(inputs_one_own)
    tokens_other, normed_one_other, _, inputs_one_other = enter(tokens_away, mods_other)
    qkv_other = project(inputs_one_other)
    out_a, lse_a = attend(qkv_own, qkv_other, bias, hot, 0, half_heads)
    out_a, qkv_own, ids = fence(out_a, qkv_own, ids)
    ids = hop(ids, CORE)
    away_a = swap(out_a.reshape(half_width, pack))
    out_b, lse_b = attend(qkv_own, qkv_other, bias, hot, half_heads, half_heads)
    out_b, proj_half, ids = fence(out_b, proj_half, ids)
    ids_all = ids.reshape(dp_size * slot_count, 2)
    away_b = swap(out_b.reshape(half_width, pack))
    proj_rest = trade(proj_half, CORE)
    proj_other = jnp.where(
        core == 0,
        jnp.concatenate([proj_half, proj_rest], axis=0),
        jnp.concatenate([proj_rest, proj_half], axis=0),
    )
    out_flat = jnp.concatenate([out_a, out_b], axis=0).reshape(local_width, pack)
    own_part, other_part = slice(0, shard), slice(shard, pack)

    def reordered(away):
        return jnp.concatenate([away[:, other_part], away[:, own_part]], axis=1)

    weight_parts = weight_t.reshape(3, 2, half_width, width)
    weight_a = weight_parts[:, 0].reshape(3 * half_width, width)
    weight_b = weight_parts[:, 1].reshape(3 * half_width, width)
    away_a, proj_other, weight_a, weight_b = fence(away_a, proj_other, weight_a, weight_b)
    first = dot(
        jnp.concatenate([out_flat, reordered(away_a)], axis=0),
        jnp.concatenate([proj_weight, proj_other[:half_width]], axis=0),
        0,
        0,
    )
    away_b, cot_a, cot_b, first = fence(away_b, cot_low[:quarter], cot_low[quarter:], first)
    cot_away_a = swap(cot_a)
    chunk_mods = per_chunk.reshape(pack // chunk, 6, width)
    branch_one, inputs_two, normed_two = middle(
        first, reordered(away_b), proj_other[half_width:], own_low, tokens_away, chunk_mods
    )
    inputs_two, cot_away_a, cot_b = fence(inputs_two, cot_away_a, cot_b)
    cot_away_b = swap(cot_b)

    active, slope = hidden_units(inputs_two, up_weight)
    active, slope, cot_away_b = fence(active, slope, cot_away_b)
    cot_away = jnp.concatenate([cot_away_a, cot_away_b], axis=0)
    grad_branch_two = jnp.concatenate(
        [
            flat((chunked(cot_low.astype(F32)) * mods_own[5]).astype(BF16)),
            flat((chunked(cot_away.astype(F32)) * mods_other[5]).astype(BF16)),
        ],
        axis=0,
    )

    down_away = trade(down_gradient(active, grad_branch_two, 1 - core), CORE)
    grad_hidden = hidden_back(grad_branch_two, down_weight, slope)
    down_sum = down_gradient(active, grad_branch_two, core, down_away)
    down_sum, grad_hidden = fence(down_sum, grad_hidden)
    down_x = trade(rows_of(down_sum, 1 - line, 2), LINE)
    mod_two_other, mod_two_away = rows_back(grad_hidden, up_weight, 1)
    mod_two_away, grad_hidden = fence(mod_two_away, grad_hidden)

    arrived_a = swap(mod_two_away[:quarter])
    up_away = trade(up_gradient(inputs_two, grad_hidden, 1 - core), CORE)
    mod_two, _ = rows_back(grad_hidden, up_weight, 0)
    arrived_a, up_away, mod_two, mod_two_next, grad_hidden, active = fence(
        arrived_a, up_away, mod_two, mod_two_away[quarter:], grad_hidden, active
    )
    arrived_b = swap(mod_two_next)
    up_sum = up_gradient(inputs_two, grad_hidden, core, up_away)
    up_x = trade(rows_of(up_sum, 1 - line, 2), LINE)
    branch_two_away = dot(active[other_part], down_weight, 1, 0)
    branch_two = dot(active[own_part], down_weight, 1, 0)
    arrived_b, mod_two, branch_two_away, branch_two, down_x = fence(
        arrived_b, mod_two, branch_two_away, branch_two, down_x
    )

    down_sum = plus(rows_of(down_sum, line, 2), down_x)
    down_z = trade(rows_of(down_sum, 1 - deep, 2), DEEP)
    grad_halfway, grad_branch_one, gate_one_sums = middle_back(
        mod_two, arrived_a, arrived_b, branch_one, own_low, cot_low, chunk_mods
    )
    grad_att_away = dot(proj_other, grad_branch_one, 1, 1).astype(BF16)
    grad_att_away, grad_branch_one = fence(grad_att_away, grad_branch_one)

    grad_att_other = swap(grad_att_away)
    grad_att_own = dot(proj_weight, grad_branch_one, 1, 1).astype(BF16)
    inputs_one = jnp.concatenate([inputs_one_own, inputs_one_other], axis=0)
    def chunk_sums(own, other):
        return jnp.concatenate([jnp.sum(own, axis=1), jnp.sum(other, axis=1)], axis=0)

    normed_two = chunked(normed_two.astype(F32))
    late_terms = jnp.concatenate(
        [
            jnp.concatenate([gate_one_sums[:, 0], jnp.zeros_like(gate_one_sums[:, 0])], axis=0),
            chunk_sums(chunked(mod_two), chunked(mod_two_other)),
            chunk_sums(
                chunked(mod_two) * normed_two[:own_chunks],
                chunked(mod_two_other) * normed_two[own_chunks:],
            ),
            chunk_sums(
                chunked(branch_two) * chunked(cot_low.astype(F32)),
                chunked(branch_two_away) * chunked(cot_away.astype(F32)),
            ),
        ],
        axis=1,
    )
    grad_att_other, grad_att_own, down_z, branch_one_next, inputs_one, late_terms = fence(
        grad_att_other, grad_att_own, down_z, grad_branch_one, inputs_one, late_terms
    )
    down_sum = plus(rows_of(down_sum, deep, 2), down_z)
    down_block = down_sum.shape[0] // 2
    down_far_a = trade(down_sum[:down_block], FAR)

    def back(out, lse, first):
        return attend_back(
            qkv_own,
            qkv_other,
            bias,
            hot,
            out,
            grad_att_own.reshape(heads, HEAD_DIM, shard),
            grad_att_other.reshape(heads, HEAD_DIM, shard),
            lse,
            first,
            half_heads,
        ).reshape(3 * half_width, pack)

    def qkv_half(grad):
        return lambda half: dot(rows_of(grad, half, 2), inputs_one, 1, 0)

    grads_one_other = swap(branch_one_next)
    grad_qkv_a = back(out_a, lse_a, 0)
    grad_qkv_a, up_x, down_far_a, down_next = fence(
        grad_qkv_a, up_x, down_far_a, down_sum[down_block:]
    )
    down_far_b = trade(down_next, FAR)
    up_sum = plus(rows_of(up_sum, line, 2), up_x)
    up_z = trade(rows_of(up_sum, 1 - deep, 2), DEEP)
    qkv_make = qkv_half(grad_qkv_a)
    qkv_a_away = trade(qkv_make(1 - core).astype(BF16), CORE)
    qkv_a = plus(qkv_make(core), qkv_a_away)
    qkv_a, grad_att_own = fence(qkv_a, grad_att_own)
    qkv_a_x = trade(rows_of(qkv_a, 1 - line, 2), LINE)
    grad_qkv_b = back(out_b, lse_b, half_heads)
    grad_qkv_b, qkv_a_x, up_z, down_far_b, grads_one_other = fence(
        grad_qkv_b, qkv_a_x, up_z, down_far_b, grads_one_other
    )
    qkv_a = plus(rows_of(qkv_a, line, 2), qkv_a_x)
    up_sum = plus(rows_of(up_sum, deep, 2), up_z)
    down_sum = plus(down_sum, jnp.concatenate([down_far_a, down_far_b], axis=0))
    down_z = trade(down_sum, DEEP)
    down_x = trade(down_sum, LINE)
    block = up_sum.shape[0] // 2
    up_far_a = trade(up_sum[:block], FAR)
    mod_one = dot(grad_qkv_a, weight_a, 0, 0) + dot(grad_qkv_b, weight_b, 0, 0)
    mod_one_own, mod_one_away = chunked(mod_one[own_part]), chunked(mod_one[other_part])
    chunk_terms = jnp.concatenate(
        [
            chunk_sums(mod_one_own, mod_one_away),
            chunk_sums(mod_one_own * normed_one, mod_one_away * normed_one_other),
            late_terms,
        ],
        axis=1,
    )
    slot_terms = dot(chunk_hot, chunk_terms, 0, 0, HIGH).astype(BF16)
    half = slot_terms.shape[1] // 2
    low, high = slot_terms[:, :half], slot_terms[:, half:]
    keep = jnp.where(position == 0, low, high)
    away = jnp.where(position == 0, high, low)
    (
        away,
        keep,
        mod_one_next,
        down_z,
        down_x,
        up_far_a,
        grad_qkv_b,
        up_next,
        qkv_a,
    ) = fence(
        away,
        keep,
        flat(mod_one_away).astype(BF16),
        down_z,
        down_x,
        up_far_a,
        grad_qkv_b,
        up_sum[block:],
        qkv_a,
    )

    gathered = plus(keep, swap(away))[None]
    down_zx = trade(down_z, LINE)
    up_far_b = trade(up_next, FAR)
    qkv_a_z = trade(rows_of(qkv_a, 1 - deep, 2), DEEP)
    qkv_make_b = qkv_half(grad_qkv_b)

    def proj_half_of(half):
        rows = rows_of(out_flat, half, 2)
        return dot(rows[:, own_part], grad_branch_one, 1, 0) + dot(
            rows[:, other_part], grads_one_other, 1, 0
        )

    rest = trade(
        jnp.concatenate(
            [qkv_make_b(1 - core).astype(BF16), proj_half_of(1 - core).astype(BF16)], axis=0
        ),
        CORE,
    )
    qkv_rows = 3 * half_width // 2
    qkv_b = plus(qkv_make_b(core), rest[:qkv_rows])
    proj_sum = plus(proj_half_of(core), rest[qkv_rows:])
    gathered, up_far_b, down_zx, qkv_a_z, qkv_b, proj_sum, mod_one_next, ids_all = fence(
        gathered, up_far_b, down_zx, qkv_a_z, qkv_b, proj_sum, mod_one_next, ids_all
    )

    def packed(qkv, proj, index):
        return jnp.concatenate([rows_of(qkv, index, 2), rows_of(proj, index, 2)], axis=0)

    def unpacked(both):
        cut = both.shape[0] * 3 // 5
        return both[:cut], both[cut:]

    def in_order(digit, own, other):
        return jnp.where(
            digit == 0,
            jnp.concatenate([own, other], axis=0),
            jnp.concatenate([other, own], axis=0),
        )

    up_low = plus(up_sum[:block], up_far_a)
    up_high = plus(up_next, up_far_b)
    up_sum = jnp.concatenate([up_low, up_high], axis=0)
    qkv_a = plus(rows_of(qkv_a, deep, 2), qkv_a_z)
    both_next = packed(qkv_b, proj_sum, 1 - line)
    up_sum, qkv_a, both_next, gathered, mod_one_next = fence(
        up_sum, qkv_a, both_next, gathered, mod_one_next
    )
    gathered = hop(gathered, LINE)
    mod_one_other = swap(mod_one_next)
    label_hot, features_all, condition_all = condition_of(ids_all)
    act_all = jax.nn.silu(condition_all).astype(BF16)
    both_x = trade(both_next, LINE)
    up_z = trade(up_sum, DEEP)
    qkv_a_far = trade(qkv_a, FAR)
    both = packed(qkv_b, proj_sum, line)
    (
        act_all,
        gathered,
        both_x,
        up_z,
        qkv_a_far,
        mod_one_other,
        both,
        down_sum,
        down_z,
        down_x,
        down_zx,
    ) = fence(
        act_all,
        gathered,
        both_x,
        up_z,
        qkv_a_far,
        mod_one_other,
        both,
        down_sum,
        down_z,
        down_x,
        down_zx,
    )
    both = plus(both, both_x)
    both_next = packed(*unpacked(both), 1 - deep)
    qkv_a = plus(qkv_a, qkv_a_far)
    both_next, qkv_a, gathered, up_sum, both, two_next = fence(
        both_next, qkv_a, gathered, up_sum, both, branch_two_away.astype(BF16)
    )
    gathered = hop(gathered, FAR)
    up_x = trade(up_sum, LINE)
    down_blocks = [jnp.stack([down_sum, down_z]), jnp.stack([down_x, down_zx])]
    down_blocks += [trade(b, CORE) for b in down_blocks]
    both_z = trade(both_next, DEEP)
    qkv_a_z = trade(qkv_a, DEEP)
    both = packed(*unpacked(both), deep)
    gathered, up_x, both_z, qkv_a_z, both, *down_blocks = fence(
        gathered, up_x, both_z, qkv_a_z, both, *down_blocks
    )
    both = plus(both, both_z)
    qkv_a = in_order(deep, qkv_a, qkv_a_z).reshape(3, HEAD_DIM, width)
    both, qkv_a, gathered, up_z, two_next = fence(both, qkv_a, gathered, up_z, two_next)
    branch_two_other = swap(two_next)
    grad_down = write_out(down_blocks, down_place, (8, hidden_width // 8, width))
    gathered = hop(gathered, DEEP)
    up_zx = trade(up_z, LINE)
    qkv_a_x = trade(qkv_a, LINE)
    both_far = trade(both, FAR)
    up_zx, qkv_a_x, both_far, gathered, branch_two_other, grad_down = fence(
        up_zx, qkv_a_x, both_far, gathered, branch_two_other, grad_down
    )
    both = plus(both, both_far)
    up_blocks = [jnp.stack([up_sum, up_z]), jnp.stack([up_x, up_zx])]
    both, gathered, *up_blocks = fence(both, gathered, *up_blocks)
    grad_mod_all = hop(gathered, CORE).reshape(dp_size * slot_count, half)
    cond_part = condition_part(grad_mod_all, ada_weight)
    both_z = trade(both, DEEP)
    result, grad_input = finish(
        grad_halfway,
        mod_one,
        mod_one_other,
        branch_one,
        branch_two,
        branch_two_other,
        own_low,
        chunk_mods,
    )
    up_blocks += [trade(b, CORE) for b in up_blocks]
    both_z, cond_part, result, *up_blocks = fence(both_z, cond_part, result, *up_blocks)
    both = jnp.concatenate(
        [in_order(deep, a, b) for a, b in zip(unpacked(both), unpacked(both_z), strict=True)],
        axis=0,
    ).reshape(5, HEAD_DIM, width)
    both_x = trade(both, LINE)
    both_c = trade(both, CORE)
    grad_act = cond_part.astype(F32) + swap(cond_part).astype(F32)
    qkv_a_c = trade(qkv_a, CORE)
    qkv_a_xc = trade(qkv_a_x, CORE)
    grad_up = write_out(up_blocks, up_place, (4, width // 4, hidden_width))
    grad_ada = ada_gradient(act_all, grad_mod_all, ada_weight.shape[1])
    both_x, both_c, grad_up, grad_act, grad_ada, qkv_a_c, qkv_a_xc = fence(
        both_x, both_c, grad_up, grad_act, grad_ada, qkv_a_c, qkv_a_xc
    )
    both_xc = trade(both_x, CORE)
    qkv_shape = (3 * heads, HEAD_DIM, width)
    grad_qkv = write_out([qkv_a, qkv_a_x, qkv_a_c, qkv_a_xc], qkv_place(0, LINE), qkv_shape)

    grad_condition = jax.vjp(jax.nn.silu, condition_all)[1](grad_act)[0]
    grad_class = dot(label_hot.astype(BF16), grad_condition.astype(BF16), 0, 0)
    grad_time = dot(features_all, grad_condition, 0, 0, HIGH)
    groups = [both, both_x, both_c, both_xc]
    grad_qkv = write_out(groups, qkv_place(half_heads, LINE), qkv_shape, grad_qkv, (0, 3))
    grad_proj = write_out(groups, proj_place, (8, HEAD_DIM, width), None, (3, 5))
    return (
        result[None],
        grad_input[None],
        grad_class,
        grad_time,
        grad_ada,
        grad_qkv.reshape(3, local_width, width).transpose(2, 0, 1),
        grad_proj.reshape(local_width, width),
        grad_up.reshape(width, hidden_width),
        grad_down.reshape(hidden_width, width),
    )


def any_body(
    tokens,
    segments,
    labels,
    timesteps,
    class_table,
    time_weight,
    ada_weight,
    qkv_weight,
    proj_weight,
    up_weight,
    down_weight,
    cotangent,
):
    own_tokens = tokens[0].astype(jnp.float32)
    shard_rows = own_tokens.shape[0]
    model_width = own_tokens.shape[1]
    seg_all = segments[0]
    pack_rows = seg_all.shape[0]
    slot_count = labels.shape[1]
    class_count = class_table.shape[0]
    freq_width = time_weight.shape[0]
    local_width = qkv_weight.shape[2]
    head_count = local_width // HEAD_DIM
    scale_factor = 1.0 / math.sqrt(HEAD_DIM)
    position = lax.axis_index("tensor")
    seg_own = lax.dynamic_slice_in_dim(seg_all, position * shard_rows, shard_rows)
    own_hot = (seg_own[:, None] == jnp.arange(slot_count, dtype=jnp.int32)[None, :]).astype(
        jnp.float32
    )
    label_hot = (labels[0][:, None] == jnp.arange(class_count, dtype=jnp.int32)[None, :]).astype(
        jnp.float32
    )
    step_feats = features(timesteps[0].astype(jnp.float32), freq_width)
    condition = jnp.dot(label_hot, class_table, precision=HIGH) + jnp.dot(
        step_feats, time_weight, precision=HIGH
    )
    act_low = jax.nn.silu(condition).astype(jnp.bfloat16)
    mod_part = jnp.dot(act_low, ada_weight, preferred_element_type=jnp.float32)
    modulation = lax.all_gather(mod_part, "tensor", axis=1, tiled=True)
    per_token = jnp.dot(own_hot, modulation, precision=HIGH)
    shift_one, scale_one, gate_one, shift_two, scale_two, gate_two = jnp.split(per_token, 6, axis=1)
    normed_one, inverse_one = normalize(own_tokens)
    modulated_one = (normed_one * (1.0 + scale_one) + shift_one).astype(jnp.bfloat16)
    inputs_one = lax.all_gather(modulated_one, "tensor", axis=0, tiled=True)
    qkv_flat = qkv_weight.reshape(model_width, 3 * local_width)
    qkv = jnp.dot(inputs_one, qkv_flat, preferred_element_type=jnp.float32).astype(jnp.bfloat16)
    qkv_heads = qkv.reshape(pack_rows, 3, head_count, HEAD_DIM).transpose(1, 2, 0, 3)
    queries = qkv_heads[0]
    keys = qkv_heads[1]
    values = qkv_heads[2]
    block = min(512, pack_rows)
    block_count = pack_rows // block
    starts = jnp.arange(block_count, dtype=jnp.int32) * block

    def scores_of(start):
        query_block = lax.dynamic_slice_in_dim(queries, start, block, 1)
        seg_block = lax.dynamic_slice_in_dim(seg_all, start, block)
        raw = (
            jnp.einsum("hqd,hkd->hqk", query_block, keys, preferred_element_type=jnp.float32)
            * scale_factor
        )
        same = (seg_block[:, None] == seg_all[None, :])[None]
        return (jnp.where(same, raw, -1e30), query_block)

    def attend(start):
        scores = scores_of(start)[0]
        top = jnp.max(scores, axis=-1, keepdims=True)
        exps = jnp.exp(scores - top)
        total = jnp.sum(exps, axis=-1, keepdims=True)
        weights = (exps / total).astype(jnp.bfloat16)
        out_block = jnp.einsum("hqk,hkd->hqd", weights, values, preferred_element_type=jnp.float32)
        return (out_block, (top + jnp.log(total))[..., 0])

    out_blocks, lse_blocks = lax.map(attend, starts)
    attended = out_blocks.transpose(0, 2, 1, 3).reshape(pack_rows, local_width).astype(jnp.bfloat16)
    lse_all = lse_blocks.transpose(1, 0, 2).reshape(head_count, pack_rows)
    branch_one = lax.psum_scatter(
        jnp.dot(attended, proj_weight, preferred_element_type=jnp.float32),
        "tensor",
        scatter_dimension=0,
        tiled=True,
    )
    halfway = own_tokens + gate_one * branch_one
    normed_two, inverse_two = normalize(halfway)
    modulated_two = (normed_two * (1.0 + scale_two) + shift_two).astype(jnp.bfloat16)
    inputs_two = lax.all_gather(modulated_two, "tensor", axis=0, tiled=True)
    hidden = jnp.dot(inputs_two, up_weight, preferred_element_type=jnp.float32)
    active = jax.nn.gelu(hidden, approximate=True).astype(jnp.bfloat16)
    branch_two = lax.psum_scatter(
        jnp.dot(active, down_weight, preferred_element_type=jnp.float32).astype(jnp.bfloat16),
        "tensor",
        scatter_dimension=0,
        tiled=True,
    ).astype(jnp.float32)
    result = halfway + gate_two * branch_two
    grad_out = cotangent[0].astype(jnp.float32)
    grad_gate_two = grad_out * branch_two
    grad_branch_two = (grad_out * gate_two).astype(jnp.bfloat16)
    grads_two = lax.all_gather(grad_branch_two, "tensor", axis=0, tiled=True)
    grad_down = contract_rows(active, grads_two)
    grad_active = times_transposed(grads_two, down_weight)
    gelu_back = jax.vjp(lambda inner: jax.nn.gelu(inner, approximate=True), hidden)[1]
    grad_hidden = gelu_back(grad_active)[0].astype(jnp.bfloat16)
    grad_up = contract_rows(inputs_two, grad_hidden)
    grad_mod_two = lax.psum_scatter(
        times_transposed(grad_hidden, up_weight), "tensor", scatter_dimension=0, tiled=True
    )
    grad_halfway = grad_out + norm_back(grad_mod_two * (1.0 + scale_two), normed_two, inverse_two)
    grad_gate_one = grad_halfway * branch_one
    grad_branch_one = (grad_halfway * gate_one).astype(jnp.bfloat16)
    grads_one = lax.all_gather(grad_branch_one, "tensor", axis=0, tiled=True)
    grad_proj = contract_rows(attended, grads_one)
    grad_attended = times_transposed(grads_one, proj_weight).astype(jnp.bfloat16)
    grad_heads = grad_attended.reshape(pack_rows, head_count, HEAD_DIM).transpose(1, 0, 2)

    def attend_back(carry, start):
        grad_keys, grad_values = carry
        scores, query_block = scores_of(start)
        lse_block = lax.dynamic_slice_in_dim(lse_all, start, block, 1)
        probs = jnp.exp(scores - lse_block[..., None])
        grad_block = lax.dynamic_slice_in_dim(grad_heads, start, block, 1)
        grad_probs = jnp.einsum(
            "hqd,hkd->hqk", grad_block, values, preferred_element_type=jnp.float32
        )
        grad_scores = (
            probs * (grad_probs - jnp.sum(probs * grad_probs, axis=-1, keepdims=True))
        ).astype(jnp.bfloat16)
        grad_query = (
            jnp.einsum("hqk,hkd->hqd", grad_scores, keys, preferred_element_type=jnp.float32)
            * scale_factor
        )
        grad_keys = (
            grad_keys
            + jnp.einsum(
                "hqk,hqd->hkd", grad_scores, query_block, preferred_element_type=jnp.float32
            )
            * scale_factor
        )
        grad_values = grad_values + jnp.einsum(
            "hqk,hqd->hkd",
            probs.astype(jnp.bfloat16),
            grad_block,
            preferred_element_type=jnp.float32,
        )
        return ((grad_keys, grad_values), grad_query)

    empty = jnp.zeros((head_count, pack_rows, HEAD_DIM), jnp.float32)
    key_grads, grad_queries = lax.scan(attend_back, (empty, empty), starts)
    query_grads = grad_queries.transpose(1, 0, 2, 3).reshape(head_count, pack_rows, HEAD_DIM)
    grad_stack = jnp.stack([query_grads, key_grads[0], key_grads[1]], axis=0)
    grad_qkv = (
        grad_stack.transpose(2, 0, 1, 3).reshape(pack_rows, 3 * local_width).astype(jnp.bfloat16)
    )
    grad_qkv_weight = contract_rows(inputs_one, grad_qkv).reshape(model_width, 3, local_width)
    grad_mod_one = lax.psum_scatter(
        times_transposed(grad_qkv, qkv_flat).astype(jnp.bfloat16),
        "tensor",
        scatter_dimension=0,
        tiled=True,
    ).astype(jnp.float32)
    grad_input = grad_halfway + norm_back(grad_mod_one * (1.0 + scale_one), normed_one, inverse_one)
    grad_per_token = jnp.concatenate(
        [
            grad_mod_one,
            grad_mod_one * normed_one,
            grad_gate_one,
            grad_mod_two,
            grad_mod_two * normed_two,
            grad_gate_two,
        ],
        axis=1,
    )
    slot_terms = contract_exact(own_hot, grad_per_token)
    grad_modulation = lax.psum_scatter(
        slot_terms.astype(jnp.bfloat16), "tensor", scatter_dimension=1, tiled=True
    )
    grad_ada = contract_rows(act_low, grad_modulation)
    cond_part = times_transposed(grad_modulation, ada_weight)
    grad_activated = lax.psum(cond_part.astype(jnp.bfloat16), "tensor").astype(jnp.float32)
    grad_condition = jax.vjp(jax.nn.silu, condition)[1](grad_activated)[0]
    grad_class = contract_exact(label_hot, grad_condition)
    grad_time = contract_exact(step_feats, grad_condition)
    summed = (
        lax.psum(grad_class.astype(jnp.bfloat16), "dp").astype(jnp.float32),
        lax.psum(grad_time.astype(jnp.bfloat16), "dp").astype(jnp.float32),
        lax.psum(grad_ada.astype(jnp.bfloat16), "dp").astype(jnp.float32),
        lax.psum(grad_qkv_weight.astype(jnp.bfloat16), "dp").astype(jnp.float32),
        lax.psum(grad_proj.astype(jnp.bfloat16), "dp").astype(jnp.float32),
        lax.psum(grad_up.astype(jnp.bfloat16), "dp").astype(jnp.float32),
        lax.psum(grad_down.astype(jnp.bfloat16), "dp").astype(jnp.float32),
    )
    grad_class, grad_time, grad_ada, grad_qkv_weight, grad_proj, grad_up, grad_down = summed
    return (
        result.astype(jnp.bfloat16)[None],
        grad_input.astype(jnp.bfloat16)[None],
        grad_class,
        grad_time,
        grad_ada,
        grad_qkv_weight,
        grad_proj,
        grad_up,
        grad_down,
    )


def solution(mesh):
    pairs = mesh.shape["dp"] == 16 and mesh.shape["tensor"] == 2
    return jax.shard_map(
        pair_body if pairs else any_body,
        mesh=mesh,
        in_specs=(
            P("dp", "tensor", None),
            P("dp", None),
            P("dp", None),
            P("dp", None),
            P(),
            P(),
            P(None, "tensor"),
            P(None, None, "tensor"),
            P("tensor", None),
            P(None, "tensor"),
            P("tensor", None),
            P("dp", "tensor", None),
        ),
        out_specs=(
            P("dp", "tensor", None),
            P("dp", "tensor", None),
            P(),
            P(),
            P(None, "tensor"),
            P(None, None, "tensor"),
            P("tensor", None),
            P(None, "tensor"),
            P("tensor", None),
        ),
        check_vma=False,
    )
```

```python
import functools
import math

import jax
import jax.numpy as jnp
from jax import lax
from jax.experimental import pallas as pl
from jax.experimental.pallas import tpu as pltpu
from jax.sharding import PartitionSpec as P

HEAD_DIM = 72
SHORT = 256
HIGH = lax.Precision.HIGHEST
F32 = jnp.float32
BF16 = jnp.bfloat16
SCALE = 1.0 / math.sqrt(HEAD_DIM)
SCALE_LOG2 = SCALE * math.log2(math.e)


def dot(left, right, left_dim, right_dim, precision=None):
    return lax.dot_general(
        left,
        right,
        (((left_dim,), (right_dim,)), ((), ())),
        precision=precision,
        preferred_element_type=F32,
    )


def features(steps_f, width_total):
    half = width_total // 2
    freqs = jnp.exp(-math.log(10000.0) * jnp.arange(half, dtype=F32) / half)
    angles = steps_f[:, None] * freqs[None, :]
    return jnp.concatenate([jnp.cos(angles), jnp.sin(angles)], axis=1)


def contract_rows(left, right):
    return dot(left, right, 0, 0)


def contract_exact(left, right):
    return dot(left, right, 0, 0, HIGH)


def times_transposed(left, right):
    return dot(left, right, 1, 1)


def normalize(values):
    average = jnp.mean(values, axis=-1, keepdims=True)
    centred = values - average
    inverse = lax.rsqrt(jnp.mean(centred * centred, axis=-1, keepdims=True) + 1e-06)
    return centred * inverse, inverse


def norm_back(grad_normed, normed, inverse):
    first = jnp.mean(grad_normed, axis=-1, keepdims=True)
    second = jnp.mean(grad_normed * normed, axis=-1, keepdims=True)
    return inverse * (grad_normed - first - normed * second)


def gelu_parts(x):
    root = math.sqrt(2.0 / math.pi)
    square = x * x
    bent = jnp.tanh(root * x * (1.0 + 0.044715 * square))
    half = 0.5 * (1.0 + bent)
    slope = half + 0.5 * x * (1.0 - bent * bent) * root * (1.0 + 3 * 0.044715 * square)
    return x * half, slope


def joined(own, other):
    return jnp.concatenate([own[0], other[0]], axis=1)


def attend_kernel(block, q0, q1, k0, k1, v0, v1, bias_ref, hot_ref, o_ref, lse_ref):
    tokens = o_ref.shape[2]
    query = jnp.concatenate([joined(q0, q1), bias_ref[...]], axis=0)
    key = jnp.concatenate([joined(k0, k1), hot_ref[...]], axis=0).T
    value = joined(v0, v1)
    for start in range(0, tokens, block):
        part = slice(start, start + block)
        scores = dot(key, query[:, part], 1, 0)
        top = jnp.max(scores, axis=0, keepdims=True) * SCALE_LOG2
        exps = jnp.exp2(scores * SCALE_LOG2 - top)
        total = jnp.sum(exps, axis=0, keepdims=True)
        out = dot(value, exps.astype(BF16), 1, 0)
        o_ref[0, :, part] = (out / total).astype(BF16)
        lse_ref[0, :, part] = top + jnp.log2(total)


def attend_back_kernel(
    block, q0, q1, k0, k1, v0, v1, bias_ref, hot_ref, o_ref, do0, do1, lse_ref, grad_ref
):
    tokens = o_ref.shape[2]
    query_all, key_all = joined(q0, q1), joined(k0, k1)
    query = jnp.concatenate([query_all, bias_ref[...]], axis=0)
    key = jnp.concatenate([key_all, hot_ref[...]], axis=0).T
    value = joined(v0, v1).T
    query_rows = query_all.T
    grad_out = joined(do0, do1)
    grad_rows = grad_out.T
    delta = jnp.sum(grad_out.astype(F32) * o_ref[0].astype(F32), axis=0, keepdims=True)
    lse = lse_ref[0]
    grad_key = grad_value = None
    for start in range(0, tokens, block):
        part = slice(start, start + block)
        scores = dot(key, query[:, part], 1, 0)
        probs = jnp.exp2(scores * SCALE_LOG2 - lse[:, part])
        grad_probs = dot(value, grad_out[:, part], 1, 0)
        grad_scores = (probs * (grad_probs - delta[:, part])).astype(BF16)
        value_term = dot(probs.astype(BF16), grad_rows[part], 1, 0)
        key_term = dot(grad_scores, query_rows[part], 1, 0)
        grad_value = value_term if grad_value is None else grad_value + value_term
        grad_key = key_term if grad_key is None else grad_key + key_term
        grad_ref[0, 0, :, part] = (dot(key_all, grad_scores, 1, 0) * SCALE).astype(BF16)
    grad_ref[1, 0] = (grad_key * SCALE).astype(BF16).T
    grad_ref[2, 0] = grad_value.astype(BF16).T


def head_spec(tokens, offset):
    return pl.BlockSpec((1, HEAD_DIM, tokens), lambda head: (head + offset, 0, 0))


def whole_spec(shape):
    return pl.BlockSpec(shape, lambda head: (0,) * len(shape))


def row_spec(tokens):
    return pl.BlockSpec((1, 1, tokens), lambda head: (head, 0, 0))


SMALL = pl.CostEstimate(flops=1 << 20, bytes_accessed=1 << 20, transcendentals=0)


def attend(own, other, bias, hot, first, count):
    heads = own.shape[0] // 3
    part = own.shape[2]
    tokens = part + other.shape[2]
    in_specs = [
        head_spec(part, component * heads + first) for component in range(3) for _ in range(2)
    ]
    return pl.pallas_call(
        functools.partial(attend_kernel, min(tokens, (1 << 20) // tokens)),
        grid=(count,),
        in_specs=in_specs + [whole_spec(bias.shape), whole_spec(hot.shape)],
        out_specs=[head_spec(tokens, 0), row_spec(tokens)],
        out_shape=[
            jax.ShapeDtypeStruct((count, HEAD_DIM, tokens), BF16),
            jax.ShapeDtypeStruct((count, 1, tokens), F32),
        ],
        compiler_params=pltpu.CompilerParams(vmem_limit_bytes=24 << 20),
        cost_estimate=SMALL,
    )(own, other, own, other, own, other, bias, hot)


def attend_back(own, other, bias, hot, out, grad_own, grad_other, lse, first, count):
    heads = own.shape[0] // 3
    part = own.shape[2]
    tokens = part + other.shape[2]
    in_specs = [
        head_spec(part, component * heads + first) for component in range(3) for _ in range(2)
    ]
    return pl.pallas_call(
        functools.partial(attend_back_kernel, min(tokens, (1 << 19) // tokens)),
        grid=(count,),
        in_specs=in_specs
        + [
            whole_spec(bias.shape),
            whole_spec(hot.shape),
            head_spec(tokens, 0),
            head_spec(part, first),
            head_spec(part, first),
            row_spec(tokens),
        ],
        out_specs=pl.BlockSpec((3, 1, HEAD_DIM, tokens), lambda head: (0, head, 0, 0)),
        out_shape=jax.ShapeDtypeStruct((3, count, HEAD_DIM, tokens), BF16),
        compiler_params=pltpu.CompilerParams(vmem_limit_bytes=24 << 20),
        cost_estimate=SMALL,
    )(own, other, own, other, own, other, bias, hot, out, grad_own, grad_other, lse)


def write_kernel(place, first, last, aliased, *refs):
    me = lax.axis_index("dp")
    sources = refs[: len(refs) - 3 - aliased]
    out_ref, wide, sems = refs[-3:]
    copies = []
    for group, source in enumerate(sources):
        for block in range(first, last):
            slot = group * (last - first) + block - first
            wide[slot] = source[block].astype(F32)
            copies.append(
                pltpu.make_async_copy(
                    wide.at[slot], place(out_ref, me, group, block), sems.at[slot]
                )
            )
            copies[-1].start()
    for copy in copies:
        copy.wait()


def write_out(groups, place, shape, onto=None, part=None):
    blocks, rows, columns = groups[0].shape
    first, last = (0, blocks) if part is None else part
    count = len(groups) * (last - first)
    anywhere = pl.BlockSpec(memory_space=pl.ANY)
    extra = [] if onto is None else [onto]
    return pl.pallas_call(
        functools.partial(write_kernel, place, first, last, len(extra)),
        in_specs=[pl.BlockSpec(memory_space=pltpu.VMEM)] * len(groups) + [anywhere] * len(extra),
        out_specs=anywhere,
        scratch_shapes=[
            pltpu.VMEM((count, rows, columns), F32),
            pltpu.SemaphoreType.DMA((count,)),
        ],
        out_shape=jax.ShapeDtypeStruct(shape, F32),
        input_output_aliases={} if onto is None else {len(groups): 0},
        compiler_params=pltpu.CompilerParams(vmem_limit_bytes=20 << 20),
        cost_estimate=SMALL,
    )(*groups, *extra)


def hidden_kernel(inputs_ref, weight_ref, active_ref, slope_ref):
    rows = inputs_ref.shape[0] // 4
    for start in range(0, 4 * rows, rows):
        part = slice(start, start + rows)
        active, slope = gelu_parts(dot(inputs_ref[part], weight_ref[...], 1, 0))
        active_ref[part] = active.astype(BF16)
        slope_ref[part] = slope.astype(BF16)


def hidden_units(inputs, weight):
    rows, width = inputs.shape
    units = weight.shape[1]
    block = units // 6
    out_block = pl.BlockSpec((rows, block), lambda i: (0, i))
    return pl.pallas_call(
        hidden_kernel,
        grid=(6,),
        in_specs=[
            pl.BlockSpec((rows, width), lambda i: (0, 0)),
            pl.BlockSpec((width, block), lambda i: (0, i)),
        ],
        out_specs=[out_block] * 2,
        out_shape=[jax.ShapeDtypeStruct((rows, units), BF16)] * 2,
        compiler_params=pltpu.CompilerParams(vmem_limit_bytes=20 << 20),
        cost_estimate=SMALL,
    )(inputs, weight)


def hidden_back_kernel(grad_ref, weight_ref, slope_ref, out_ref):
    rows = grad_ref.shape[0] // 4
    for start in range(0, 4 * rows, rows):
        part = slice(start, start + rows)
        grads = dot(grad_ref[part], weight_ref[...], 1, 1)
        out_ref[part] = (grads * slope_ref[part].astype(F32)).astype(BF16)


def hidden_back(grads, weight, slope):
    rows, width = grads.shape
    units = weight.shape[0]
    block = units // 6
    out_block = pl.BlockSpec((rows, block), lambda i: (0, i))
    return pl.pallas_call(
        hidden_back_kernel,
        grid=(6,),
        in_specs=[
            pl.BlockSpec((rows, width), lambda i: (0, 0)),
            pl.BlockSpec((block, width), lambda i: (i, 0)),
            out_block,
        ],
        out_specs=out_block,
        out_shape=jax.ShapeDtypeStruct((rows, units), BF16),
        compiler_params=pltpu.CompilerParams(vmem_limit_bytes=20 << 20),
        cost_estimate=SMALL,
    )(grads, weight, slope)


def gradient_kernel(left_is_blocked, half_ref, left_ref, right_ref, *refs):
    total = dot(left_ref[...], right_ref[...], 0, 0)
    if len(refs) == 2:
        total = total + refs[0][...].astype(F32)
    refs[-1][...] = total.astype(BF16)


def half_gradient(left, right, half, away, left_is_blocked):
    rows = left.shape[0]
    blocked = left if left_is_blocked else right
    whole = right if left_is_blocked else left
    units = blocked.shape[1] // 2
    block = units // 3
    half_spec = pl.BlockSpec((rows, block), lambda i, half_ref: (0, half_ref[0] * 3 + i))
    whole_block = pl.BlockSpec(whole.shape, lambda i, half_ref: (0, 0))
    if left_is_blocked:
        shape = (units, whole.shape[1])
        out_spec = pl.BlockSpec((block, shape[1]), lambda i, half_ref: (i, 0))
        in_specs = [half_spec, whole_block]
    else:
        shape = (whole.shape[1], units)
        out_spec = pl.BlockSpec((shape[0], block), lambda i, half_ref: (0, i))
        in_specs = [whole_block, half_spec]
    extra = [] if away is None else [away]
    return pl.pallas_call(
        functools.partial(gradient_kernel, left_is_blocked),
        grid_spec=pltpu.PrefetchScalarGridSpec(
            num_scalar_prefetch=1,
            grid=(3,),
            in_specs=in_specs + [out_spec] * len(extra),
            out_specs=out_spec,
        ),
        out_shape=jax.ShapeDtypeStruct(shape, BF16),
        compiler_params=pltpu.CompilerParams(vmem_limit_bytes=22 << 20),
        cost_estimate=SMALL,
    )(half.astype(jnp.int32)[None], left, right, *extra)


def down_gradient(active, grads, half, away=None):
    return half_gradient(active, grads, half, away, True)


def up_gradient(inputs, grads, half, away=None):
    return half_gradient(inputs, grads, half, away, False)


def rows_back_kernel(grad_ref, weight_ref, wide_ref, low_ref):
    total = dot(grad_ref[...], weight_ref[...], 1, 1)
    wide_ref[...] = total
    low_ref[...] = total.astype(BF16)


def rows_back(grads, weight, which):
    rows = grads.shape[0] // 2
    units = grads.shape[1]
    width = weight.shape[0]
    block = width // 3
    out_block = pl.BlockSpec((rows, block), lambda i: (0, i))
    return pl.pallas_call(
        rows_back_kernel,
        grid=(3,),
        in_specs=[
            pl.BlockSpec((rows, units), lambda i: (which, 0)),
            pl.BlockSpec((block, units), lambda i: (i, 0)),
        ],
        out_specs=[out_block] * 2,
        out_shape=[
            jax.ShapeDtypeStruct((rows, width), F32),
            jax.ShapeDtypeStruct((rows, width), BF16),
        ],
        compiler_params=pltpu.CompilerParams(vmem_limit_bytes=20 << 20),
        cost_estimate=SMALL,
    )(grads, weight)


def finish_kernel(
    half_steps,
    halfway_ref,
    own_ref,
    away_ref,
    branch_ref,
    two_ref,
    two_first_ref,
    two_last_ref,
    tokens_ref,
    mods_ref,
    result_ref,
    grad_ref,
):
    values = tokens_ref[...].astype(F32)
    two_away = jnp.where(
        pl.program_id(0) < half_steps, two_first_ref[...].astype(F32), two_last_ref[...].astype(F32)
    )
    two = two_ref[...] + two_away
    halfway = values + mods_ref[0, 2:3] * branch_ref[...]
    result_ref[...] = (halfway + mods_ref[0, 5:6] * two).astype(BF16)
    normed, inverse = normalize(values)
    grad_mod = own_ref[...] + away_ref[...].astype(F32)
    back = norm_back(grad_mod * (1.0 + mods_ref[0, 1:2]), normed, inverse)
    grad_ref[...] = (halfway_ref[...] + back).astype(BF16)


def finish(grad_halfway, own, away, branch, two, two_first, two_last, tokens, mods):
    rows, width = tokens.shape
    chunk = own.shape[0] // mods.shape[0]
    steps = rows // chunk
    half_steps = steps // 2
    row_block = pl.BlockSpec((chunk, width), lambda i: (i, 0))
    return pl.pallas_call(
        functools.partial(finish_kernel, half_steps),
        grid=(steps,),
        in_specs=[
            row_block,
            row_block,
            row_block,
            row_block,
            row_block,
            pl.BlockSpec((chunk, width), lambda i: (jnp.minimum(i, half_steps - 1), 0)),
            pl.BlockSpec((chunk, width), lambda i: (jnp.maximum(i - half_steps, 0), 0)),
            row_block,
            pl.BlockSpec((1, 6, width), lambda i: (i, 0, 0)),
        ],
        out_specs=[row_block, row_block],
        out_shape=[jax.ShapeDtypeStruct((rows, width), BF16)] * 2,
        compiler_params=pltpu.CompilerParams(vmem_limit_bytes=16 << 20),
        cost_estimate=SMALL,
    )(grad_halfway, own, away, branch, two, two_first, two_last, tokens, mods)


def heads_back_kernel(first_ref, second_ref, first_weight, second_weight, wide_ref, low_ref):
    total = dot(first_ref[...], first_weight[...], 0, 0)
    total = total + dot(second_ref[...], second_weight[...], 0, 0)
    wide_ref[...] = total
    low_ref[...] = total.astype(BF16)


def heads_back(first, second, first_weight, second_weight):
    rows = first.shape[1]
    width = first_weight.shape[1]
    block = width // 3
    out_block = pl.BlockSpec((rows, block), lambda i: (0, i))
    return pl.pallas_call(
        heads_back_kernel,
        grid=(3,),
        in_specs=[
            pl.BlockSpec(first.shape, lambda i: (0, 0)),
            pl.BlockSpec(second.shape, lambda i: (0, 0)),
            pl.BlockSpec((first_weight.shape[0], block), lambda i: (0, i)),
            pl.BlockSpec((second.shape[0], block), lambda i: (0, i)),
        ],
        out_specs=[out_block] * 2,
        out_shape=[
            jax.ShapeDtypeStruct((rows, width), F32),
            jax.ShapeDtypeStruct((rows, width), BF16),
        ],
        compiler_params=pltpu.CompilerParams(vmem_limit_bytes=22 << 20),
        cost_estimate=SMALL,
    )(first, second, first_weight, second_weight)


def condition_kernel(grad_ref, weight_ref, out_ref):
    out_ref[...] = dot(grad_ref[...], weight_ref[...], 1, 1).astype(BF16)


def condition_part(grads, weight):
    rows, depth = weight.shape
    block = rows // 3
    return pl.pallas_call(
        condition_kernel,
        grid=(3,),
        in_specs=[
            pl.BlockSpec((grads.shape[0], depth), lambda i: (0, 0)),
            pl.BlockSpec((block, depth), lambda i: (i, 0)),
        ],
        out_specs=pl.BlockSpec((grads.shape[0], block), lambda i: (0, i)),
        out_shape=jax.ShapeDtypeStruct((grads.shape[0], rows), BF16),
        compiler_params=pltpu.CompilerParams(vmem_limit_bytes=14 << 20),
        cost_estimate=SMALL,
    )(grads, weight)


def ada_kernel(act_ref, grad_ref, out_ref):
    out_ref[...] = dot(act_ref[...], grad_ref[...], 0, 0)


def ada_gradient(act, grads, columns):
    block = columns // 9
    return pl.pallas_call(
        ada_kernel,
        grid=(9,),
        in_specs=[
            pl.BlockSpec(act.shape, lambda i: (0, 0)),
            pl.BlockSpec((act.shape[0], block), lambda i: (0, i)),
        ],
        out_specs=pl.BlockSpec((act.shape[1], block), lambda i: (0, i)),
        out_shape=jax.ShapeDtypeStruct((act.shape[1], columns), F32),
        compiler_params=pltpu.CompilerParams(vmem_limit_bytes=14 << 20),
        cost_estimate=SMALL,
    )(act, grads)


def middle_kernel(own_steps, first_ref, heads_ref, weight_ref, own_ref, away_ref, mods_ref, *outs):
    branch_ref, inputs_ref, normed_ref = outs
    branch = first_ref[...] + dot(heads_ref[...], weight_ref[...], 0, 0)
    is_own = pl.program_id(0) < own_steps
    values = jnp.where(is_own, own_ref[...].astype(F32), away_ref[...].astype(F32))
    normed, _ = normalize(values + mods_ref[0, 2:3] * branch)
    branch_ref[...] = branch
    inputs_ref[...] = (normed * (1.0 + mods_ref[0, 4:5]) + mods_ref[0, 3:4]).astype(BF16)
    normed_ref[...] = normed.astype(BF16)


def middle(first, heads_away, weight, own, away, mods):
    rows, width = first.shape
    steps = mods.shape[0]
    chunk = rows // steps
    own_steps = own.shape[0] // chunk
    depth = heads_away.shape[0]
    row_block = pl.BlockSpec((chunk, width), lambda i: (i, 0))
    return pl.pallas_call(
        functools.partial(middle_kernel, own_steps),
        grid=(steps,),
        in_specs=[
            row_block,
            pl.BlockSpec((depth, chunk), lambda i: (0, (i + steps // 2) % steps)),
            pl.BlockSpec((depth, width), lambda i: (1, 0)),
            pl.BlockSpec((chunk, width), lambda i: (jnp.minimum(i, own_steps - 1), 0)),
            pl.BlockSpec((chunk, width), lambda i: (jnp.maximum(i - own_steps, 0), 0)),
            pl.BlockSpec((1, 6, width), lambda i: (i, 0, 0)),
        ],
        out_specs=[row_block] * 3,
        out_shape=[
            jax.ShapeDtypeStruct((rows, width), F32),
            jax.ShapeDtypeStruct((rows, width), BF16),
            jax.ShapeDtypeStruct((rows, width), BF16),
        ],
        compiler_params=pltpu.CompilerParams(vmem_limit_bytes=14 << 20),
        cost_estimate=SMALL,
    )(first, heads_away, weight, own, away, mods)


def middle_back_kernel(
    half_steps, own_ref, first_ref, second_ref, branch_ref, tokens_ref, cot_ref, mods_ref, *outs
):
    grad_ref, low_ref, sums_ref = outs
    arrived = jnp.where(
        pl.program_id(0) < half_steps, first_ref[...].astype(F32), second_ref[...].astype(F32)
    )
    branch = branch_ref[...]
    gate = mods_ref[0, 2:3]
    normed, inverse = normalize(tokens_ref[...].astype(F32) + gate * branch)
    grad_mod = own_ref[...] + arrived
    grad = cot_ref[...].astype(F32) + norm_back(
        grad_mod * (1.0 + mods_ref[0, 4:5]), normed, inverse
    )
    grad_ref[...] = grad
    low_ref[...] = (grad * gate).astype(BF16)
    sums_ref[0] = jnp.sum(grad * branch, axis=0, keepdims=True)


def middle_back(own, first, second, branch, tokens, cot, mods):
    rows, width = own.shape
    chunk = branch.shape[0] // mods.shape[0]
    steps = rows // chunk
    half_steps = steps // 2
    row_block = pl.BlockSpec((chunk, width), lambda i: (i, 0))
    return pl.pallas_call(
        functools.partial(middle_back_kernel, half_steps),
        grid=(steps,),
        in_specs=[
            row_block,
            pl.BlockSpec((chunk, width), lambda i: (jnp.minimum(i, half_steps - 1), 0)),
            pl.BlockSpec((chunk, width), lambda i: (jnp.maximum(i - half_steps, 0), 0)),
            row_block,
            row_block,
            row_block,
            pl.BlockSpec((1, 6, width), lambda i: (i, 0, 0)),
        ],
        out_specs=[row_block, row_block, pl.BlockSpec((1, 1, width), lambda i: (i, 0, 0))],
        out_shape=[
            jax.ShapeDtypeStruct((rows, width), F32),
            jax.ShapeDtypeStruct((rows, width), BF16),
            jax.ShapeDtypeStruct((steps, 1, width), F32),
        ],
        compiler_params=pltpu.CompilerParams(vmem_limit_bytes=14 << 20),
        cost_estimate=SMALL,
    )(own, first, second, branch, tokens, cot, mods)


def pair_body(
    tokens,
    segments,
    labels,
    timesteps,
    class_table,
    time_weight,
    ada_weight,
    qkv_weight,
    proj_weight,
    up_weight,
    down_weight,
    cotangent,
):
    position = lax.axis_index("tensor")
    rank = lax.axis_index("dp")
    dp_size = 16
    core, line, deep = rank % 2, rank // 2 % 2, rank // 4 % 2
    own_low = tokens[0]
    cot_low = cotangent[0]
    shard, width = own_low.shape
    pack = segments.shape[1]
    slot_count = labels.shape[1]
    class_count = class_table.shape[0]
    freq_width = time_weight.shape[0]
    local_width = qkv_weight.shape[2]
    heads = local_width // HEAD_DIM
    half_heads = heads // 2
    half_width = local_width // 2
    hidden_width = up_weight.shape[1]
    chunk = shard * SHORT // pack
    own_chunks = shard // chunk
    CORE, LINE, DEEP, FAR = 1, 2, 4, 8

    def fence(*values):
        return lax.optimization_barrier(values)

    def swap(x):
        return lax.ppermute(x, "tensor", [(0, 1), (1, 0)])

    def trade(x, bits):
        return lax.ppermute(x, "dp", [(i, i ^ bits) for i in range(dp_size)])

    def rows_of(x, index, count):
        size = x.shape[0] // count
        return lax.dynamic_slice_in_dim(x, index * size, size, 0)

    def columns_of(x, index, count):
        size = x.shape[1] // count
        return lax.dynamic_slice_in_dim(x, index * size, size, 1)

    def plus(a, b):
        return (a.astype(F32) + b.astype(F32)).astype(BF16)

    def halve(x, digit, bits):
        return plus(rows_of(x, digit, 2), trade(rows_of(x, 1 - digit, 2), bits))

    def digit(me, bits):
        return me // bits % 2

    def down_place(ref, me, group, block):
        index = (
            (digit(me, CORE) + group) % 2 * 4
            + (digit(me, LINE) + block // 2) % 2 * 2
            + (digit(me, DEEP) + block) % 2
        )
        return ref.at[index]

    def proj_place(ref, me, group, block):
        index = (digit(me, CORE) + group // 2) % 2 * 4 + (digit(me, LINE) + group % 2) % 2 * 2
        return ref.at[index + block - 3]

    def up_place(ref, me, group, block):
        index = (digit(me, LINE) + block // 2) % 2 * 2 + (digit(me, DEEP) + block) % 2
        column = (digit(me, CORE) + group) % 2 * (hidden_width // 2)
        return ref.at[index, :, pl.ds(pl.multiple_of(column, 128), hidden_width // 2)]

    def qkv_place(offset, bits):
        def place(ref, me, group, block):
            unit = (
                (digit(me, CORE) + group // 2) % 2 * 2 + (digit(me, bits) + group % 2) % 2
            ) * 3 + block
            return ref.at[unit // half_heads * heads + unit % half_heads + offset]

        return place

    def chunked(x):
        return x.reshape(x.shape[0] // chunk, chunk, x.shape[1])

    def flat(x):
        return x.reshape(x.shape[0] * chunk, x.shape[2])

    quarter = shard // 2
    tokens_away = swap(own_low)
    ids = jnp.stack([labels[0], timesteps[0]], axis=1)

    seg = segments[0]
    seg = jnp.where(position == 0, seg, jnp.roll(seg, shard))
    slots = jnp.arange(slot_count, dtype=jnp.int32)
    chunk_hot = (seg[::chunk][:, None] == slots[None, :]).astype(F32)
    mask_rows = -(-slot_count // 8) * 8
    same = jnp.arange(mask_rows, dtype=jnp.int32)[:, None] == seg[None, :]
    hot = same.astype(BF16)
    bias = jnp.where(same, 0.0, -1e30).astype(BF16)

    classes = jnp.arange(class_count, dtype=jnp.int32)

    def condition_of(ids):
        label_hot = (ids[:, 0][:, None] == classes[None, :]).astype(F32)
        feats = features(ids[:, 1].astype(F32), freq_width)
        values = dot(label_hot, class_table, 1, 0, HIGH) + dot(feats, time_weight, 1, 0, HIGH)
        return label_hot, feats, values

    def hop(y, bits):
        return jnp.concatenate([y, trade(y, bits)], axis=0)

    condition = condition_of(ids)[2]
    pad = jnp.zeros((slot_count, 124), jnp.int32)
    digits = jnp.concatenate([ids // 32, ids % 32, pad], axis=1).astype(BF16)
    act_low = jax.nn.silu(condition).astype(BF16)
    weight_t = qkv_weight.transpose(1, 2, 0).reshape(3 * local_width, width)
    weight_parts = weight_t.reshape(3, 2, half_width, width)
    weight_a = weight_parts[:, 0].reshape(3 * half_width, width)
    weight_b = weight_parts[:, 1].reshape(3 * half_width, width)
    mod_part, tokens_away, proj_half, weight_a, weight_b = fence(
        dot(act_low, ada_weight, 1, 0),
        tokens_away,
        rows_of(proj_weight, core, 2),
        weight_a,
        weight_b,
    )
    mod_away, tokens_away = fence(swap(mod_part), tokens_away)
    modulation = jnp.where(
        position == 0,
        jnp.concatenate([mod_part, mod_away], axis=1),
        jnp.concatenate([mod_away, mod_part], axis=1),
    )
    proj_half = swap(proj_half)
    per_chunk = dot(chunk_hot, modulation, 1, 0, HIGH)
    mods_own = [m[:, None, :] for m in jnp.split(per_chunk[:own_chunks], 6, axis=1)]
    mods_other = [m[:, None, :] for m in jnp.split(per_chunk[own_chunks:], 6, axis=1)]


    def enter(low, mods):
        values = chunked(low.astype(F32))
        normed, inverse = normalize(values)
        inputs = flat((normed * (1.0 + mods[1]) + mods[0]).astype(BF16))
        return values, normed, inverse, inputs

    def project(inputs):
        return dot(weight_t, inputs, 1, 1).astype(BF16).reshape(3 * heads, HEAD_DIM, shard)

    tokens_own, normed_one, inverse_one, inputs_one_own = enter(own_low, mods_own)
    qkv_own = project(inputs_one_own)
    tokens_other, normed_one_other, _, inputs_one_other = enter(tokens_away, mods_other)
    qkv_other = project(inputs_one_other)
    out_a, lse_a = attend(qkv_own, qkv_other, bias, hot, 0, half_heads)
    chunk_mods = per_chunk.reshape(pack // chunk, 6, width)
    out_a, qkv_own, chunk_mods = fence(out_a, qkv_own, chunk_mods)
    away_a = swap(out_a.reshape(half_width, pack))
    out_b, lse_b = attend(qkv_own, qkv_other, bias, hot, half_heads, half_heads)
    out_b, proj_half, away_a = fence(out_b, proj_half, away_a)
    away_b = swap(out_b.reshape(half_width, pack))
    proj_rest = trade(proj_half, CORE)
    proj_other = jnp.where(
        core == 0,
        jnp.concatenate([proj_half, proj_rest], axis=0),
        jnp.concatenate([proj_rest, proj_half], axis=0),
    )
    out_flat = jnp.concatenate([out_a, out_b], axis=0).reshape(local_width, pack)
    own_part, other_part = slice(0, shard), slice(shard, pack)

    def reordered(away):
        return jnp.concatenate([away[:, other_part], away[:, own_part]], axis=1)

    away_a, proj_other = fence(away_a, proj_other)
    first, _ = heads_back(out_flat, reordered(away_a), proj_weight, proj_other)
    away_b, cot_next, first = fence(away_b, cot_low, first)
    cot_away = swap(cot_next)
    branch_one, inputs_two, normed_two = middle(
        first, away_b, proj_other, own_low, tokens_away, chunk_mods
    )

    active, slope = hidden_units(inputs_two, up_weight)
    active, slope, cot_away = fence(active, slope, cot_away)
    grad_branch_two = jnp.concatenate(
        [
            flat((chunked(cot_low.astype(F32)) * mods_own[5]).astype(BF16)),
            flat((chunked(cot_away.astype(F32)) * mods_other[5]).astype(BF16)),
        ],
        axis=0,
    )

    down_away = trade(down_gradient(active, grad_branch_two, 1 - core), CORE)
    grad_hidden = hidden_back(grad_branch_two, down_weight, slope)
    down_sum = down_gradient(active, grad_branch_two, core, down_away)
    down_sum, grad_hidden = fence(down_sum, grad_hidden)
    down_x = trade(rows_of(down_sum, 1 - line, 2), LINE)
    mod_two_other, mod_two_away = rows_back(grad_hidden, up_weight, 1)
    mod_two_away, grad_hidden = fence(mod_two_away, grad_hidden)

    arrived_a = swap(mod_two_away[:quarter])
    up_away = trade(up_gradient(inputs_two, grad_hidden, 1 - core), CORE)
    mod_two, _ = rows_back(grad_hidden, up_weight, 0)
    arrived_a, up_away, mod_two, mod_two_next, grad_hidden, active = fence(
        arrived_a, up_away, mod_two, mod_two_away[quarter:], grad_hidden, active
    )
    arrived_b = swap(mod_two_next)
    up_sum = up_gradient(inputs_two, grad_hidden, core, up_away)
    up_x = trade(rows_of(up_sum, 1 - line, 2), LINE)
    branch_two_away = dot(active[other_part], down_weight, 1, 0)
    branch_two = dot(active[own_part], down_weight, 1, 0)
    arrived_b, mod_two, branch_two_away, branch_two, down_x = fence(
        arrived_b, mod_two, branch_two_away, branch_two, down_x
    )

    down_sum = plus(rows_of(down_sum, line, 2), down_x)
    down_z = trade(rows_of(down_sum, 1 - deep, 2), DEEP)
    grad_halfway, grad_branch_one, gate_one_sums = middle_back(
        mod_two, arrived_a, arrived_b, branch_one, own_low, cot_low, chunk_mods
    )
    grad_att_away = dot(proj_other, grad_branch_one, 1, 1).astype(BF16)
    grad_att_away, grad_branch_one = fence(grad_att_away, grad_branch_one)

    grad_att_other = swap(grad_att_away)
    grad_att_own = dot(proj_weight, grad_branch_one, 1, 1).astype(BF16)
    def chunk_sums(own, other):
        return jnp.concatenate([jnp.sum(own, axis=1), jnp.sum(other, axis=1)], axis=0)

    normed_two = chunked(normed_two.astype(F32))
    late_terms = jnp.concatenate(
        [
            jnp.concatenate([gate_one_sums[:, 0], jnp.zeros_like(gate_one_sums[:, 0])], axis=0),
            chunk_sums(chunked(mod_two), chunked(mod_two_other)),
            chunk_sums(
                chunked(mod_two) * normed_two[:own_chunks],
                chunked(mod_two_other) * normed_two[own_chunks:],
            ),
            chunk_sums(
                chunked(branch_two) * chunked(cot_low.astype(F32)),
                chunked(branch_two_away) * chunked(cot_away.astype(F32)),
            ),
        ],
        axis=1,
    )
    inputs_one = jnp.concatenate([inputs_one_own, inputs_one_other], axis=0)
    grad_att_other, grad_att_own, down_z, branch_one_next, inputs_one, late_terms = fence(
        grad_att_other, grad_att_own, down_z, grad_branch_one, inputs_one, late_terms
    )
    down_sum = plus(rows_of(down_sum, deep, 2), down_z)
    down_block = down_sum.shape[0] // 2
    down_far_a = trade(down_sum[:down_block], FAR)

    def back(out, lse, first):
        return attend_back(
            qkv_own,
            qkv_other,
            bias,
            hot,
            out,
            grad_att_own.reshape(heads, HEAD_DIM, shard),
            grad_att_other.reshape(heads, HEAD_DIM, shard),
            lse,
            first,
            half_heads,
        ).reshape(3 * half_width, pack)

    def qkv_half(grad):
        return lambda half: dot(rows_of(grad, half, 2), inputs_one, 1, 0)

    grads_one_other = swap(branch_one_next)
    grad_qkv_a = back(out_a, lse_a, 0)
    grad_qkv_a, up_x, down_far_a, down_next = fence(
        grad_qkv_a, up_x, down_far_a, down_sum[down_block:]
    )
    down_far_b = trade(down_next, FAR)
    up_sum = plus(rows_of(up_sum, line, 2), up_x)
    up_z = trade(rows_of(up_sum, 1 - deep, 2), DEEP)
    qkv_make = qkv_half(grad_qkv_a)
    qkv_a_away = trade(qkv_make(1 - core).astype(BF16), CORE)
    qkv_a = plus(qkv_make(core), qkv_a_away)
    qkv_a, grad_att_own = fence(qkv_a, grad_att_own)
    qkv_a_x = trade(rows_of(qkv_a, 1 - line, 2), LINE)
    grad_qkv_b = back(out_b, lse_b, half_heads)
    grad_qkv_b, qkv_a_x, up_z, down_far_b, grads_one_other = fence(
        grad_qkv_b, qkv_a_x, up_z, down_far_b, grads_one_other
    )
    qkv_a = plus(rows_of(qkv_a, line, 2), qkv_a_x)
    up_sum = plus(rows_of(up_sum, deep, 2), up_z)
    down_sum = plus(down_sum, jnp.concatenate([down_far_a, down_far_b], axis=0))
    down_z = trade(down_sum, DEEP)
    down_x = trade(down_sum, LINE)
    block = up_sum.shape[0] // 2
    up_far_a = trade(up_sum[:block], FAR)
    mod_one = dot(grad_qkv_a, weight_a, 0, 0) + dot(grad_qkv_b, weight_b, 0, 0)
    mod_one_own, mod_one_away = chunked(mod_one[own_part]), chunked(mod_one[other_part])
    chunk_terms = jnp.concatenate(
        [
            chunk_sums(mod_one_own, mod_one_away),
            chunk_sums(mod_one_own * normed_one, mod_one_away * normed_one_other),
            late_terms,
        ],
        axis=1,
    )
    slot_terms = dot(chunk_hot, chunk_terms, 0, 0, HIGH).astype(BF16)
    half = slot_terms.shape[1] // 2
    low, high = slot_terms[:, :half], slot_terms[:, half:]
    keep = jnp.where(position == 0, low, high)
    away = jnp.where(position == 0, high, low)
    (
        away,
        keep,
        mod_one_next,
        down_z,
        down_x,
        up_far_a,
        grad_qkv_b,
        up_next,
        qkv_a,
    ) = fence(
        away,
        keep,
        flat(mod_one_away).astype(BF16),
        down_z,
        down_x,
        up_far_a,
        grad_qkv_b,
        up_sum[block:],
        qkv_a,
    )

    gathered = jnp.concatenate([plus(keep, swap(away)), digits], axis=1)[None]
    down_zx = trade(down_z, LINE)
    up_far_b = trade(up_next, FAR)
    qkv_a_z = trade(rows_of(qkv_a, 1 - deep, 2), DEEP)
    qkv_make_b = qkv_half(grad_qkv_b)

    def proj_half_of(half):
        rows = rows_of(out_flat, half, 2)
        return dot(rows[:, own_part], grad_branch_one, 1, 0) + dot(
            rows[:, other_part], grads_one_other, 1, 0
        )

    def packed(qkv, proj, index):
        return jnp.concatenate([rows_of(qkv, index, 2), rows_of(proj, index, 2)], axis=0)

    def unpacked(both):
        cut = both.shape[0] * 3 // 5
        return both[:cut], both[cut:]

    def in_order(digit, own, other):
        return jnp.where(
            digit == 0,
            jnp.concatenate([own, other], axis=0),
            jnp.concatenate([other, own], axis=0),
        )

    rest = trade(
        jnp.concatenate(
            [qkv_make_b(1 - core).astype(BF16), proj_half_of(1 - core).astype(BF16)], axis=0
        ),
        CORE,
    )
    qkv_rows = 3 * half_width // 2
    qkv_b = plus(qkv_make_b(core), rest[:qkv_rows])
    proj_sum = plus(proj_half_of(core), rest[qkv_rows:])
    both_next = packed(qkv_b, proj_sum, 1 - line)
    both = packed(qkv_b, proj_sum, line)
    gathered, up_far_b, down_zx, qkv_a_z, both_next, both, mod_one_next = fence(
        gathered, up_far_b, down_zx, qkv_a_z, both_next, both, mod_one_next
    )

    up_low = plus(up_sum[:block], up_far_a)
    up_high = plus(up_next, up_far_b)
    up_sum = jnp.concatenate([up_low, up_high], axis=0)
    qkv_a = plus(rows_of(qkv_a, deep, 2), qkv_a_z)
    up_sum, qkv_a, both_next, gathered, mod_one_next = fence(
        up_sum, qkv_a, both_next, gathered, mod_one_next
    )
    gathered = hop(gathered, LINE)
    mod_one_other = swap(mod_one_next)
    both_x = trade(both_next, LINE)
    up_z = trade(up_sum, DEEP)
    qkv_a_far = trade(qkv_a, FAR)
    (
        gathered,
        both_x,
        up_z,
        qkv_a_far,
        mod_one_other,
        both,
        down_sum,
        down_z,
        down_x,
        down_zx,
    ) = fence(
        gathered,
        both_x,
        up_z,
        qkv_a_far,
        mod_one_other,
        both,
        down_sum,
        down_z,
        down_x,
        down_zx,
    )
    both = plus(both, both_x)
    both_next = packed(*unpacked(both), 1 - deep)
    qkv_a = plus(qkv_a, qkv_a_far)
    both_next, qkv_a, gathered, up_sum, both, two_low = fence(
        both_next, qkv_a, gathered, up_sum, both, branch_two_away.astype(BF16)
    )
    two_first = swap(two_low[:quarter])
    gathered = hop(gathered, FAR)
    up_x = trade(up_sum, LINE)
    down_blocks = jnp.stack([down_sum, down_z, down_x, down_zx])
    both_z = trade(both_next, DEEP)
    qkv_a_z = trade(qkv_a, DEEP)
    both = packed(*unpacked(both), deep)
    gathered, up_x, both_z, qkv_a_z, both, down_blocks, two_first, two_next = fence(
        gathered, up_x, both_z, qkv_a_z, both, down_blocks, two_first, two_low[quarter:]
    )
    both = plus(both, both_z)
    qkv_a = in_order(deep, qkv_a, qkv_a_z).reshape(3, HEAD_DIM, width)
    both, qkv_a, gathered, up_z, down_blocks, two_next = fence(
        both, qkv_a, gathered, up_z, down_blocks, two_next
    )
    two_last = swap(two_next)
    grad_down = write_out(
        [down_blocks, trade(down_blocks, CORE)], down_place, (8, hidden_width // 8, width)
    )
    gathered = hop(gathered, DEEP)
    up_zx = trade(up_z, LINE)
    both_far = trade(both, FAR)
    up_zx, both_far, gathered, grad_down, two_last = fence(
        up_zx, both_far, gathered, grad_down, two_last
    )
    both = plus(both, both_far)
    up_blocks = jnp.stack([up_sum, up_z, up_x, up_zx])
    both, gathered, up_blocks, qkv_a = fence(both, gathered, up_blocks, qkv_a)
    both_z = trade(both, DEEP)
    qkv_a_x = trade(qkv_a, LINE)
    up_blocks_c = trade(up_blocks, CORE)
    grad_mod_all = hop(gathered, CORE).reshape(dp_size * slot_count, half + 128)
    cond_part = condition_part(grad_mod_all, ada_weight)
    ids_all = grad_mod_all[:, half : half + 4].astype(jnp.int32)
    label_hot, features_all, condition_all = condition_of(ids_all[:, :2] * 32 + ids_all[:, 2:])
    act_all = jax.nn.silu(condition_all).astype(BF16)
    both_z, cond_part, act_all, up_blocks_c, qkv_a_x = fence(
        both_z, cond_part, act_all, up_blocks_c, qkv_a_x
    )
    both = jnp.concatenate(
        [in_order(deep, a, b) for a, b in zip(unpacked(both), unpacked(both_z), strict=True)],
        axis=0,
    ).reshape(5, HEAD_DIM, width)
    both_x = trade(both, LINE)
    both_c = trade(both, CORE)
    grad_act = cond_part.astype(F32) + swap(cond_part).astype(F32)
    result, grad_input = finish(
        grad_halfway,
        mod_one,
        mod_one_other,
        branch_one,
        branch_two,
        two_first,
        two_last,
        own_low,
        chunk_mods,
    )
    qkv_a_c = trade(qkv_a, CORE)
    qkv_a_xc = trade(qkv_a_x, CORE)
    grad_up = write_out([up_blocks, up_blocks_c], up_place, (4, width // 4, hidden_width))
    grad_ada = ada_gradient(act_all, grad_mod_all, ada_weight.shape[1])
    both_x, both_c, grad_up, grad_act, grad_ada, qkv_a_c, qkv_a_xc, result = fence(
        both_x, both_c, grad_up, grad_act, grad_ada, qkv_a_c, qkv_a_xc, result
    )
    both_xc = trade(both_x, CORE)
    qkv_shape = (3 * heads, HEAD_DIM, width)
    grad_qkv = write_out([qkv_a, qkv_a_x, qkv_a_c, qkv_a_xc], qkv_place(0, LINE), qkv_shape)

    grad_condition = jax.vjp(jax.nn.silu, condition_all)[1](grad_act)[0]
    grad_class = dot(label_hot.astype(BF16), grad_condition.astype(BF16), 0, 0)
    grad_time = dot(features_all, grad_condition, 0, 0, HIGH)
    groups = [both, both_x, both_c, both_xc]
    grad_qkv = write_out(groups, qkv_place(half_heads, LINE), qkv_shape, grad_qkv, (0, 3))
    grad_proj = write_out(groups, proj_place, (8, HEAD_DIM, width), None, (3, 5))
    return (
        result[None],
        grad_input[None],
        grad_class,
        grad_time,
        grad_ada,
        grad_qkv.reshape(3, local_width, width).transpose(2, 0, 1),
        grad_proj.reshape(local_width, width),
        grad_up.reshape(width, hidden_width),
        grad_down.reshape(hidden_width, width),
    )


def any_body(
    tokens,
    segments,
    labels,
    timesteps,
    class_table,
    time_weight,
    ada_weight,
    qkv_weight,
    proj_weight,
    up_weight,
    down_weight,
    cotangent,
):
    own_tokens = tokens[0].astype(jnp.float32)
    shard_rows = own_tokens.shape[0]
    model_width = own_tokens.shape[1]
    seg_all = segments[0]
    pack_rows = seg_all.shape[0]
    slot_count = labels.shape[1]
    class_count = class_table.shape[0]
    freq_width = time_weight.shape[0]
    local_width = qkv_weight.shape[2]
    head_count = local_width // HEAD_DIM
    scale_factor = 1.0 / math.sqrt(HEAD_DIM)
    position = lax.axis_index("tensor")
    seg_own = lax.dynamic_slice_in_dim(seg_all, position * shard_rows, shard_rows)
    own_hot = (seg_own[:, None] == jnp.arange(slot_count, dtype=jnp.int32)[None, :]).astype(
        jnp.float32
    )
    label_hot = (labels[0][:, None] == jnp.arange(class_count, dtype=jnp.int32)[None, :]).astype(
        jnp.float32
    )
    step_feats = features(timesteps[0].astype(jnp.float32), freq_width)
    condition = jnp.dot(label_hot, class_table, precision=HIGH) + jnp.dot(
        step_feats, time_weight, precision=HIGH
    )
    act_low = jax.nn.silu(condition).astype(jnp.bfloat16)
    mod_part = jnp.dot(act_low, ada_weight, preferred_element_type=jnp.float32)
    modulation = lax.all_gather(mod_part, "tensor", axis=1, tiled=True)
    per_token = jnp.dot(own_hot, modulation, precision=HIGH)
    shift_one, scale_one, gate_one, shift_two, scale_two, gate_two = jnp.split(per_token, 6, axis=1)
    normed_one, inverse_one = normalize(own_tokens)
    modulated_one = (normed_one * (1.0 + scale_one) + shift_one).astype(jnp.bfloat16)
    inputs_one = lax.all_gather(modulated_one, "tensor", axis=0, tiled=True)
    qkv_flat = qkv_weight.reshape(model_width, 3 * local_width)
    qkv = jnp.dot(inputs_one, qkv_flat, preferred_element_type=jnp.float32).astype(jnp.bfloat16)
    qkv_heads = qkv.reshape(pack_rows, 3, head_count, HEAD_DIM).transpose(1, 2, 0, 3)
    queries = qkv_heads[0]
    keys = qkv_heads[1]
    values = qkv_heads[2]
    block = min(512, pack_rows)
    block_count = pack_rows // block
    starts = jnp.arange(block_count, dtype=jnp.int32) * block

    def scores_of(start):
        query_block = lax.dynamic_slice_in_dim(queries, start, block, 1)
        seg_block = lax.dynamic_slice_in_dim(seg_all, start, block)
        raw = (
            jnp.einsum("hqd,hkd->hqk", query_block, keys, preferred_element_type=jnp.float32)
            * scale_factor
        )
        same = (seg_block[:, None] == seg_all[None, :])[None]
        return (jnp.where(same, raw, -1e30), query_block)

    def attend(start):
        scores = scores_of(start)[0]
        top = jnp.max(scores, axis=-1, keepdims=True)
        exps = jnp.exp(scores - top)
        total = jnp.sum(exps, axis=-1, keepdims=True)
        weights = (exps / total).astype(jnp.bfloat16)
        out_block = jnp.einsum("hqk,hkd->hqd", weights, values, preferred_element_type=jnp.float32)
        return (out_block, (top + jnp.log(total))[..., 0])

    out_blocks, lse_blocks = lax.map(attend, starts)
    attended = out_blocks.transpose(0, 2, 1, 3).reshape(pack_rows, local_width).astype(jnp.bfloat16)
    lse_all = lse_blocks.transpose(1, 0, 2).reshape(head_count, pack_rows)
    branch_one = lax.psum_scatter(
        jnp.dot(attended, proj_weight, preferred_element_type=jnp.float32),
        "tensor",
        scatter_dimension=0,
        tiled=True,
    )
    halfway = own_tokens + gate_one * branch_one
    normed_two, inverse_two = normalize(halfway)
    modulated_two = (normed_two * (1.0 + scale_two) + shift_two).astype(jnp.bfloat16)
    inputs_two = lax.all_gather(modulated_two, "tensor", axis=0, tiled=True)
    hidden = jnp.dot(inputs_two, up_weight, preferred_element_type=jnp.float32)
    active = jax.nn.gelu(hidden, approximate=True).astype(jnp.bfloat16)
    branch_two = lax.psum_scatter(
        jnp.dot(active, down_weight, preferred_element_type=jnp.float32).astype(jnp.bfloat16),
        "tensor",
        scatter_dimension=0,
        tiled=True,
    ).astype(jnp.float32)
    result = halfway + gate_two * branch_two
    grad_out = cotangent[0].astype(jnp.float32)
    grad_gate_two = grad_out * branch_two
    grad_branch_two = (grad_out * gate_two).astype(jnp.bfloat16)
    grads_two = lax.all_gather(grad_branch_two, "tensor", axis=0, tiled=True)
    grad_down = contract_rows(active, grads_two)
    grad_active = times_transposed(grads_two, down_weight)
    gelu_back = jax.vjp(lambda inner: jax.nn.gelu(inner, approximate=True), hidden)[1]
    grad_hidden = gelu_back(grad_active)[0].astype(jnp.bfloat16)
    grad_up = contract_rows(inputs_two, grad_hidden)
    grad_mod_two = lax.psum_scatter(
        times_transposed(grad_hidden, up_weight), "tensor", scatter_dimension=0, tiled=True
    )
    grad_halfway = grad_out + norm_back(grad_mod_two * (1.0 + scale_two), normed_two, inverse_two)
    grad_gate_one = grad_halfway * branch_one
    grad_branch_one = (grad_halfway * gate_one).astype(jnp.bfloat16)
    grads_one = lax.all_gather(grad_branch_one, "tensor", axis=0, tiled=True)
    grad_proj = contract_rows(attended, grads_one)
    grad_attended = times_transposed(grads_one, proj_weight).astype(jnp.bfloat16)
    grad_heads = grad_attended.reshape(pack_rows, head_count, HEAD_DIM).transpose(1, 0, 2)

    def attend_back(carry, start):
        grad_keys, grad_values = carry
        scores, query_block = scores_of(start)
        lse_block = lax.dynamic_slice_in_dim(lse_all, start, block, 1)
        probs = jnp.exp(scores - lse_block[..., None])
        grad_block = lax.dynamic_slice_in_dim(grad_heads, start, block, 1)
        grad_probs = jnp.einsum(
            "hqd,hkd->hqk", grad_block, values, preferred_element_type=jnp.float32
        )
        grad_scores = (
            probs * (grad_probs - jnp.sum(probs * grad_probs, axis=-1, keepdims=True))
        ).astype(jnp.bfloat16)
        grad_query = (
            jnp.einsum("hqk,hkd->hqd", grad_scores, keys, preferred_element_type=jnp.float32)
            * scale_factor
        )
        grad_keys = (
            grad_keys
            + jnp.einsum(
                "hqk,hqd->hkd", grad_scores, query_block, preferred_element_type=jnp.float32
            )
            * scale_factor
        )
        grad_values = grad_values + jnp.einsum(
            "hqk,hqd->hkd",
            probs.astype(jnp.bfloat16),
            grad_block,
            preferred_element_type=jnp.float32,
        )
        return ((grad_keys, grad_values), grad_query)

    empty = jnp.zeros((head_count, pack_rows, HEAD_DIM), jnp.float32)
    key_grads, grad_queries = lax.scan(attend_back, (empty, empty), starts)
    query_grads = grad_queries.transpose(1, 0, 2, 3).reshape(head_count, pack_rows, HEAD_DIM)
    grad_stack = jnp.stack([query_grads, key_grads[0], key_grads[1]], axis=0)
    grad_qkv = (
        grad_stack.transpose(2, 0, 1, 3).reshape(pack_rows, 3 * local_width).astype(jnp.bfloat16)
    )
    grad_qkv_weight = contract_rows(inputs_one, grad_qkv).reshape(model_width, 3, local_width)
    grad_mod_one = lax.psum_scatter(
        times_transposed(grad_qkv, qkv_flat).astype(jnp.bfloat16),
        "tensor",
        scatter_dimension=0,
        tiled=True,
    ).astype(jnp.float32)
    grad_input = grad_halfway + norm_back(grad_mod_one * (1.0 + scale_one), normed_one, inverse_one)
    grad_per_token = jnp.concatenate(
        [
            grad_mod_one,
            grad_mod_one * normed_one,
            grad_gate_one,
            grad_mod_two,
            grad_mod_two * normed_two,
            grad_gate_two,
        ],
        axis=1,
    )
    slot_terms = contract_exact(own_hot, grad_per_token)
    grad_modulation = lax.psum_scatter(
        slot_terms.astype(jnp.bfloat16), "tensor", scatter_dimension=1, tiled=True
    )
    grad_ada = contract_rows(act_low, grad_modulation)
    cond_part = times_transposed(grad_modulation, ada_weight)
    grad_activated = lax.psum(cond_part.astype(jnp.bfloat16), "tensor").astype(jnp.float32)
    grad_condition = jax.vjp(jax.nn.silu, condition)[1](grad_activated)[0]
    grad_class = contract_exact(label_hot, grad_condition)
    grad_time = contract_exact(step_feats, grad_condition)
    summed = (
        lax.psum(grad_class.astype(jnp.bfloat16), "dp").astype(jnp.float32),
        lax.psum(grad_time.astype(jnp.bfloat16), "dp").astype(jnp.float32),
        lax.psum(grad_ada.astype(jnp.bfloat16), "dp").astype(jnp.float32),
        lax.psum(grad_qkv_weight.astype(jnp.bfloat16), "dp").astype(jnp.float32),
        lax.psum(grad_proj.astype(jnp.bfloat16), "dp").astype(jnp.float32),
        lax.psum(grad_up.astype(jnp.bfloat16), "dp").astype(jnp.float32),
        lax.psum(grad_down.astype(jnp.bfloat16), "dp").astype(jnp.float32),
    )
    grad_class, grad_time, grad_ada, grad_qkv_weight, grad_proj, grad_up, grad_down = summed
    return (
        result.astype(jnp.bfloat16)[None],
        grad_input.astype(jnp.bfloat16)[None],
        grad_class,
        grad_time,
        grad_ada,
        grad_qkv_weight,
        grad_proj,
        grad_up,
        grad_down,
    )


def solution(mesh):
    pairs = mesh.shape["dp"] == 16 and mesh.shape["tensor"] == 2
    return jax.shard_map(
        pair_body if pairs else any_body,
        mesh=mesh,
        in_specs=(
            P("dp", "tensor", None),
            P("dp", None),
            P("dp", None),
            P("dp", None),
            P(),
            P(),
            P(None, "tensor"),
            P(None, None, "tensor"),
            P("tensor", None),
            P(None, "tensor"),
            P("tensor", None),
            P("dp", "tensor", None),
        ),
        out_specs=(
            P("dp", "tensor", None),
            P("dp", "tensor", None),
            P(),
            P(),
            P(None, "tensor"),
            P(None, None, "tensor"),
            P("tensor", None),
            P(None, "tensor"),
            P("tensor", None),
        ),
        check_vma=False,
    )
```

```python
import functools
import math

import jax
import jax.numpy as jnp
from jax import lax
from jax.experimental import pallas as pl
from jax.experimental.pallas import tpu as pltpu
from jax.sharding import PartitionSpec as P

HEAD_DIM = 72
SHORT = 256
HIGH = lax.Precision.HIGHEST
F32 = jnp.float32
BF16 = jnp.bfloat16
SCALE = 1.0 / math.sqrt(HEAD_DIM)
SCALE_LOG2 = SCALE * math.log2(math.e)


def dot(left, right, left_dim, right_dim, precision=None):
    return lax.dot_general(
        left,
        right,
        (((left_dim,), (right_dim,)), ((), ())),
        precision=precision,
        preferred_element_type=F32,
    )


def features(steps_f, width_total):
    half = width_total // 2
    freqs = jnp.exp(-math.log(10000.0) * jnp.arange(half, dtype=F32) / half)
    angles = steps_f[:, None] * freqs[None, :]
    return jnp.concatenate([jnp.cos(angles), jnp.sin(angles)], axis=1)


def contract_rows(left, right):
    return dot(left, right, 0, 0)


def contract_exact(left, right):
    return dot(left, right, 0, 0, HIGH)


def times_transposed(left, right):
    return dot(left, right, 1, 1)


def normalize(values):
    average = jnp.mean(values, axis=-1, keepdims=True)
    centred = values - average
    inverse = lax.rsqrt(jnp.mean(centred * centred, axis=-1, keepdims=True) + 1e-06)
    return centred * inverse, inverse


def norm_back(grad_normed, normed, inverse):
    first = jnp.mean(grad_normed, axis=-1, keepdims=True)
    second = jnp.mean(grad_normed * normed, axis=-1, keepdims=True)
    return inverse * (grad_normed - first - normed * second)


def gelu_parts(x):
    root = math.sqrt(2.0 / math.pi)
    square = x * x
    bent = jnp.tanh(root * x * (1.0 + 0.044715 * square))
    half = 0.5 * (1.0 + bent)
    slope = half + 0.5 * x * (1.0 - bent * bent) * root * (1.0 + 3 * 0.044715 * square)
    return x * half, slope


def joined(own, other):
    return jnp.concatenate([own[0], other[0]], axis=1)


def attend_kernel(block, q0, q1, k0, k1, v0, v1, bias_ref, hot_ref, o_ref, lse_ref):
    tokens = o_ref.shape[2]
    query = jnp.concatenate([joined(q0, q1), bias_ref[...]], axis=0)
    key = jnp.concatenate([joined(k0, k1), hot_ref[...]], axis=0).T
    value = joined(v0, v1)
    for start in range(0, tokens, block):
        part = slice(start, start + block)
        scores = dot(key, query[:, part], 1, 0)
        top = jnp.max(scores, axis=0, keepdims=True) * SCALE_LOG2
        exps = jnp.exp2(scores * SCALE_LOG2 - top)
        total = jnp.sum(exps, axis=0, keepdims=True)
        out = dot(value, exps.astype(BF16), 1, 0)
        o_ref[0, :, part] = (out / total).astype(BF16)
        lse_ref[0, :, part] = top + jnp.log2(total)


def attend_back_kernel(
    block, q0, q1, k0, k1, v0, v1, bias_ref, hot_ref, o_ref, do0, do1, lse_ref, grad_ref
):
    tokens = o_ref.shape[2]
    query_all, key_all = joined(q0, q1), joined(k0, k1)
    query = jnp.concatenate([query_all, bias_ref[...]], axis=0)
    key = jnp.concatenate([key_all, hot_ref[...]], axis=0).T
    value = joined(v0, v1).T
    query_rows = query_all.T
    grad_out = joined(do0, do1)
    grad_rows = grad_out.T
    delta = jnp.sum(grad_out.astype(F32) * o_ref[0].astype(F32), axis=0, keepdims=True)
    lse = lse_ref[0]
    grad_key = grad_value = None
    for start in range(0, tokens, block):
        part = slice(start, start + block)
        scores = dot(key, query[:, part], 1, 0)
        probs = jnp.exp2(scores * SCALE_LOG2 - lse[:, part])
        grad_probs = dot(value, grad_out[:, part], 1, 0)
        grad_scores = (probs * (grad_probs - delta[:, part])).astype(BF16)
        value_term = dot(probs.astype(BF16), grad_rows[part], 1, 0)
        key_term = dot(grad_scores, query_rows[part], 1, 0)
        grad_value = value_term if grad_value is None else grad_value + value_term
        grad_key = key_term if grad_key is None else grad_key + key_term
        grad_ref[0, 0, :, part] = (dot(key_all, grad_scores, 1, 0) * SCALE).astype(BF16)
    grad_ref[1, 0] = (grad_key * SCALE).astype(BF16).T
    grad_ref[2, 0] = grad_value.astype(BF16).T


def head_spec(tokens, offset):
    return pl.BlockSpec((1, HEAD_DIM, tokens), lambda head: (head + offset, 0, 0))


def whole_spec(shape):
    return pl.BlockSpec(shape, lambda head: (0,) * len(shape))


def row_spec(tokens):
    return pl.BlockSpec((1, 1, tokens), lambda head: (head, 0, 0))


SMALL = pl.CostEstimate(flops=1 << 20, bytes_accessed=1 << 20, transcendentals=0)


def attend(own, other, bias, hot, first, count):
    heads = own.shape[0] // 3
    part = own.shape[2]
    tokens = part + other.shape[2]
    in_specs = [
        head_spec(part, component * heads + first) for component in range(3) for _ in range(2)
    ]
    return pl.pallas_call(
        functools.partial(attend_kernel, min(tokens, (1 << 20) // tokens)),
        grid=(count,),
        in_specs=in_specs + [whole_spec(bias.shape), whole_spec(hot.shape)],
        out_specs=[head_spec(tokens, 0), row_spec(tokens)],
        out_shape=[
            jax.ShapeDtypeStruct((count, HEAD_DIM, tokens), BF16),
            jax.ShapeDtypeStruct((count, 1, tokens), F32),
        ],
        compiler_params=pltpu.CompilerParams(vmem_limit_bytes=24 << 20),
        cost_estimate=SMALL,
    )(own, other, own, other, own, other, bias, hot)


def attend_back(own, other, bias, hot, out, grad_own, grad_other, lse, first, count):
    heads = own.shape[0] // 3
    part = own.shape[2]
    tokens = part + other.shape[2]
    in_specs = [
        head_spec(part, component * heads + first) for component in range(3) for _ in range(2)
    ]
    return pl.pallas_call(
        functools.partial(attend_back_kernel, min(tokens, (1 << 19) // tokens)),
        grid=(count,),
        in_specs=in_specs
        + [
            whole_spec(bias.shape),
            whole_spec(hot.shape),
            head_spec(tokens, 0),
            head_spec(part, first),
            head_spec(part, first),
            row_spec(tokens),
        ],
        out_specs=pl.BlockSpec((3, 1, HEAD_DIM, tokens), lambda head: (0, head, 0, 0)),
        out_shape=jax.ShapeDtypeStruct((3, count, HEAD_DIM, tokens), BF16),
        compiler_params=pltpu.CompilerParams(vmem_limit_bytes=24 << 20),
        cost_estimate=SMALL,
    )(own, other, own, other, own, other, bias, hot, out, grad_own, grad_other, lse)


def write_kernel(place, first, last, aliased, *refs):
    me = lax.axis_index("dp")
    sources = refs[: len(refs) - 3 - aliased]
    out_ref, wide, sems = refs[-3:]
    copies = []
    for group, source in enumerate(sources):
        for block in range(first, last):
            slot = group * (last - first) + block - first
            wide[slot] = source[block].astype(F32)
            copies.append(
                pltpu.make_async_copy(
                    wide.at[slot], place(out_ref, me, group, block), sems.at[slot]
                )
            )
            copies[-1].start()
    for copy in copies:
        copy.wait()


def write_out(groups, place, shape, onto=None, part=None):
    blocks, rows, columns = groups[0].shape
    first, last = (0, blocks) if part is None else part
    count = len(groups) * (last - first)
    anywhere = pl.BlockSpec(memory_space=pl.ANY)
    extra = [] if onto is None else [onto]
    return pl.pallas_call(
        functools.partial(write_kernel, place, first, last, len(extra)),
        in_specs=[pl.BlockSpec(memory_space=pltpu.VMEM)] * len(groups) + [anywhere] * len(extra),
        out_specs=anywhere,
        scratch_shapes=[
            pltpu.VMEM((count, rows, columns), F32),
            pltpu.SemaphoreType.DMA((count,)),
        ],
        out_shape=jax.ShapeDtypeStruct(shape, F32),
        input_output_aliases={} if onto is None else {len(groups): 0},
        compiler_params=pltpu.CompilerParams(vmem_limit_bytes=20 << 20),
        cost_estimate=SMALL,
    )(*groups, *extra)


def hidden_kernel(inputs_ref, weight_ref, active_ref, slope_ref):
    rows = inputs_ref.shape[0] // 4
    for start in range(0, 4 * rows, rows):
        part = slice(start, start + rows)
        active, slope = gelu_parts(dot(inputs_ref[part], weight_ref[...], 1, 0))
        active_ref[part] = active.astype(BF16)
        slope_ref[part] = slope.astype(BF16)


def hidden_units(inputs, weight):
    rows, width = inputs.shape
    units = weight.shape[1]
    block = units // 6
    out_block = pl.BlockSpec((rows, block), lambda i: (0, i))
    return pl.pallas_call(
        hidden_kernel,
        grid=(6,),
        in_specs=[
            pl.BlockSpec((rows, width), lambda i: (0, 0)),
            pl.BlockSpec((width, block), lambda i: (0, i)),
        ],
        out_specs=[out_block] * 2,
        out_shape=[jax.ShapeDtypeStruct((rows, units), BF16)] * 2,
        compiler_params=pltpu.CompilerParams(vmem_limit_bytes=20 << 20),
        cost_estimate=SMALL,
    )(inputs, weight)


def hidden_back_kernel(grad_ref, weight_ref, slope_ref, out_ref):
    rows = grad_ref.shape[0] // 4
    for start in range(0, 4 * rows, rows):
        part = slice(start, start + rows)
        grads = dot(grad_ref[part], weight_ref[...], 1, 1)
        out_ref[part] = (grads * slope_ref[part].astype(F32)).astype(BF16)


def hidden_back(grads, weight, slope):
    rows, width = grads.shape
    units = weight.shape[0]
    block = units // 6
    out_block = pl.BlockSpec((rows, block), lambda i: (0, i))
    return pl.pallas_call(
        hidden_back_kernel,
        grid=(6,),
        in_specs=[
            pl.BlockSpec((rows, width), lambda i: (0, 0)),
            pl.BlockSpec((block, width), lambda i: (i, 0)),
            out_block,
        ],
        out_specs=out_block,
        out_shape=jax.ShapeDtypeStruct((rows, units), BF16),
        compiler_params=pltpu.CompilerParams(vmem_limit_bytes=20 << 20),
        cost_estimate=SMALL,
    )(grads, weight, slope)


def gradient_kernel(left_is_blocked, half_ref, left_ref, right_ref, *refs):
    total = dot(left_ref[...], right_ref[...], 0, 0)
    if len(refs) == 2:
        total = total + refs[0][...].astype(F32)
    refs[-1][...] = total.astype(BF16)


def half_gradient(left, right, half, away, left_is_blocked):
    rows = left.shape[0]
    blocked = left if left_is_blocked else right
    whole = right if left_is_blocked else left
    units = blocked.shape[1] // 2
    block = units // 3
    half_spec = pl.BlockSpec((rows, block), lambda i, half_ref: (0, half_ref[0] * 3 + i))
    whole_block = pl.BlockSpec(whole.shape, lambda i, half_ref: (0, 0))
    if left_is_blocked:
        shape = (units, whole.shape[1])
        out_spec = pl.BlockSpec((block, shape[1]), lambda i, half_ref: (i, 0))
        in_specs = [half_spec, whole_block]
    else:
        shape = (whole.shape[1], units)
        out_spec = pl.BlockSpec((shape[0], block), lambda i, half_ref: (0, i))
        in_specs = [whole_block, half_spec]
    extra = [] if away is None else [away]
    return pl.pallas_call(
        functools.partial(gradient_kernel, left_is_blocked),
        grid_spec=pltpu.PrefetchScalarGridSpec(
            num_scalar_prefetch=1,
            grid=(3,),
            in_specs=in_specs + [out_spec] * len(extra),
            out_specs=out_spec,
        ),
        out_shape=jax.ShapeDtypeStruct(shape, BF16),
        compiler_params=pltpu.CompilerParams(vmem_limit_bytes=22 << 20),
        cost_estimate=SMALL,
    )(half.astype(jnp.int32)[None], left, right, *extra)


def down_gradient(active, grads, half, away=None):
    return half_gradient(active, grads, half, away, True)


def up_gradient(inputs, grads, half, away=None):
    return half_gradient(inputs, grads, half, away, False)


def rows_back_kernel(grad_ref, weight_ref, wide_ref, low_ref):
    total = dot(grad_ref[...], weight_ref[...], 1, 1)
    wide_ref[...] = total
    low_ref[...] = total.astype(BF16)


def rows_back(grads, weight, which):
    rows = grads.shape[0] // 2
    units = grads.shape[1]
    width = weight.shape[0]
    block = width // 3
    out_block = pl.BlockSpec((rows, block), lambda i: (0, i))
    return pl.pallas_call(
        rows_back_kernel,
        grid=(3,),
        in_specs=[
            pl.BlockSpec((rows, units), lambda i: (which, 0)),
            pl.BlockSpec((block, units), lambda i: (i, 0)),
        ],
        out_specs=[out_block] * 2,
        out_shape=[
            jax.ShapeDtypeStruct((rows, width), F32),
            jax.ShapeDtypeStruct((rows, width), BF16),
        ],
        compiler_params=pltpu.CompilerParams(vmem_limit_bytes=20 << 20),
        cost_estimate=SMALL,
    )(grads, weight)


def finish_kernel(
    half_steps,
    halfway_ref,
    own_ref,
    away_ref,
    branch_ref,
    two_ref,
    two_first_ref,
    two_last_ref,
    tokens_ref,
    mods_ref,
    result_ref,
    grad_ref,
):
    values = tokens_ref[...].astype(F32)
    two_away = jnp.where(
        pl.program_id(0) < half_steps, two_first_ref[...].astype(F32), two_last_ref[...].astype(F32)
    )
    two = two_ref[...] + two_away
    halfway = values + mods_ref[0, 2:3] * branch_ref[...]
    result_ref[...] = (halfway + mods_ref[0, 5:6] * two).astype(BF16)
    normed, inverse = normalize(values)
    grad_mod = own_ref[...] + away_ref[...].astype(F32)
    back = norm_back(grad_mod * (1.0 + mods_ref[0, 1:2]), normed, inverse)
    grad_ref[...] = (halfway_ref[...] + back).astype(BF16)


def finish(grad_halfway, own, away, branch, two, two_first, two_last, tokens, mods):
    rows, width = tokens.shape
    chunk = own.shape[0] // mods.shape[0]
    steps = rows // chunk
    half_steps = steps // 2
    row_block = pl.BlockSpec((chunk, width), lambda i: (i, 0))
    return pl.pallas_call(
        functools.partial(finish_kernel, half_steps),
        grid=(steps,),
        in_specs=[
            row_block,
            row_block,
            row_block,
            row_block,
            row_block,
            pl.BlockSpec((chunk, width), lambda i: (jnp.minimum(i, half_steps - 1), 0)),
            pl.BlockSpec((chunk, width), lambda i: (jnp.maximum(i - half_steps, 0), 0)),
            row_block,
            pl.BlockSpec((1, 6, width), lambda i: (i, 0, 0)),
        ],
        out_specs=[row_block, row_block],
        out_shape=[jax.ShapeDtypeStruct((rows, width), BF16)] * 2,
        compiler_params=pltpu.CompilerParams(vmem_limit_bytes=16 << 20),
        cost_estimate=SMALL,
    )(grad_halfway, own, away, branch, two, two_first, two_last, tokens, mods)


def heads_back_kernel(first_ref, second_ref, first_weight, second_weight, wide_ref, low_ref):
    total = dot(first_ref[...], first_weight[...], 0, 0)
    total = total + dot(second_ref[...], second_weight[...], 0, 0)
    wide_ref[...] = total
    low_ref[...] = total.astype(BF16)


def heads_back(first, second, first_weight, second_weight):
    rows = first.shape[1]
    width = first_weight.shape[1]
    block = width // 3
    out_block = pl.BlockSpec((rows, block), lambda i: (0, i))
    return pl.pallas_call(
        heads_back_kernel,
        grid=(3,),
        in_specs=[
            pl.BlockSpec(first.shape, lambda i: (0, 0)),
            pl.BlockSpec(second.shape, lambda i: (0, 0)),
            pl.BlockSpec((first_weight.shape[0], block), lambda i: (0, i)),
            pl.BlockSpec((second.shape[0], block), lambda i: (0, i)),
        ],
        out_specs=[out_block] * 2,
        out_shape=[
            jax.ShapeDtypeStruct((rows, width), F32),
            jax.ShapeDtypeStruct((rows, width), BF16),
        ],
        compiler_params=pltpu.CompilerParams(vmem_limit_bytes=22 << 20),
        cost_estimate=SMALL,
    )(first, second, first_weight, second_weight)


def condition_kernel(grad_ref, weight_ref, out_ref):
    out_ref[...] = dot(grad_ref[...], weight_ref[...], 1, 1).astype(BF16)


def condition_part(grads, weight):
    rows, depth = weight.shape
    block = rows // 3
    return pl.pallas_call(
        condition_kernel,
        grid=(3,),
        in_specs=[
            pl.BlockSpec((grads.shape[0], depth), lambda i: (0, 0)),
            pl.BlockSpec((block, depth), lambda i: (i, 0)),
        ],
        out_specs=pl.BlockSpec((grads.shape[0], block), lambda i: (0, i)),
        out_shape=jax.ShapeDtypeStruct((grads.shape[0], rows), BF16),
        compiler_params=pltpu.CompilerParams(vmem_limit_bytes=14 << 20),
        cost_estimate=SMALL,
    )(grads, weight)


def ada_kernel(act_ref, grad_ref, out_ref):
    out_ref[...] = dot(act_ref[...], grad_ref[...], 0, 0)


def ada_gradient(act, grads, columns):
    block = columns // 9
    return pl.pallas_call(
        ada_kernel,
        grid=(9,),
        in_specs=[
            pl.BlockSpec(act.shape, lambda i: (0, 0)),
            pl.BlockSpec((act.shape[0], block), lambda i: (0, i)),
        ],
        out_specs=pl.BlockSpec((act.shape[1], block), lambda i: (0, i)),
        out_shape=jax.ShapeDtypeStruct((act.shape[1], columns), F32),
        compiler_params=pltpu.CompilerParams(vmem_limit_bytes=14 << 20),
        cost_estimate=SMALL,
    )(act, grads)


def middle_kernel(own_steps, first_ref, heads_ref, weight_ref, own_ref, away_ref, mods_ref, *outs):
    branch_ref, inputs_ref, normed_ref = outs
    branch = first_ref[...] + dot(heads_ref[...], weight_ref[...], 0, 0)
    is_own = pl.program_id(0) < own_steps
    values = jnp.where(is_own, own_ref[...].astype(F32), away_ref[...].astype(F32))
    normed, _ = normalize(values + mods_ref[0, 2:3] * branch)
    branch_ref[...] = branch
    inputs_ref[...] = (normed * (1.0 + mods_ref[0, 4:5]) + mods_ref[0, 3:4]).astype(BF16)
    normed_ref[...] = normed.astype(BF16)


def middle(first, heads_away, weight, own, away, mods):
    rows, width = first.shape
    steps = mods.shape[0]
    chunk = rows // steps
    own_steps = own.shape[0] // chunk
    depth = heads_away.shape[0]
    row_block = pl.BlockSpec((chunk, width), lambda i: (i, 0))
    return pl.pallas_call(
        functools.partial(middle_kernel, own_steps),
        grid=(steps,),
        in_specs=[
            row_block,
            pl.BlockSpec((depth, chunk), lambda i: (0, (i + steps // 2) % steps)),
            pl.BlockSpec((depth, width), lambda i: (1, 0)),
            pl.BlockSpec((chunk, width), lambda i: (jnp.minimum(i, own_steps - 1), 0)),
            pl.BlockSpec((chunk, width), lambda i: (jnp.maximum(i - own_steps, 0), 0)),
            pl.BlockSpec((1, 6, width), lambda i: (i, 0, 0)),
        ],
        out_specs=[row_block] * 3,
        out_shape=[
            jax.ShapeDtypeStruct((rows, width), F32),
            jax.ShapeDtypeStruct((rows, width), BF16),
            jax.ShapeDtypeStruct((rows, width), BF16),
        ],
        compiler_params=pltpu.CompilerParams(vmem_limit_bytes=14 << 20),
        cost_estimate=SMALL,
    )(first, heads_away, weight, own, away, mods)


def middle_back_kernel(
    half_steps, own_ref, first_ref, second_ref, branch_ref, tokens_ref, cot_ref, mods_ref, *outs
):
    grad_ref, low_ref, sums_ref = outs
    arrived = jnp.where(
        pl.program_id(0) < half_steps, first_ref[...].astype(F32), second_ref[...].astype(F32)
    )
    branch = branch_ref[...]
    gate = mods_ref[0, 2:3]
    normed, inverse = normalize(tokens_ref[...].astype(F32) + gate * branch)
    grad_mod = own_ref[...] + arrived
    grad = cot_ref[...].astype(F32) + norm_back(
        grad_mod * (1.0 + mods_ref[0, 4:5]), normed, inverse
    )
    grad_ref[...] = grad
    low_ref[...] = (grad * gate).astype(BF16)
    sums_ref[0] = jnp.sum(grad * branch, axis=0, keepdims=True)


def middle_back(own, first, second, branch, tokens, cot, mods):
    rows, width = own.shape
    chunk = branch.shape[0] // mods.shape[0]
    steps = rows // chunk
    half_steps = steps // 2
    row_block = pl.BlockSpec((chunk, width), lambda i: (i, 0))
    return pl.pallas_call(
        functools.partial(middle_back_kernel, half_steps),
        grid=(steps,),
        in_specs=[
            row_block,
            pl.BlockSpec((chunk, width), lambda i: (jnp.minimum(i, half_steps - 1), 0)),
            pl.BlockSpec((chunk, width), lambda i: (jnp.maximum(i - half_steps, 0), 0)),
            row_block,
            row_block,
            row_block,
            pl.BlockSpec((1, 6, width), lambda i: (i, 0, 0)),
        ],
        out_specs=[row_block, row_block, pl.BlockSpec((1, 1, width), lambda i: (i, 0, 0))],
        out_shape=[
            jax.ShapeDtypeStruct((rows, width), F32),
            jax.ShapeDtypeStruct((rows, width), BF16),
            jax.ShapeDtypeStruct((steps, 1, width), F32),
        ],
        compiler_params=pltpu.CompilerParams(vmem_limit_bytes=14 << 20),
        cost_estimate=SMALL,
    )(own, first, second, branch, tokens, cot, mods)


def pair_body(
    tokens,
    segments,
    labels,
    timesteps,
    class_table,
    time_weight,
    ada_weight,
    qkv_weight,
    proj_weight,
    up_weight,
    down_weight,
    cotangent,
):
    position = lax.axis_index("tensor")
    rank = lax.axis_index("dp")
    dp_size = 16
    core, line, deep = rank % 2, rank // 2 % 2, rank // 4 % 2
    own_low = tokens[0]
    cot_low = cotangent[0]
    shard, width = own_low.shape
    pack = segments.shape[1]
    slot_count = labels.shape[1]
    class_count = class_table.shape[0]
    freq_width = time_weight.shape[0]
    local_width = qkv_weight.shape[2]
    heads = local_width // HEAD_DIM
    half_heads = heads // 2
    half_width = local_width // 2
    hidden_width = up_weight.shape[1]
    chunk = shard * SHORT // pack
    own_chunks = shard // chunk
    CORE, LINE, DEEP, FAR = 1, 2, 4, 8

    def fence(*values):
        return lax.optimization_barrier(values)

    def swap(x):
        return lax.ppermute(x, "tensor", [(0, 1), (1, 0)])

    def trade(x, bits):
        return lax.ppermute(x, "dp", [(i, i ^ bits) for i in range(dp_size)])

    def rows_of(x, index, count):
        size = x.shape[0] // count
        return lax.dynamic_slice_in_dim(x, index * size, size, 0)

    def columns_of(x, index, count):
        size = x.shape[1] // count
        return lax.dynamic_slice_in_dim(x, index * size, size, 1)

    def plus(a, b):
        return (a.astype(F32) + b.astype(F32)).astype(BF16)

    def halve(x, digit, bits):
        return plus(rows_of(x, digit, 2), trade(rows_of(x, 1 - digit, 2), bits))

    def digit(me, bits):
        return me // bits % 2

    def down_place(ref, me, group, block):
        index = (
            (digit(me, CORE) + group) % 2 * 4
            + (digit(me, LINE) + block // 2) % 2 * 2
            + (digit(me, DEEP) + block) % 2
        )
        return ref.at[index]

    def proj_place(ref, me, group, block):
        index = (digit(me, CORE) + group // 2) % 2 * 4 + (digit(me, LINE) + group % 2) % 2 * 2
        return ref.at[index + block - 3]

    def up_place(ref, me, group, block):
        index = (digit(me, LINE) + block // 2) % 2 * 2 + (digit(me, DEEP) + block) % 2
        column = (digit(me, CORE) + group) % 2 * (hidden_width // 2)
        return ref.at[index, :, pl.ds(pl.multiple_of(column, 128), hidden_width // 2)]

    def qkv_place(offset, bits):
        def place(ref, me, group, block):
            unit = (
                (digit(me, CORE) + group // 2) % 2 * 2 + (digit(me, bits) + group % 2) % 2
            ) * 3 + block
            return ref.at[unit // half_heads * heads + unit % half_heads + offset]

        return place

    def chunked(x):
        return x.reshape(x.shape[0] // chunk, chunk, x.shape[1])

    def flat(x):
        return x.reshape(x.shape[0] * chunk, x.shape[2])

    quarter = shard // 2
    tokens_away = swap(own_low)
    ids = jnp.stack([labels[0], timesteps[0]], axis=1)

    seg = segments[0]
    seg = jnp.where(position == 0, seg, jnp.roll(seg, shard))
    slots = jnp.arange(slot_count, dtype=jnp.int32)
    chunk_hot = (seg[::chunk][:, None] == slots[None, :]).astype(F32)
    mask_rows = -(-slot_count // 8) * 8
    same = jnp.arange(mask_rows, dtype=jnp.int32)[:, None] == seg[None, :]
    hot = same.astype(BF16)
    bias = jnp.where(same, 0.0, -1e30).astype(BF16)

    classes = jnp.arange(class_count, dtype=jnp.int32)

    def condition_of(ids):
        label_hot = (ids[:, 0][:, None] == classes[None, :]).astype(F32)
        feats = features(ids[:, 1].astype(F32), freq_width)
        values = dot(label_hot, class_table, 1, 0, HIGH) + dot(feats, time_weight, 1, 0, HIGH)
        return label_hot, feats, values

    def hop(y, bits):
        return jnp.concatenate([y, trade(y, bits)], axis=0)

    condition = condition_of(ids)[2]
    pad = jnp.zeros((slot_count, 124), jnp.int32)
    digits = jnp.concatenate([ids // 32, ids % 32, pad], axis=1).astype(BF16)
    act_low = jax.nn.silu(condition).astype(BF16)
    weight_t = qkv_weight.transpose(1, 2, 0).reshape(3 * local_width, width)
    weight_parts = weight_t.reshape(3, 2, half_width, width)
    weight_a = weight_parts[:, 0].reshape(3 * half_width, width)
    weight_b = weight_parts[:, 1].reshape(3 * half_width, width)
    mod_part, tokens_away, proj_half, weight_a, weight_b = fence(
        dot(act_low, ada_weight, 1, 0),
        tokens_away,
        rows_of(proj_weight, core, 2),
        weight_a,
        weight_b,
    )
    mod_away, tokens_away = fence(swap(mod_part), tokens_away)
    modulation = jnp.where(
        position == 0,
        jnp.concatenate([mod_part, mod_away], axis=1),
        jnp.concatenate([mod_away, mod_part], axis=1),
    )
    proj_half = swap(proj_half)
    per_chunk = dot(chunk_hot, modulation, 1, 0, HIGH)
    mods_own = [m[:, None, :] for m in jnp.split(per_chunk[:own_chunks], 6, axis=1)]
    mods_other = [m[:, None, :] for m in jnp.split(per_chunk[own_chunks:], 6, axis=1)]


    def enter(low, mods):
        values = chunked(low.astype(F32))
        normed, inverse = normalize(values)
        inputs = flat((normed * (1.0 + mods[1]) + mods[0]).astype(BF16))
        return values, normed, inverse, inputs

    def project(inputs):
        return dot(weight_t, inputs, 1, 1).astype(BF16).reshape(3 * heads, HEAD_DIM, shard)

    tokens_own, normed_one, inverse_one, inputs_one_own = enter(own_low, mods_own)
    qkv_own = project(inputs_one_own)
    tokens_other, normed_one_other, _, inputs_one_other = enter(tokens_away, mods_other)
    qkv_other = project(inputs_one_other)
    out_a, lse_a = attend(qkv_own, qkv_other, bias, hot, 0, half_heads)
    chunk_mods = per_chunk.reshape(pack // chunk, 6, width)
    out_a, qkv_own, chunk_mods = fence(out_a, qkv_own, chunk_mods)
    away_a = swap(out_a.reshape(half_width, pack))
    out_b, lse_b = attend(qkv_own, qkv_other, bias, hot, half_heads, half_heads)
    out_b, proj_half, away_a = fence(out_b, proj_half, away_a)
    away_b = swap(out_b.reshape(half_width, pack))
    proj_rest = trade(proj_half, CORE)
    proj_other = jnp.where(
        core == 0,
        jnp.concatenate([proj_half, proj_rest], axis=0),
        jnp.concatenate([proj_rest, proj_half], axis=0),
    )
    out_flat = jnp.concatenate([out_a, out_b], axis=0).reshape(local_width, pack)
    own_part, other_part = slice(0, shard), slice(shard, pack)

    def reordered(away):
        return jnp.concatenate([away[:, other_part], away[:, own_part]], axis=1)

    away_a, proj_other = fence(away_a, proj_other)
    first, _ = heads_back(out_flat, reordered(away_a), proj_weight, proj_other)
    away_b, cot_next, first = fence(away_b, cot_low, first)
    cot_away = swap(cot_next)
    branch_one, inputs_two, normed_two = middle(
        first, away_b, proj_other, own_low, tokens_away, chunk_mods
    )

    active, slope = hidden_units(inputs_two, up_weight)
    active, slope, cot_away = fence(active, slope, cot_away)
    grad_branch_two = jnp.concatenate(
        [
            flat((chunked(cot_low.astype(F32)) * mods_own[5]).astype(BF16)),
            flat((chunked(cot_away.astype(F32)) * mods_other[5]).astype(BF16)),
        ],
        axis=0,
    )

    down_away = trade(down_gradient(active, grad_branch_two, 1 - core), CORE)
    grad_hidden = hidden_back(grad_branch_two, down_weight, slope)
    down_sum = down_gradient(active, grad_branch_two, core, down_away)
    down_sum, grad_hidden = fence(down_sum, grad_hidden)
    down_x = trade(rows_of(down_sum, 1 - line, 2), LINE)
    mod_two_other, mod_two_away = rows_back(grad_hidden, up_weight, 1)
    mod_two_away, grad_hidden = fence(mod_two_away, grad_hidden)

    arrived_a = swap(mod_two_away[:quarter])
    up_away = trade(up_gradient(inputs_two, grad_hidden, 1 - core), CORE)
    mod_two, _ = rows_back(grad_hidden, up_weight, 0)
    arrived_a, up_away, mod_two, mod_two_next, grad_hidden, active = fence(
        arrived_a, up_away, mod_two, mod_two_away[quarter:], grad_hidden, active
    )
    arrived_b = swap(mod_two_next)
    up_sum = up_gradient(inputs_two, grad_hidden, core, up_away)
    up_x = trade(rows_of(up_sum, 1 - line, 2), LINE)
    branch_two_away = dot(active[other_part], down_weight, 1, 0)
    branch_two = dot(active[own_part], down_weight, 1, 0)
    arrived_b, mod_two, branch_two_away, branch_two, down_x = fence(
        arrived_b, mod_two, branch_two_away, branch_two, down_x
    )

    down_sum = plus(rows_of(down_sum, line, 2), down_x)
    down_z = trade(rows_of(down_sum, 1 - deep, 2), DEEP)
    grad_halfway, grad_branch_one, gate_one_sums = middle_back(
        mod_two, arrived_a, arrived_b, branch_one, own_low, cot_low, chunk_mods
    )
    grad_att_away = dot(proj_other, grad_branch_one, 1, 1).astype(BF16)
    grad_att_away, grad_branch_one = fence(grad_att_away, grad_branch_one)

    grad_att_other = swap(grad_att_away)
    grad_att_own = dot(proj_weight, grad_branch_one, 1, 1).astype(BF16)
    def chunk_sums(own, other):
        return jnp.concatenate([jnp.sum(own, axis=1), jnp.sum(other, axis=1)], axis=0)

    normed_two = chunked(normed_two.astype(F32))
    late_terms = jnp.concatenate(
        [
            jnp.concatenate([gate_one_sums[:, 0], jnp.zeros_like(gate_one_sums[:, 0])], axis=0),
            chunk_sums(chunked(mod_two), chunked(mod_two_other)),
            chunk_sums(
                chunked(mod_two) * normed_two[:own_chunks],
                chunked(mod_two_other) * normed_two[own_chunks:],
            ),
            chunk_sums(
                chunked(branch_two) * chunked(cot_low.astype(F32)),
                chunked(branch_two_away) * chunked(cot_away.astype(F32)),
            ),
        ],
        axis=1,
    )
    inputs_one = jnp.concatenate([inputs_one_own, inputs_one_other], axis=0)
    grad_att_other, grad_att_own, down_z, branch_one_next, inputs_one, late_terms = fence(
        grad_att_other, grad_att_own, down_z, grad_branch_one, inputs_one, late_terms
    )
    down_sum = plus(rows_of(down_sum, deep, 2), down_z)
    down_block = down_sum.shape[0] // 2
    down_far_a = trade(down_sum[:down_block], FAR)

    def back(out, lse, first):
        return attend_back(
            qkv_own,
            qkv_other,
            bias,
            hot,
            out,
            grad_att_own.reshape(heads, HEAD_DIM, shard),
            grad_att_other.reshape(heads, HEAD_DIM, shard),
            lse,
            first,
            half_heads,
        ).reshape(3 * half_width, pack)

    def qkv_half(grad):
        return lambda half: dot(rows_of(grad, half, 2), inputs_one, 1, 0)

    grads_one_other = swap(branch_one_next)
    grad_qkv_a = back(out_a, lse_a, 0)
    grad_qkv_a, up_x, down_far_a, down_next = fence(
        grad_qkv_a, up_x, down_far_a, down_sum[down_block:]
    )
    down_far_b = trade(down_next, FAR)
    up_sum = plus(rows_of(up_sum, line, 2), up_x)
    up_z = trade(rows_of(up_sum, 1 - deep, 2), DEEP)
    qkv_make = qkv_half(grad_qkv_a)
    qkv_a_away = trade(qkv_make(1 - core).astype(BF16), CORE)
    qkv_a = plus(qkv_make(core), qkv_a_away)
    qkv_a, grad_att_own = fence(qkv_a, grad_att_own)
    qkv_a_x = trade(rows_of(qkv_a, 1 - line, 2), LINE)
    grad_qkv_b = back(out_b, lse_b, half_heads)
    grad_qkv_b, qkv_a_x, up_z, down_far_b, grads_one_other = fence(
        grad_qkv_b, qkv_a_x, up_z, down_far_b, grads_one_other
    )
    qkv_a = plus(rows_of(qkv_a, line, 2), qkv_a_x)
    up_sum = plus(rows_of(up_sum, deep, 2), up_z)
    down_sum = plus(down_sum, jnp.concatenate([down_far_a, down_far_b], axis=0))
    down_z = trade(down_sum, DEEP)
    down_x = trade(down_sum, LINE)
    block = up_sum.shape[0] // 2
    up_far_a = trade(up_sum[:block], FAR)
    mod_one = dot(grad_qkv_a, weight_a, 0, 0) + dot(grad_qkv_b, weight_b, 0, 0)
    mod_one_own, mod_one_away = chunked(mod_one[own_part]), chunked(mod_one[other_part])
    chunk_terms = jnp.concatenate(
        [
            chunk_sums(mod_one_own, mod_one_away),
            chunk_sums(mod_one_own * normed_one, mod_one_away * normed_one_other),
            late_terms,
        ],
        axis=1,
    )
    slot_terms = dot(chunk_hot, chunk_terms, 0, 0, HIGH).astype(BF16)
    half = slot_terms.shape[1] // 2
    low, high = slot_terms[:, :half], slot_terms[:, half:]
    keep = jnp.where(position == 0, low, high)
    away = jnp.where(position == 0, high, low)
    (
        away,
        keep,
        mod_one_next,
        down_z,
        down_x,
        up_far_a,
        grad_qkv_b,
        up_next,
        qkv_a,
    ) = fence(
        away,
        keep,
        flat(mod_one_away).astype(BF16),
        down_z,
        down_x,
        up_far_a,
        grad_qkv_b,
        up_sum[block:],
        qkv_a,
    )

    gathered = jnp.concatenate([plus(keep, swap(away)), digits], axis=1)[None]
    down_zx = trade(down_z, LINE)
    up_far_b = trade(up_next, FAR)
    qkv_a_z = trade(rows_of(qkv_a, 1 - deep, 2), DEEP)
    qkv_make_b = qkv_half(grad_qkv_b)

    def proj_half_of(half):
        rows = rows_of(out_flat, half, 2)
        return dot(rows[:, own_part], grad_branch_one, 1, 0) + dot(
            rows[:, other_part], grads_one_other, 1, 0
        )

    def packed(qkv, proj, index):
        return jnp.concatenate([rows_of(qkv, index, 2), rows_of(proj, index, 2)], axis=0)

    def unpacked(both):
        cut = both.shape[0] * 3 // 5
        return both[:cut], both[cut:]

    def in_order(digit, own, other):
        return jnp.where(
            digit == 0,
            jnp.concatenate([own, other], axis=0),
            jnp.concatenate([other, own], axis=0),
        )

    rest = trade(
        jnp.concatenate(
            [qkv_make_b(1 - core).astype(BF16), proj_half_of(1 - core).astype(BF16)], axis=0
        ),
        CORE,
    )
    qkv_rows = 3 * half_width // 2
    qkv_b = plus(qkv_make_b(core), rest[:qkv_rows])
    proj_sum = plus(proj_half_of(core), rest[qkv_rows:])
    both_next = packed(qkv_b, proj_sum, 1 - line)
    both = packed(qkv_b, proj_sum, line)
    gathered, up_far_b, down_zx, qkv_a_z, both_next, both, mod_one_next = fence(
        gathered, up_far_b, down_zx, qkv_a_z, both_next, both, mod_one_next
    )

    up_low = plus(up_sum[:block], up_far_a)
    up_high = plus(up_next, up_far_b)
    up_sum = jnp.concatenate([up_low, up_high], axis=0)
    qkv_a = plus(rows_of(qkv_a, deep, 2), qkv_a_z)
    up_sum, qkv_a, both_next, gathered, mod_one_next = fence(
        up_sum, qkv_a, both_next, gathered, mod_one_next
    )
    gathered = hop(gathered, LINE)
    mod_one_other = swap(mod_one_next)
    both_x = trade(both_next, LINE)
    up_z = trade(up_sum, DEEP)
    qkv_a_far = trade(qkv_a, FAR)
    (
        gathered,
        both_x,
        up_z,
        qkv_a_far,
        mod_one_other,
        both,
        down_sum,
        down_z,
        down_x,
        down_zx,
    ) = fence(
        gathered,
        both_x,
        up_z,
        qkv_a_far,
        mod_one_other,
        both,
        down_sum,
        down_z,
        down_x,
        down_zx,
    )
    both = plus(both, both_x)
    both_next = packed(*unpacked(both), 1 - deep)
    qkv_a = plus(qkv_a, qkv_a_far)
    both_next, qkv_a, gathered, up_sum, both, two_low = fence(
        both_next, qkv_a, gathered, up_sum, both, branch_two_away.astype(BF16)
    )
    two_first = swap(two_low[:quarter])
    gathered = hop(gathered, FAR)
    up_x = trade(up_sum, LINE)
    down_blocks = jnp.stack([down_sum, down_z, down_x, down_zx])
    both_z = trade(both_next, DEEP)
    qkv_a_z = trade(qkv_a, DEEP)
    both = packed(*unpacked(both), deep)
    gathered, up_x, both_z, qkv_a_z, both, down_blocks, two_first, two_next = fence(
        gathered, up_x, both_z, qkv_a_z, both, down_blocks, two_first, two_low[quarter:]
    )
    both = plus(both, both_z)
    qkv_a = in_order(deep, qkv_a, qkv_a_z).reshape(3, HEAD_DIM, width)
    both, qkv_a, gathered, up_z, down_blocks, two_next = fence(
        both, qkv_a, gathered, up_z, down_blocks, two_next
    )
    two_last = swap(two_next)
    grad_down = write_out(
        [down_blocks, trade(down_blocks, CORE)], down_place, (8, hidden_width // 8, width)
    )
    gathered = hop(gathered, DEEP)
    up_zx = trade(up_z, LINE)
    both_far = trade(both, FAR)
    up_zx, both_far, gathered, grad_down, two_last = fence(
        up_zx, both_far, gathered, grad_down, two_last
    )
    both = plus(both, both_far)
    both, gathered, qkv_a = fence(both, gathered, qkv_a)
    up_blocks = jnp.stack([up_sum, up_z, up_x, up_zx])
    both_z = trade(both, DEEP)
    qkv_a_x = trade(qkv_a, LINE)
    up_blocks_c = trade(up_blocks, CORE)
    grad_mod_all = hop(gathered, CORE).reshape(dp_size * slot_count, half + 128)
    cond_part = condition_part(grad_mod_all, ada_weight)
    result, grad_input = finish(
        grad_halfway,
        mod_one,
        mod_one_other,
        branch_one,
        branch_two,
        two_first,
        two_last,
        own_low,
        chunk_mods,
    )
    both_z, cond_part, grad_mod_all, up_blocks_c, qkv_a_x, result = fence(
        both_z, cond_part, grad_mod_all, up_blocks_c, qkv_a_x, result
    )
    both = jnp.concatenate(
        [in_order(deep, a, b) for a, b in zip(unpacked(both), unpacked(both_z), strict=True)],
        axis=0,
    ).reshape(5, HEAD_DIM, width)
    both_x = trade(both, LINE)
    both_c = trade(both, CORE)
    grad_act = cond_part.astype(F32) + swap(cond_part).astype(F32)
    qkv_a_c = trade(qkv_a, CORE)
    qkv_a_xc = trade(qkv_a_x, CORE)
    grad_up = write_out([up_blocks, up_blocks_c], up_place, (4, width // 4, hidden_width))
    ids_all = grad_mod_all[:, half : half + 4].astype(jnp.int32)
    label_hot, features_all, condition_all = condition_of(ids_all[:, :2] * 32 + ids_all[:, 2:])
    act_all = jax.nn.silu(condition_all).astype(BF16)
    grad_ada = ada_gradient(act_all, grad_mod_all, ada_weight.shape[1])
    both_x, both_c, grad_up, grad_act, grad_ada, qkv_a_c, qkv_a_xc = fence(
        both_x, both_c, grad_up, grad_act, grad_ada, qkv_a_c, qkv_a_xc
    )
    both_xc = trade(both_x, CORE)
    qkv_shape = (3 * heads, HEAD_DIM, width)
    grad_qkv = write_out([qkv_a, qkv_a_x, qkv_a_c, qkv_a_xc], qkv_place(0, LINE), qkv_shape)

    grad_condition = jax.vjp(jax.nn.silu, condition_all)[1](grad_act)[0]
    grad_class = dot(label_hot.astype(BF16), grad_condition.astype(BF16), 0, 0)
    grad_time = dot(features_all, grad_condition, 0, 0, HIGH)
    groups = [both, both_x, both_c, both_xc]
    grad_qkv = write_out(groups, qkv_place(half_heads, LINE), qkv_shape, grad_qkv, (0, 3))
    grad_proj = write_out(groups, proj_place, (8, HEAD_DIM, width), None, (3, 5))
    return (
        result[None],
        grad_input[None],
        grad_class,
        grad_time,
        grad_ada,
        grad_qkv.reshape(3, local_width, width).transpose(2, 0, 1),
        grad_proj.reshape(local_width, width),
        grad_up.reshape(width, hidden_width),
        grad_down.reshape(hidden_width, width),
    )


def any_body(
    tokens,
    segments,
    labels,
    timesteps,
    class_table,
    time_weight,
    ada_weight,
    qkv_weight,
    proj_weight,
    up_weight,
    down_weight,
    cotangent,
):
    own_tokens = tokens[0].astype(jnp.float32)
    shard_rows = own_tokens.shape[0]
    model_width = own_tokens.shape[1]
    seg_all = segments[0]
    pack_rows = seg_all.shape[0]
    slot_count = labels.shape[1]
    class_count = class_table.shape[0]
    freq_width = time_weight.shape[0]
    local_width = qkv_weight.shape[2]
    head_count = local_width // HEAD_DIM
    scale_factor = 1.0 / math.sqrt(HEAD_DIM)
    position = lax.axis_index("tensor")
    seg_own = lax.dynamic_slice_in_dim(seg_all, position * shard_rows, shard_rows)
    own_hot = (seg_own[:, None] == jnp.arange(slot_count, dtype=jnp.int32)[None, :]).astype(
        jnp.float32
    )
    label_hot = (labels[0][:, None] == jnp.arange(class_count, dtype=jnp.int32)[None, :]).astype(
        jnp.float32
    )
    step_feats = features(timesteps[0].astype(jnp.float32), freq_width)
    condition = jnp.dot(label_hot, class_table, precision=HIGH) + jnp.dot(
        step_feats, time_weight, precision=HIGH
    )
    act_low = jax.nn.silu(condition).astype(jnp.bfloat16)
    mod_part = jnp.dot(act_low, ada_weight, preferred_element_type=jnp.float32)
    modulation = lax.all_gather(mod_part, "tensor", axis=1, tiled=True)
    per_token = jnp.dot(own_hot, modulation, precision=HIGH)
    shift_one, scale_one, gate_one, shift_two, scale_two, gate_two = jnp.split(per_token, 6, axis=1)
    normed_one, inverse_one = normalize(own_tokens)
    modulated_one = (normed_one * (1.0 + scale_one) + shift_one).astype(jnp.bfloat16)
    inputs_one = lax.all_gather(modulated_one, "tensor", axis=0, tiled=True)
    qkv_flat = qkv_weight.reshape(model_width, 3 * local_width)
    qkv = jnp.dot(inputs_one, qkv_flat, preferred_element_type=jnp.float32).astype(jnp.bfloat16)
    qkv_heads = qkv.reshape(pack_rows, 3, head_count, HEAD_DIM).transpose(1, 2, 0, 3)
    queries = qkv_heads[0]
    keys = qkv_heads[1]
    values = qkv_heads[2]
    block = min(512, pack_rows)
    block_count = pack_rows // block
    starts = jnp.arange(block_count, dtype=jnp.int32) * block

    def scores_of(start):
        query_block = lax.dynamic_slice_in_dim(queries, start, block, 1)
        seg_block = lax.dynamic_slice_in_dim(seg_all, start, block)
        raw = (
            jnp.einsum("hqd,hkd->hqk", query_block, keys, preferred_element_type=jnp.float32)
            * scale_factor
        )
        same = (seg_block[:, None] == seg_all[None, :])[None]
        return (jnp.where(same, raw, -1e30), query_block)

    def attend(start):
        scores = scores_of(start)[0]
        top = jnp.max(scores, axis=-1, keepdims=True)
        exps = jnp.exp(scores - top)
        total = jnp.sum(exps, axis=-1, keepdims=True)
        weights = (exps / total).astype(jnp.bfloat16)
        out_block = jnp.einsum("hqk,hkd->hqd", weights, values, preferred_element_type=jnp.float32)
        return (out_block, (top + jnp.log(total))[..., 0])

    out_blocks, lse_blocks = lax.map(attend, starts)
    attended = out_blocks.transpose(0, 2, 1, 3).reshape(pack_rows, local_width).astype(jnp.bfloat16)
    lse_all = lse_blocks.transpose(1, 0, 2).reshape(head_count, pack_rows)
    branch_one = lax.psum_scatter(
        jnp.dot(attended, proj_weight, preferred_element_type=jnp.float32),
        "tensor",
        scatter_dimension=0,
        tiled=True,
    )
    halfway = own_tokens + gate_one * branch_one
    normed_two, inverse_two = normalize(halfway)
    modulated_two = (normed_two * (1.0 + scale_two) + shift_two).astype(jnp.bfloat16)
    inputs_two = lax.all_gather(modulated_two, "tensor", axis=0, tiled=True)
    hidden = jnp.dot(inputs_two, up_weight, preferred_element_type=jnp.float32)
    active = jax.nn.gelu(hidden, approximate=True).astype(jnp.bfloat16)
    branch_two = lax.psum_scatter(
        jnp.dot(active, down_weight, preferred_element_type=jnp.float32).astype(jnp.bfloat16),
        "tensor",
        scatter_dimension=0,
        tiled=True,
    ).astype(jnp.float32)
    result = halfway + gate_two * branch_two
    grad_out = cotangent[0].astype(jnp.float32)
    grad_gate_two = grad_out * branch_two
    grad_branch_two = (grad_out * gate_two).astype(jnp.bfloat16)
    grads_two = lax.all_gather(grad_branch_two, "tensor", axis=0, tiled=True)
    grad_down = contract_rows(active, grads_two)
    grad_active = times_transposed(grads_two, down_weight)
    gelu_back = jax.vjp(lambda inner: jax.nn.gelu(inner, approximate=True), hidden)[1]
    grad_hidden = gelu_back(grad_active)[0].astype(jnp.bfloat16)
    grad_up = contract_rows(inputs_two, grad_hidden)
    grad_mod_two = lax.psum_scatter(
        times_transposed(grad_hidden, up_weight), "tensor", scatter_dimension=0, tiled=True
    )
    grad_halfway = grad_out + norm_back(grad_mod_two * (1.0 + scale_two), normed_two, inverse_two)
    grad_gate_one = grad_halfway * branch_one
    grad_branch_one = (grad_halfway * gate_one).astype(jnp.bfloat16)
    grads_one = lax.all_gather(grad_branch_one, "tensor", axis=0, tiled=True)
    grad_proj = contract_rows(attended, grads_one)
    grad_attended = times_transposed(grads_one, proj_weight).astype(jnp.bfloat16)
    grad_heads = grad_attended.reshape(pack_rows, head_count, HEAD_DIM).transpose(1, 0, 2)

    def attend_back(carry, start):
        grad_keys, grad_values = carry
        scores, query_block = scores_of(start)
        lse_block = lax.dynamic_slice_in_dim(lse_all, start, block, 1)
        probs = jnp.exp(scores - lse_block[..., None])
        grad_block = lax.dynamic_slice_in_dim(grad_heads, start, block, 1)
        grad_probs = jnp.einsum(
            "hqd,hkd->hqk", grad_block, values, preferred_element_type=jnp.float32
        )
        grad_scores = (
            probs * (grad_probs - jnp.sum(probs * grad_probs, axis=-1, keepdims=True))
        ).astype(jnp.bfloat16)
        grad_query = (
            jnp.einsum("hqk,hkd->hqd", grad_scores, keys, preferred_element_type=jnp.float32)
            * scale_factor
        )
        grad_keys = (
            grad_keys
            + jnp.einsum(
                "hqk,hqd->hkd", grad_scores, query_block, preferred_element_type=jnp.float32
            )
            * scale_factor
        )
        grad_values = grad_values + jnp.einsum(
            "hqk,hqd->hkd",
            probs.astype(jnp.bfloat16),
            grad_block,
            preferred_element_type=jnp.float32,
        )
        return ((grad_keys, grad_values), grad_query)

    empty = jnp.zeros((head_count, pack_rows, HEAD_DIM), jnp.float32)
    key_grads, grad_queries = lax.scan(attend_back, (empty, empty), starts)
    query_grads = grad_queries.transpose(1, 0, 2, 3).reshape(head_count, pack_rows, HEAD_DIM)
    grad_stack = jnp.stack([query_grads, key_grads[0], key_grads[1]], axis=0)
    grad_qkv = (
        grad_stack.transpose(2, 0, 1, 3).reshape(pack_rows, 3 * local_width).astype(jnp.bfloat16)
    )
    grad_qkv_weight = contract_rows(inputs_one, grad_qkv).reshape(model_width, 3, local_width)
    grad_mod_one = lax.psum_scatter(
        times_transposed(grad_qkv, qkv_flat).astype(jnp.bfloat16),
        "tensor",
        scatter_dimension=0,
        tiled=True,
    ).astype(jnp.float32)
    grad_input = grad_halfway + norm_back(grad_mod_one * (1.0 + scale_one), normed_one, inverse_one)
    grad_per_token = jnp.concatenate(
        [
            grad_mod_one,
            grad_mod_one * normed_one,
            grad_gate_one,
            grad_mod_two,
            grad_mod_two * normed_two,
            grad_gate_two,
        ],
        axis=1,
    )
    slot_terms = contract_exact(own_hot, grad_per_token)
    grad_modulation = lax.psum_scatter(
        slot_terms.astype(jnp.bfloat16), "tensor", scatter_dimension=1, tiled=True
    )
    grad_ada = contract_rows(act_low, grad_modulation)
    cond_part = times_transposed(grad_modulation, ada_weight)
    grad_activated = lax.psum(cond_part.astype(jnp.bfloat16), "tensor").astype(jnp.float32)
    grad_condition = jax.vjp(jax.nn.silu, condition)[1](grad_activated)[0]
    grad_class = contract_exact(label_hot, grad_condition)
    grad_time = contract_exact(step_feats, grad_condition)
    summed = (
        lax.psum(grad_class.astype(jnp.bfloat16), "dp").astype(jnp.float32),
        lax.psum(grad_time.astype(jnp.bfloat16), "dp").astype(jnp.float32),
        lax.psum(grad_ada.astype(jnp.bfloat16), "dp").astype(jnp.float32),
        lax.psum(grad_qkv_weight.astype(jnp.bfloat16), "dp").astype(jnp.float32),
        lax.psum(grad_proj.astype(jnp.bfloat16), "dp").astype(jnp.float32),
        lax.psum(grad_up.astype(jnp.bfloat16), "dp").astype(jnp.float32),
        lax.psum(grad_down.astype(jnp.bfloat16), "dp").astype(jnp.float32),
    )
    grad_class, grad_time, grad_ada, grad_qkv_weight, grad_proj, grad_up, grad_down = summed
    return (
        result.astype(jnp.bfloat16)[None],
        grad_input.astype(jnp.bfloat16)[None],
        grad_class,
        grad_time,
        grad_ada,
        grad_qkv_weight,
        grad_proj,
        grad_up,
        grad_down,
    )


def solution(mesh):
    pairs = mesh.shape["dp"] == 16 and mesh.shape["tensor"] == 2
    return jax.shard_map(
        pair_body if pairs else any_body,
        mesh=mesh,
        in_specs=(
            P("dp", "tensor", None),
            P("dp", None),
            P("dp", None),
            P("dp", None),
            P(),
            P(),
            P(None, "tensor"),
            P(None, None, "tensor"),
            P("tensor", None),
            P(None, "tensor"),
            P("tensor", None),
            P("dp", "tensor", None),
        ),
        out_specs=(
            P("dp", "tensor", None),
            P("dp", "tensor", None),
            P(),
            P(),
            P(None, "tensor"),
            P(None, None, "tensor"),
            P("tensor", None),
            P(None, "tensor"),
            P("tensor", None),
        ),
        check_vma=False,
    )
```

```python
import functools
import math

import jax
import jax.numpy as jnp
from jax import lax
from jax.experimental import pallas as pl
from jax.experimental.pallas import tpu as pltpu
from jax.sharding import PartitionSpec as P

HEAD_DIM = 72
SHORT = 256
HIGH = lax.Precision.HIGHEST
F32 = jnp.float32
BF16 = jnp.bfloat16
SCALE = 1.0 / math.sqrt(HEAD_DIM)
SCALE_LOG2 = SCALE * math.log2(math.e)


def dot(left, right, left_dim, right_dim, precision=None):
    return lax.dot_general(
        left,
        right,
        (((left_dim,), (right_dim,)), ((), ())),
        precision=precision,
        preferred_element_type=F32,
    )


def features(steps_f, width_total):
    half = width_total // 2
    freqs = jnp.exp(-math.log(10000.0) * jnp.arange(half, dtype=F32) / half)
    angles = steps_f[:, None] * freqs[None, :]
    return jnp.concatenate([jnp.cos(angles), jnp.sin(angles)], axis=1)


def contract_rows(left, right):
    return dot(left, right, 0, 0)


def contract_exact(left, right):
    return dot(left, right, 0, 0, HIGH)


def times_transposed(left, right):
    return dot(left, right, 1, 1)


def normalize(values):
    average = jnp.mean(values, axis=-1, keepdims=True)
    centred = values - average
    inverse = lax.rsqrt(jnp.mean(centred * centred, axis=-1, keepdims=True) + 1e-06)
    return centred * inverse, inverse


def norm_back(grad_normed, normed, inverse):
    first = jnp.mean(grad_normed, axis=-1, keepdims=True)
    second = jnp.mean(grad_normed * normed, axis=-1, keepdims=True)
    return inverse * (grad_normed - first - normed * second)


def gelu_parts(x):
    root = math.sqrt(2.0 / math.pi)
    square = x * x
    bent = jnp.tanh(root * x * (1.0 + 0.044715 * square))
    half = 0.5 * (1.0 + bent)
    slope = half + 0.5 * x * (1.0 - bent * bent) * root * (1.0 + 3 * 0.044715 * square)
    return x * half, slope


def joined(own, other):
    return jnp.concatenate([own[0], other[0]], axis=1)


def attend_kernel(block, q0, q1, k0, k1, v0, v1, bias_ref, hot_ref, o_ref, lse_ref):
    tokens = o_ref.shape[2]
    query = jnp.concatenate([joined(q0, q1), bias_ref[...]], axis=0)
    key = jnp.concatenate([joined(k0, k1), hot_ref[...]], axis=0).T
    value = joined(v0, v1)
    for start in range(0, tokens, block):
        part = slice(start, start + block)
        scores = dot(key, query[:, part], 1, 0)
        top = jnp.max(scores, axis=0, keepdims=True) * SCALE_LOG2
        exps = jnp.exp2(scores * SCALE_LOG2 - top)
        total = jnp.sum(exps, axis=0, keepdims=True)
        out = dot(value, exps.astype(BF16), 1, 0)
        o_ref[0, :, part] = (out / total).astype(BF16)
        lse_ref[0, :, part] = top + jnp.log2(total)


def attend_back_kernel(
    block, q0, q1, k0, k1, v0, v1, bias_ref, hot_ref, o_ref, do0, do1, lse_ref, grad_ref
):
    tokens = o_ref.shape[2]
    query_all, key_all = joined(q0, q1), joined(k0, k1)
    query = jnp.concatenate([query_all, bias_ref[...]], axis=0)
    key = jnp.concatenate([key_all, hot_ref[...]], axis=0).T
    value = joined(v0, v1).T
    query_rows = query_all.T
    grad_out = joined(do0, do1)
    grad_rows = grad_out.T
    delta = jnp.sum(grad_out.astype(F32) * o_ref[0].astype(F32), axis=0, keepdims=True)
    lse = lse_ref[0]
    grad_key = grad_value = None
    for start in range(0, tokens, block):
        part = slice(start, start + block)
        scores = dot(key, query[:, part], 1, 0)
        probs = jnp.exp2(scores * SCALE_LOG2 - lse[:, part])
        grad_probs = dot(value, grad_out[:, part], 1, 0)
        grad_scores = (probs * (grad_probs - delta[:, part])).astype(BF16)
        value_term = dot(probs.astype(BF16), grad_rows[part], 1, 0)
        key_term = dot(grad_scores, query_rows[part], 1, 0)
        grad_value = value_term if grad_value is None else grad_value + value_term
        grad_key = key_term if grad_key is None else grad_key + key_term
        grad_ref[0, 0, :, part] = (dot(key_all, grad_scores, 1, 0) * SCALE).astype(BF16)
    grad_ref[1, 0] = (grad_key * SCALE).astype(BF16).T
    grad_ref[2, 0] = grad_value.astype(BF16).T


def head_spec(tokens, offset):
    return pl.BlockSpec((1, HEAD_DIM, tokens), lambda head: (head + offset, 0, 0))


def whole_spec(shape):
    return pl.BlockSpec(shape, lambda head: (0,) * len(shape))


def row_spec(tokens):
    return pl.BlockSpec((1, 1, tokens), lambda head: (head, 0, 0))


SMALL = pl.CostEstimate(flops=1 << 20, bytes_accessed=1 << 20, transcendentals=0)


def attend(own, other, bias, hot, first, count):
    heads = own.shape[0] // 3
    part = own.shape[2]
    tokens = part + other.shape[2]
    in_specs = [
        head_spec(part, component * heads + first) for component in range(3) for _ in range(2)
    ]
    return pl.pallas_call(
        functools.partial(attend_kernel, min(tokens, (1 << 20) // tokens)),
        grid=(count,),
        in_specs=in_specs + [whole_spec(bias.shape), whole_spec(hot.shape)],
        out_specs=[head_spec(tokens, 0), row_spec(tokens)],
        out_shape=[
            jax.ShapeDtypeStruct((count, HEAD_DIM, tokens), BF16),
            jax.ShapeDtypeStruct((count, 1, tokens), F32),
        ],
        compiler_params=pltpu.CompilerParams(vmem_limit_bytes=24 << 20),
        cost_estimate=SMALL,
    )(own, other, own, other, own, other, bias, hot)


def attend_back(own, other, bias, hot, out, grad_own, grad_other, lse, first, count):
    heads = own.shape[0] // 3
    part = own.shape[2]
    tokens = part + other.shape[2]
    in_specs = [
        head_spec(part, component * heads + first) for component in range(3) for _ in range(2)
    ]
    return pl.pallas_call(
        functools.partial(attend_back_kernel, min(tokens, (1 << 19) // tokens)),
        grid=(count,),
        in_specs=in_specs
        + [
            whole_spec(bias.shape),
            whole_spec(hot.shape),
            head_spec(tokens, 0),
            head_spec(part, first),
            head_spec(part, first),
            row_spec(tokens),
        ],
        out_specs=pl.BlockSpec((3, 1, HEAD_DIM, tokens), lambda head: (0, head, 0, 0)),
        out_shape=jax.ShapeDtypeStruct((3, count, HEAD_DIM, tokens), BF16),
        compiler_params=pltpu.CompilerParams(vmem_limit_bytes=24 << 20),
        cost_estimate=SMALL,
    )(own, other, own, other, own, other, bias, hot, out, grad_own, grad_other, lse)


def write_kernel(place, first, last, aliased, *refs):
    me = lax.axis_index("dp")
    sources = refs[: len(refs) - 3 - aliased]
    out_ref, wide, sems = refs[-3:]
    copies = []
    for group, source in enumerate(sources):
        for block in range(first, last):
            slot = group * (last - first) + block - first
            wide[slot] = source[block].astype(F32)
            copies.append(
                pltpu.make_async_copy(
                    wide.at[slot], place(out_ref, me, group, block), sems.at[slot]
                )
            )
            copies[-1].start()
    for copy in copies:
        copy.wait()


def write_out(groups, place, shape, onto=None, part=None):
    blocks, rows, columns = groups[0].shape
    first, last = (0, blocks) if part is None else part
    count = len(groups) * (last - first)
    anywhere = pl.BlockSpec(memory_space=pl.ANY)
    extra = [] if onto is None else [onto]
    return pl.pallas_call(
        functools.partial(write_kernel, place, first, last, len(extra)),
        in_specs=[pl.BlockSpec(memory_space=pltpu.VMEM)] * len(groups) + [anywhere] * len(extra),
        out_specs=anywhere,
        scratch_shapes=[
            pltpu.VMEM((count, rows, columns), F32),
            pltpu.SemaphoreType.DMA((count,)),
        ],
        out_shape=jax.ShapeDtypeStruct(shape, F32),
        input_output_aliases={} if onto is None else {len(groups): 0},
        compiler_params=pltpu.CompilerParams(vmem_limit_bytes=20 << 20),
        cost_estimate=SMALL,
    )(*groups, *extra)


def hidden_kernel(inputs_ref, weight_ref, active_ref, slope_ref):
    rows = inputs_ref.shape[0] // 4
    for start in range(0, 4 * rows, rows):
        part = slice(start, start + rows)
        active, slope = gelu_parts(dot(inputs_ref[part], weight_ref[...], 1, 0))
        active_ref[part] = active.astype(BF16)
        slope_ref[part] = slope.astype(BF16)


def hidden_units(inputs, weight):
    rows, width = inputs.shape
    units = weight.shape[1]
    block = units // 6
    out_block = pl.BlockSpec((rows, block), lambda i: (0, i))
    return pl.pallas_call(
        hidden_kernel,
        grid=(6,),
        in_specs=[
            pl.BlockSpec((rows, width), lambda i: (0, 0)),
            pl.BlockSpec((width, block), lambda i: (0, i)),
        ],
        out_specs=[out_block] * 2,
        out_shape=[jax.ShapeDtypeStruct((rows, units), BF16)] * 2,
        compiler_params=pltpu.CompilerParams(vmem_limit_bytes=20 << 20),
        cost_estimate=SMALL,
    )(inputs, weight)


def hidden_back_kernel(grad_ref, weight_ref, slope_ref, out_ref):
    rows = grad_ref.shape[0] // 4
    for start in range(0, 4 * rows, rows):
        part = slice(start, start + rows)
        grads = dot(grad_ref[part], weight_ref[...], 1, 1)
        out_ref[part] = (grads * slope_ref[part].astype(F32)).astype(BF16)


def hidden_back(grads, weight, slope):
    rows, width = grads.shape
    units = weight.shape[0]
    block = units // 6
    out_block = pl.BlockSpec((rows, block), lambda i: (0, i))
    return pl.pallas_call(
        hidden_back_kernel,
        grid=(6,),
        in_specs=[
            pl.BlockSpec((rows, width), lambda i: (0, 0)),
            pl.BlockSpec((block, width), lambda i: (i, 0)),
            out_block,
        ],
        out_specs=out_block,
        out_shape=jax.ShapeDtypeStruct((rows, units), BF16),
        compiler_params=pltpu.CompilerParams(vmem_limit_bytes=20 << 20),
        cost_estimate=SMALL,
    )(grads, weight, slope)


def gradient_kernel(left_is_blocked, half_ref, left_ref, right_ref, *refs):
    total = dot(left_ref[...], right_ref[...], 0, 0)
    if len(refs) == 2:
        total = total + refs[0][...].astype(F32)
    refs[-1][...] = total.astype(BF16)


def half_gradient(left, right, half, away, left_is_blocked):
    rows = left.shape[0]
    blocked = left if left_is_blocked else right
    whole = right if left_is_blocked else left
    units = blocked.shape[1] // 2
    block = units // 3
    half_spec = pl.BlockSpec((rows, block), lambda i, half_ref: (0, half_ref[0] * 3 + i))
    whole_block = pl.BlockSpec(whole.shape, lambda i, half_ref: (0, 0))
    if left_is_blocked:
        shape = (units, whole.shape[1])
        out_spec = pl.BlockSpec((block, shape[1]), lambda i, half_ref: (i, 0))
        in_specs = [half_spec, whole_block]
    else:
        shape = (whole.shape[1], units)
        out_spec = pl.BlockSpec((shape[0], block), lambda i, half_ref: (0, i))
        in_specs = [whole_block, half_spec]
    extra = [] if away is None else [away]
    return pl.pallas_call(
        functools.partial(gradient_kernel, left_is_blocked),
        grid_spec=pltpu.PrefetchScalarGridSpec(
            num_scalar_prefetch=1,
            grid=(3,),
            in_specs=in_specs + [out_spec] * len(extra),
            out_specs=out_spec,
        ),
        out_shape=jax.ShapeDtypeStruct(shape, BF16),
        compiler_params=pltpu.CompilerParams(vmem_limit_bytes=22 << 20),
        cost_estimate=SMALL,
    )(half.astype(jnp.int32)[None], left, right, *extra)


def down_gradient(active, grads, half, away=None):
    return half_gradient(active, grads, half, away, True)


def up_gradient(inputs, grads, half, away=None):
    return half_gradient(inputs, grads, half, away, False)


def rows_back_kernel(grad_ref, weight_ref, wide_ref, low_ref):
    total = dot(grad_ref[...], weight_ref[...], 1, 1)
    wide_ref[...] = total
    low_ref[...] = total.astype(BF16)


def rows_back(grads, weight, which):
    rows = grads.shape[0] // 2
    units = grads.shape[1]
    width = weight.shape[0]
    block = width // 3
    out_block = pl.BlockSpec((rows, block), lambda i: (0, i))
    return pl.pallas_call(
        rows_back_kernel,
        grid=(3,),
        in_specs=[
            pl.BlockSpec((rows, units), lambda i: (which, 0)),
            pl.BlockSpec((block, units), lambda i: (i, 0)),
        ],
        out_specs=[out_block] * 2,
        out_shape=[
            jax.ShapeDtypeStruct((rows, width), F32),
            jax.ShapeDtypeStruct((rows, width), BF16),
        ],
        compiler_params=pltpu.CompilerParams(vmem_limit_bytes=20 << 20),
        cost_estimate=SMALL,
    )(grads, weight)


def finish_kernel(
    half_steps,
    halfway_ref,
    own_ref,
    away_ref,
    branch_ref,
    two_ref,
    two_first_ref,
    two_last_ref,
    tokens_ref,
    mods_ref,
    result_ref,
    grad_ref,
):
    values = tokens_ref[...].astype(F32)
    two_away = jnp.where(
        pl.program_id(0) < half_steps, two_first_ref[...].astype(F32), two_last_ref[...].astype(F32)
    )
    two = two_ref[...] + two_away
    halfway = values + mods_ref[0, 2:3] * branch_ref[...]
    result_ref[...] = (halfway + mods_ref[0, 5:6] * two).astype(BF16)
    normed, inverse = normalize(values)
    grad_mod = own_ref[...] + away_ref[...].astype(F32)
    back = norm_back(grad_mod * (1.0 + mods_ref[0, 1:2]), normed, inverse)
    grad_ref[...] = (halfway_ref[...] + back).astype(BF16)


def finish(grad_halfway, own, away, branch, two, two_first, two_last, tokens, mods):
    rows, width = tokens.shape
    chunk = own.shape[0] // mods.shape[0]
    steps = rows // chunk
    half_steps = steps // 2
    row_block = pl.BlockSpec((chunk, width), lambda i: (i, 0))
    return pl.pallas_call(
        functools.partial(finish_kernel, half_steps),
        grid=(steps,),
        in_specs=[
            row_block,
            row_block,
            row_block,
            row_block,
            row_block,
            pl.BlockSpec((chunk, width), lambda i: (jnp.minimum(i, half_steps - 1), 0)),
            pl.BlockSpec((chunk, width), lambda i: (jnp.maximum(i - half_steps, 0), 0)),
            row_block,
            pl.BlockSpec((1, 6, width), lambda i: (i, 0, 0)),
        ],
        out_specs=[row_block, row_block],
        out_shape=[jax.ShapeDtypeStruct((rows, width), BF16)] * 2,
        compiler_params=pltpu.CompilerParams(vmem_limit_bytes=16 << 20),
        cost_estimate=SMALL,
    )(grad_halfway, own, away, branch, two, two_first, two_last, tokens, mods)


def heads_back_kernel(first_ref, second_ref, first_weight, second_weight, wide_ref, low_ref):
    total = dot(first_ref[...], first_weight[...], 0, 0)
    total = total + dot(second_ref[...], second_weight[...], 0, 0)
    wide_ref[...] = total
    low_ref[...] = total.astype(BF16)


def heads_back(first, second, first_weight, second_weight):
    rows = first.shape[1]
    width = first_weight.shape[1]
    block = width // 3
    out_block = pl.BlockSpec((rows, block), lambda i: (0, i))
    return pl.pallas_call(
        heads_back_kernel,
        grid=(3,),
        in_specs=[
            pl.BlockSpec(first.shape, lambda i: (0, 0)),
            pl.BlockSpec(second.shape, lambda i: (0, 0)),
            pl.BlockSpec((first_weight.shape[0], block), lambda i: (0, i)),
            pl.BlockSpec((second.shape[0], block), lambda i: (0, i)),
        ],
        out_specs=[out_block] * 2,
        out_shape=[
            jax.ShapeDtypeStruct((rows, width), F32),
            jax.ShapeDtypeStruct((rows, width), BF16),
        ],
        compiler_params=pltpu.CompilerParams(vmem_limit_bytes=22 << 20),
        cost_estimate=SMALL,
    )(first, second, first_weight, second_weight)


def condition_kernel(grad_ref, weight_ref, out_ref):
    out_ref[...] = dot(grad_ref[...], weight_ref[...], 1, 1).astype(BF16)


def condition_part(grads, weight):
    rows, depth = weight.shape
    block = rows // 3
    return pl.pallas_call(
        condition_kernel,
        grid=(3,),
        in_specs=[
            pl.BlockSpec((grads.shape[0], depth), lambda i: (0, 0)),
            pl.BlockSpec((block, depth), lambda i: (i, 0)),
        ],
        out_specs=pl.BlockSpec((grads.shape[0], block), lambda i: (0, i)),
        out_shape=jax.ShapeDtypeStruct((grads.shape[0], rows), BF16),
        compiler_params=pltpu.CompilerParams(vmem_limit_bytes=14 << 20),
        cost_estimate=SMALL,
    )(grads, weight)


def ada_kernel(act_ref, grad_ref, out_ref):
    out_ref[...] = dot(act_ref[...], grad_ref[...], 0, 0)


def ada_gradient(act, grads, columns):
    block = columns // 9
    return pl.pallas_call(
        ada_kernel,
        grid=(9,),
        in_specs=[
            pl.BlockSpec(act.shape, lambda i: (0, 0)),
            pl.BlockSpec((act.shape[0], block), lambda i: (0, i)),
        ],
        out_specs=pl.BlockSpec((act.shape[1], block), lambda i: (0, i)),
        out_shape=jax.ShapeDtypeStruct((act.shape[1], columns), F32),
        compiler_params=pltpu.CompilerParams(vmem_limit_bytes=14 << 20),
        cost_estimate=SMALL,
    )(act, grads)


def middle_kernel(own_steps, first_ref, heads_ref, weight_ref, own_ref, away_ref, mods_ref, *outs):
    branch_ref, inputs_ref, normed_ref = outs
    branch = first_ref[...] + dot(heads_ref[...], weight_ref[...], 0, 0)
    is_own = pl.program_id(0) < own_steps
    values = jnp.where(is_own, own_ref[...].astype(F32), away_ref[...].astype(F32))
    normed, _ = normalize(values + mods_ref[0, 2:3] * branch)
    branch_ref[...] = branch
    inputs_ref[...] = (normed * (1.0 + mods_ref[0, 4:5]) + mods_ref[0, 3:4]).astype(BF16)
    normed_ref[...] = normed.astype(BF16)


def middle(first, heads_away, weight, own, away, mods):
    rows, width = first.shape
    steps = mods.shape[0]
    chunk = rows // steps
    own_steps = own.shape[0] // chunk
    depth = heads_away.shape[0]
    row_block = pl.BlockSpec((chunk, width), lambda i: (i, 0))
    return pl.pallas_call(
        functools.partial(middle_kernel, own_steps),
        grid=(steps,),
        in_specs=[
            row_block,
            pl.BlockSpec((depth, chunk), lambda i: (0, (i + steps // 2) % steps)),
            pl.BlockSpec((depth, width), lambda i: (1, 0)),
            pl.BlockSpec((chunk, width), lambda i: (jnp.minimum(i, own_steps - 1), 0)),
            pl.BlockSpec((chunk, width), lambda i: (jnp.maximum(i - own_steps, 0), 0)),
            pl.BlockSpec((1, 6, width), lambda i: (i, 0, 0)),
        ],
        out_specs=[row_block] * 3,
        out_shape=[
            jax.ShapeDtypeStruct((rows, width), F32),
            jax.ShapeDtypeStruct((rows, width), BF16),
            jax.ShapeDtypeStruct((rows, width), BF16),
        ],
        compiler_params=pltpu.CompilerParams(vmem_limit_bytes=14 << 20),
        cost_estimate=SMALL,
    )(first, heads_away, weight, own, away, mods)


def middle_back_kernel(
    half_steps, own_ref, first_ref, second_ref, branch_ref, tokens_ref, cot_ref, mods_ref, *outs
):
    grad_ref, low_ref, sums_ref = outs
    arrived = jnp.where(
        pl.program_id(0) < half_steps, first_ref[...].astype(F32), second_ref[...].astype(F32)
    )
    branch = branch_ref[...]
    gate = mods_ref[0, 2:3]
    normed, inverse = normalize(tokens_ref[...].astype(F32) + gate * branch)
    grad_mod = own_ref[...] + arrived
    grad = cot_ref[...].astype(F32) + norm_back(
        grad_mod * (1.0 + mods_ref[0, 4:5]), normed, inverse
    )
    grad_ref[...] = grad
    low_ref[...] = (grad * gate).astype(BF16)
    sums_ref[0] = jnp.sum(grad * branch, axis=0, keepdims=True)


def middle_back(own, first, second, branch, tokens, cot, mods):
    rows, width = own.shape
    chunk = branch.shape[0] // mods.shape[0]
    steps = rows // chunk
    half_steps = steps // 2
    row_block = pl.BlockSpec((chunk, width), lambda i: (i, 0))
    return pl.pallas_call(
        functools.partial(middle_back_kernel, half_steps),
        grid=(steps,),
        in_specs=[
            row_block,
            pl.BlockSpec((chunk, width), lambda i: (jnp.minimum(i, half_steps - 1), 0)),
            pl.BlockSpec((chunk, width), lambda i: (jnp.maximum(i - half_steps, 0), 0)),
            row_block,
            row_block,
            row_block,
            pl.BlockSpec((1, 6, width), lambda i: (i, 0, 0)),
        ],
        out_specs=[row_block, row_block, pl.BlockSpec((1, 1, width), lambda i: (i, 0, 0))],
        out_shape=[
            jax.ShapeDtypeStruct((rows, width), F32),
            jax.ShapeDtypeStruct((rows, width), BF16),
            jax.ShapeDtypeStruct((steps, 1, width), F32),
        ],
        compiler_params=pltpu.CompilerParams(vmem_limit_bytes=14 << 20),
        cost_estimate=SMALL,
    )(own, first, second, branch, tokens, cot, mods)


def pair_body(
    tokens,
    segments,
    labels,
    timesteps,
    class_table,
    time_weight,
    ada_weight,
    qkv_weight,
    proj_weight,
    up_weight,
    down_weight,
    cotangent,
):
    position = lax.axis_index("tensor")
    rank = lax.axis_index("dp")
    dp_size = 16
    core, line, deep = rank % 2, rank // 2 % 2, rank // 4 % 2
    own_low = tokens[0]
    cot_low = cotangent[0]
    shard, width = own_low.shape
    pack = segments.shape[1]
    slot_count = labels.shape[1]
    class_count = class_table.shape[0]
    freq_width = time_weight.shape[0]
    local_width = qkv_weight.shape[2]
    heads = local_width // HEAD_DIM
    half_heads = heads // 2
    half_width = local_width // 2
    hidden_width = up_weight.shape[1]
    chunk = shard * SHORT // pack
    own_chunks = shard // chunk
    CORE, LINE, DEEP, FAR = 1, 2, 4, 8

    def fence(*values):
        return lax.optimization_barrier(values)

    def swap(x):
        return lax.ppermute(x, "tensor", [(0, 1), (1, 0)])

    def trade(x, bits):
        return lax.ppermute(x, "dp", [(i, i ^ bits) for i in range(dp_size)])

    def rows_of(x, index, count):
        size = x.shape[0] // count
        return lax.dynamic_slice_in_dim(x, index * size, size, 0)

    def columns_of(x, index, count):
        size = x.shape[1] // count
        return lax.dynamic_slice_in_dim(x, index * size, size, 1)

    def plus(a, b):
        return (a.astype(F32) + b.astype(F32)).astype(BF16)

    def halve(x, digit, bits):
        return plus(rows_of(x, digit, 2), trade(rows_of(x, 1 - digit, 2), bits))

    def digit(me, bits):
        return me // bits % 2

    def down_place(ref, me, group, block):
        index = (
            (digit(me, CORE) + group) % 2 * 4
            + (digit(me, LINE) + block // 2) % 2 * 2
            + (digit(me, DEEP) + block) % 2
        )
        return ref.at[index]

    def proj_place(ref, me, group, block):
        index = (digit(me, CORE) + group // 2) % 2 * 4 + (digit(me, LINE) + group % 2) % 2 * 2
        return ref.at[index + block - 3]

    def up_place(ref, me, group, block):
        index = (digit(me, LINE) + block // 2) % 2 * 2 + (digit(me, DEEP) + block) % 2
        column = (digit(me, CORE) + group) % 2 * (hidden_width // 2)
        return ref.at[index, :, pl.ds(pl.multiple_of(column, 128), hidden_width // 2)]

    def qkv_place(offset, bits):
        def place(ref, me, group, block):
            unit = (
                (digit(me, CORE) + group // 2) % 2 * 2 + (digit(me, bits) + group % 2) % 2
            ) * 3 + block
            return ref.at[unit // half_heads * heads + unit % half_heads + offset]

        return place

    def chunked(x):
        return x.reshape(x.shape[0] // chunk, chunk, x.shape[1])

    def flat(x):
        return x.reshape(x.shape[0] * chunk, x.shape[2])

    quarter = shard // 2
    tokens_away = swap(own_low)
    ids = jnp.stack([labels[0], timesteps[0]], axis=1)

    seg = segments[0]
    seg = jnp.where(position == 0, seg, jnp.roll(seg, shard))
    slots = jnp.arange(slot_count, dtype=jnp.int32)
    chunk_hot = (seg[::chunk][:, None] == slots[None, :]).astype(F32)
    mask_rows = -(-slot_count // 8) * 8
    same = jnp.arange(mask_rows, dtype=jnp.int32)[:, None] == seg[None, :]
    hot = same.astype(BF16)
    bias = jnp.where(same, 0.0, -1e30).astype(BF16)

    classes = jnp.arange(class_count, dtype=jnp.int32)

    def condition_of(ids):
        label_hot = (ids[:, 0][:, None] == classes[None, :]).astype(F32)
        feats = features(ids[:, 1].astype(F32), freq_width)
        values = dot(label_hot, class_table, 1, 0, HIGH) + dot(feats, time_weight, 1, 0, HIGH)
        return label_hot, feats, values

    def hop(y, bits):
        return jnp.concatenate([y, trade(y, bits)], axis=0)

    condition = condition_of(ids)[2]
    pad = jnp.zeros((slot_count, 124), jnp.int32)
    digits = jnp.concatenate([ids // 32, ids % 32, pad], axis=1).astype(BF16)
    act_low = jax.nn.silu(condition).astype(BF16)
    weight_t = qkv_weight.transpose(1, 2, 0).reshape(3 * local_width, width)
    weight_parts = weight_t.reshape(3, 2, half_width, width)
    weight_a = weight_parts[:, 0].reshape(3 * half_width, width)
    weight_b = weight_parts[:, 1].reshape(3 * half_width, width)
    mod_part, tokens_away, proj_half, weight_a, weight_b = fence(
        dot(act_low, ada_weight, 1, 0),
        tokens_away,
        rows_of(proj_weight, core, 2),
        weight_a,
        weight_b,
    )
    mod_away, tokens_away = fence(swap(mod_part), tokens_away)
    modulation = jnp.where(
        position == 0,
        jnp.concatenate([mod_part, mod_away], axis=1),
        jnp.concatenate([mod_away, mod_part], axis=1),
    )
    proj_half = swap(proj_half)
    per_chunk = dot(chunk_hot, modulation, 1, 0, HIGH)
    mods_own = [m[:, None, :] for m in jnp.split(per_chunk[:own_chunks], 6, axis=1)]
    mods_other = [m[:, None, :] for m in jnp.split(per_chunk[own_chunks:], 6, axis=1)]


    def enter(low, mods):
        values = chunked(low.astype(F32))
        normed, inverse = normalize(values)
        inputs = flat((normed * (1.0 + mods[1]) + mods[0]).astype(BF16))
        return values, normed, inverse, inputs

    def project(inputs):
        return dot(weight_t, inputs, 1, 1).astype(BF16).reshape(3 * heads, HEAD_DIM, shard)

    tokens_own, normed_one, inverse_one, inputs_one_own = enter(own_low, mods_own)
    qkv_own = project(inputs_one_own)
    tokens_other, normed_one_other, _, inputs_one_other = enter(tokens_away, mods_other)
    qkv_other = project(inputs_one_other)
    out_a, lse_a = attend(qkv_own, qkv_other, bias, hot, 0, half_heads)
    chunk_mods = per_chunk.reshape(pack // chunk, 6, width)
    out_a, qkv_own, chunk_mods = fence(out_a, qkv_own, chunk_mods)
    away_a = swap(out_a.reshape(half_width, pack))
    out_b, lse_b = attend(qkv_own, qkv_other, bias, hot, half_heads, half_heads)
    out_b, proj_half, away_a = fence(out_b, proj_half, away_a)
    away_b = swap(out_b.reshape(half_width, pack))
    proj_rest = trade(proj_half, CORE)
    proj_other = jnp.where(
        core == 0,
        jnp.concatenate([proj_half, proj_rest], axis=0),
        jnp.concatenate([proj_rest, proj_half], axis=0),
    )
    out_flat = jnp.concatenate([out_a, out_b], axis=0).reshape(local_width, pack)
    own_part, other_part = slice(0, shard), slice(shard, pack)

    def reordered(away):
        return jnp.concatenate([away[:, other_part], away[:, own_part]], axis=1)

    away_a, proj_other = fence(away_a, proj_other)
    first, _ = heads_back(out_flat, reordered(away_a), proj_weight, proj_other)
    away_b, cot_next, first = fence(away_b, cot_low, first)
    cot_away = swap(cot_next)
    branch_one, inputs_two, normed_two = middle(
        first, away_b, proj_other, own_low, tokens_away, chunk_mods
    )

    active, slope = hidden_units(inputs_two, up_weight)
    active, slope, cot_away = fence(active, slope, cot_away)
    grad_branch_two = jnp.concatenate(
        [
            flat((chunked(cot_low.astype(F32)) * mods_own[5]).astype(BF16)),
            flat((chunked(cot_away.astype(F32)) * mods_other[5]).astype(BF16)),
        ],
        axis=0,
    )

    down_away = trade(down_gradient(active, grad_branch_two, 1 - core), CORE)
    grad_hidden = hidden_back(grad_branch_two, down_weight, slope)
    down_sum = down_gradient(active, grad_branch_two, core, down_away)
    down_sum, grad_hidden = fence(down_sum, grad_hidden)
    down_x = trade(rows_of(down_sum, 1 - line, 2), LINE)
    mod_two_other, mod_two_away = rows_back(grad_hidden, up_weight, 1)
    mod_two_away, grad_hidden = fence(mod_two_away, grad_hidden)

    arrived_a = swap(mod_two_away[:quarter])
    up_away = trade(up_gradient(inputs_two, grad_hidden, 1 - core), CORE)
    mod_two, _ = rows_back(grad_hidden, up_weight, 0)
    arrived_a, up_away, mod_two, mod_two_next, grad_hidden, active = fence(
        arrived_a, up_away, mod_two, mod_two_away[quarter:], grad_hidden, active
    )
    arrived_b = swap(mod_two_next)
    up_sum = up_gradient(inputs_two, grad_hidden, core, up_away)
    up_x = trade(rows_of(up_sum, 1 - line, 2), LINE)
    branch_two_away = dot(active[other_part], down_weight, 1, 0)
    branch_two = dot(active[own_part], down_weight, 1, 0)
    arrived_b, mod_two, branch_two_away, branch_two, down_x = fence(
        arrived_b, mod_two, branch_two_away, branch_two, down_x
    )

    down_sum = plus(rows_of(down_sum, line, 2), down_x)
    down_z = trade(rows_of(down_sum, 1 - deep, 2), DEEP)
    grad_halfway, grad_branch_one, gate_one_sums = middle_back(
        mod_two, arrived_a, arrived_b, branch_one, own_low, cot_low, chunk_mods
    )
    grad_att_away = dot(proj_other, grad_branch_one, 1, 1).astype(BF16)
    grad_att_away, grad_branch_one = fence(grad_att_away, grad_branch_one)

    grad_att_other = swap(grad_att_away)
    grad_att_own = dot(proj_weight, grad_branch_one, 1, 1).astype(BF16)
    def chunk_sums(own, other):
        return jnp.concatenate([jnp.sum(own, axis=1), jnp.sum(other, axis=1)], axis=0)

    normed_two = chunked(normed_two.astype(F32))
    late_terms = jnp.concatenate(
        [
            jnp.concatenate([gate_one_sums[:, 0], jnp.zeros_like(gate_one_sums[:, 0])], axis=0),
            chunk_sums(chunked(mod_two), chunked(mod_two_other)),
            chunk_sums(
                chunked(mod_two) * normed_two[:own_chunks],
                chunked(mod_two_other) * normed_two[own_chunks:],
            ),
            chunk_sums(
                chunked(branch_two) * chunked(cot_low.astype(F32)),
                chunked(branch_two_away) * chunked(cot_away.astype(F32)),
            ),
        ],
        axis=1,
    )
    inputs_one = jnp.concatenate([inputs_one_own, inputs_one_other], axis=0)
    grad_att_other, grad_att_own, down_z, branch_one_next, inputs_one, late_terms = fence(
        grad_att_other, grad_att_own, down_z, grad_branch_one, inputs_one, late_terms
    )
    down_sum = plus(rows_of(down_sum, deep, 2), down_z)
    down_block = down_sum.shape[0] // 2
    down_far_a = trade(down_sum[:down_block], FAR)

    def back(out, lse, first):
        return attend_back(
            qkv_own,
            qkv_other,
            bias,
            hot,
            out,
            grad_att_own.reshape(heads, HEAD_DIM, shard),
            grad_att_other.reshape(heads, HEAD_DIM, shard),
            lse,
            first,
            half_heads,
        ).reshape(3 * half_width, pack)

    def qkv_half(grad):
        return lambda half: dot(rows_of(grad, half, 2), inputs_one, 1, 0)

    grads_one_other = swap(branch_one_next)
    grad_qkv_a = back(out_a, lse_a, 0)
    grad_qkv_a, up_x, down_far_a, down_next = fence(
        grad_qkv_a, up_x, down_far_a, down_sum[down_block:]
    )
    down_far_b = trade(down_next, FAR)
    up_sum = plus(rows_of(up_sum, line, 2), up_x)
    up_z = trade(rows_of(up_sum, 1 - deep, 2), DEEP)
    qkv_make = qkv_half(grad_qkv_a)
    qkv_a_away = trade(qkv_make(1 - core).astype(BF16), CORE)
    qkv_a = plus(qkv_make(core), qkv_a_away)
    qkv_a, grad_att_own = fence(qkv_a, grad_att_own)
    qkv_a_x = trade(rows_of(qkv_a, 1 - line, 2), LINE)
    grad_qkv_b = back(out_b, lse_b, half_heads)
    grad_qkv_b, qkv_a_x, up_z, down_far_b, grads_one_other = fence(
        grad_qkv_b, qkv_a_x, up_z, down_far_b, grads_one_other
    )
    qkv_a = plus(rows_of(qkv_a, line, 2), qkv_a_x)
    up_sum = plus(rows_of(up_sum, deep, 2), up_z)
    down_sum = plus(down_sum, jnp.concatenate([down_far_a, down_far_b], axis=0))
    down_z = trade(down_sum, DEEP)
    down_x = trade(down_sum, LINE)
    block = up_sum.shape[0] // 2
    up_far_a = trade(up_sum[:block], FAR)
    mod_one = dot(grad_qkv_a, weight_a, 0, 0) + dot(grad_qkv_b, weight_b, 0, 0)
    mod_one_own, mod_one_away = chunked(mod_one[own_part]), chunked(mod_one[other_part])
    chunk_terms = jnp.concatenate(
        [
            chunk_sums(mod_one_own, mod_one_away),
            chunk_sums(mod_one_own * normed_one, mod_one_away * normed_one_other),
            late_terms,
        ],
        axis=1,
    )
    slot_terms = dot(chunk_hot, chunk_terms, 0, 0, HIGH).astype(BF16)
    half = slot_terms.shape[1] // 2
    low, high = slot_terms[:, :half], slot_terms[:, half:]
    keep = jnp.where(position == 0, low, high)
    away = jnp.where(position == 0, high, low)
    (
        away,
        keep,
        mod_one_next,
        down_z,
        down_x,
        up_far_a,
        grad_qkv_b,
        up_next,
        qkv_a,
    ) = fence(
        away,
        keep,
        flat(mod_one_away).astype(BF16),
        down_z,
        down_x,
        up_far_a,
        grad_qkv_b,
        up_sum[block:],
        qkv_a,
    )

    gathered = jnp.concatenate([plus(keep, swap(away)), digits], axis=1)[None]
    down_zx = trade(down_z, LINE)
    up_far_b = trade(up_next, FAR)
    qkv_a_z = trade(rows_of(qkv_a, 1 - deep, 2), DEEP)
    qkv_make_b = qkv_half(grad_qkv_b)

    def proj_half_of(half):
        rows = rows_of(out_flat, half, 2)
        return dot(rows[:, own_part], grad_branch_one, 1, 0) + dot(
            rows[:, other_part], grads_one_other, 1, 0
        )

    def packed(qkv, proj, index):
        return jnp.concatenate([rows_of(qkv, index, 2), rows_of(proj, index, 2)], axis=0)

    def unpacked(both):
        cut = both.shape[0] * 3 // 5
        return both[:cut], both[cut:]

    def in_order(digit, own, other):
        return jnp.where(
            digit == 0,
            jnp.concatenate([own, other], axis=0),
            jnp.concatenate([other, own], axis=0),
        )

    rest = trade(
        jnp.concatenate(
            [qkv_make_b(1 - core).astype(BF16), proj_half_of(1 - core).astype(BF16)], axis=0
        ),
        CORE,
    )
    qkv_rows = 3 * half_width // 2
    qkv_b = plus(qkv_make_b(core), rest[:qkv_rows])
    proj_sum = plus(proj_half_of(core), rest[qkv_rows:])
    both_next = packed(qkv_b, proj_sum, 1 - line)
    both = packed(qkv_b, proj_sum, line)
    gathered, up_far_b, down_zx, qkv_a_z, both_next, both, mod_one_next = fence(
        gathered, up_far_b, down_zx, qkv_a_z, both_next, both, mod_one_next
    )

    up_low = plus(up_sum[:block], up_far_a)
    up_high = plus(up_next, up_far_b)
    up_sum = jnp.concatenate([up_low, up_high], axis=0)
    qkv_a = plus(rows_of(qkv_a, deep, 2), qkv_a_z)
    up_sum, qkv_a, both_next, gathered, mod_one_next = fence(
        up_sum, qkv_a, both_next, gathered, mod_one_next
    )
    gathered = hop(gathered, LINE)
    eighth = quarter // 2
    mod_one_other = swap(mod_one_next[: shard - eighth])
    both_x = trade(both_next, LINE)
    up_z = trade(up_sum, DEEP)
    qkv_a_far = trade(qkv_a, FAR)
    (
        gathered,
        both_x,
        up_z,
        qkv_a_far,
        mod_one_other,
        both,
        down_sum,
        down_z,
        down_x,
        down_zx,
    ) = fence(
        gathered,
        both_x,
        up_z,
        qkv_a_far,
        mod_one_other,
        both,
        down_sum,
        down_z,
        down_x,
        down_zx,
    )
    both = plus(both, both_x)
    both_next = packed(*unpacked(both), 1 - deep)
    qkv_a = plus(qkv_a, qkv_a_far)
    two_low = branch_two_away.astype(BF16)
    both_next, qkv_a, gathered, up_sum, both, mixed = fence(
        both_next,
        qkv_a,
        gathered,
        up_sum,
        both,
        jnp.concatenate([mod_one_next[shard - eighth :], two_low[:eighth]], axis=0),
    )
    mixed = swap(mixed)
    gathered = hop(gathered, FAR)
    up_x = trade(up_sum, LINE)
    down_blocks = jnp.stack([down_sum, down_z, down_x, down_zx])
    both_z = trade(both_next, DEEP)
    qkv_a_z = trade(qkv_a, DEEP)
    both = packed(*unpacked(both), deep)
    gathered, up_x, both_z, qkv_a_z, both, down_blocks, mixed, two_next = fence(
        gathered, up_x, both_z, qkv_a_z, both, down_blocks, mixed, two_low[eighth:]
    )
    both = plus(both, both_z)
    qkv_a = in_order(deep, qkv_a, qkv_a_z).reshape(3, HEAD_DIM, width)
    both, qkv_a, gathered, up_z, down_blocks, two_next = fence(
        both, qkv_a, gathered, up_z, down_blocks, two_next
    )
    two_last = swap(two_next)
    grad_down = write_out(
        [down_blocks, trade(down_blocks, CORE)], down_place, (8, hidden_width // 8, width)
    )
    gathered = hop(gathered, DEEP)
    up_zx = trade(up_z, LINE)
    both_far = trade(both, FAR)
    up_zx, both_far, gathered, grad_down, two_last = fence(
        up_zx, both_far, gathered, grad_down, two_last
    )
    both = plus(both, both_far)
    both, gathered, qkv_a = fence(both, gathered, qkv_a)
    up_blocks = jnp.stack([up_sum, up_z, up_x, up_zx])
    both_z = trade(both, DEEP)
    qkv_a_x = trade(qkv_a, LINE)
    up_blocks_c = trade(up_blocks, CORE)
    grad_mod_all = hop(gathered, CORE).reshape(dp_size * slot_count, half + 128)
    cond_part = condition_part(grad_mod_all, ada_weight)
    mod_one_other = jnp.concatenate([mod_one_other, mixed[:eighth]], axis=0)
    two_first = jnp.concatenate([mixed[eighth:], two_last[:eighth]], axis=0)
    result, grad_input = finish(
        grad_halfway,
        mod_one,
        mod_one_other,
        branch_one,
        branch_two,
        two_first,
        two_last[eighth:],
        own_low,
        chunk_mods,
    )
    both_z, cond_part, grad_mod_all, up_blocks_c, qkv_a_x, result = fence(
        both_z, cond_part, grad_mod_all, up_blocks_c, qkv_a_x, result
    )
    both = jnp.concatenate(
        [in_order(deep, a, b) for a, b in zip(unpacked(both), unpacked(both_z), strict=True)],
        axis=0,
    ).reshape(5, HEAD_DIM, width)
    both_x = trade(both, LINE)
    both_c = trade(both, CORE)
    grad_act = cond_part.astype(F32) + swap(cond_part).astype(F32)
    qkv_a_c = trade(qkv_a, CORE)
    qkv_a_xc = trade(qkv_a_x, CORE)
    grad_up = write_out([up_blocks, up_blocks_c], up_place, (4, width // 4, hidden_width))
    ids_all = grad_mod_all[:, half : half + 4].astype(jnp.int32)
    label_hot, features_all, condition_all = condition_of(ids_all[:, :2] * 32 + ids_all[:, 2:])
    act_all = jax.nn.silu(condition_all).astype(BF16)
    grad_ada = ada_gradient(act_all, grad_mod_all, ada_weight.shape[1])
    both_x, both_c, grad_up, grad_act, grad_ada, qkv_a_c, qkv_a_xc = fence(
        both_x, both_c, grad_up, grad_act, grad_ada, qkv_a_c, qkv_a_xc
    )
    both_xc = trade(both_x, CORE)
    qkv_shape = (3 * heads, HEAD_DIM, width)
    grad_qkv = write_out([qkv_a, qkv_a_x, qkv_a_c, qkv_a_xc], qkv_place(0, LINE), qkv_shape)

    grad_condition = jax.vjp(jax.nn.silu, condition_all)[1](grad_act)[0]
    grad_class = dot(label_hot.astype(BF16), grad_condition.astype(BF16), 0, 0)
    grad_time = dot(features_all, grad_condition, 0, 0, HIGH)
    groups = [both, both_x, both_c, both_xc]
    grad_qkv = write_out(groups, qkv_place(half_heads, LINE), qkv_shape, grad_qkv, (0, 3))
    grad_proj = write_out(groups, proj_place, (8, HEAD_DIM, width), None, (3, 5))
    return (
        result[None],
        grad_input[None],
        grad_class,
        grad_time,
        grad_ada,
        grad_qkv.reshape(3, local_width, width).transpose(2, 0, 1),
        grad_proj.reshape(local_width, width),
        grad_up.reshape(width, hidden_width),
        grad_down.reshape(hidden_width, width),
    )


def any_body(
    tokens,
    segments,
    labels,
    timesteps,
    class_table,
    time_weight,
    ada_weight,
    qkv_weight,
    proj_weight,
    up_weight,
    down_weight,
    cotangent,
):
    own_tokens = tokens[0].astype(jnp.float32)
    shard_rows = own_tokens.shape[0]
    model_width = own_tokens.shape[1]
    seg_all = segments[0]
    pack_rows = seg_all.shape[0]
    slot_count = labels.shape[1]
    class_count = class_table.shape[0]
    freq_width = time_weight.shape[0]
    local_width = qkv_weight.shape[2]
    head_count = local_width // HEAD_DIM
    scale_factor = 1.0 / math.sqrt(HEAD_DIM)
    position = lax.axis_index("tensor")
    seg_own = lax.dynamic_slice_in_dim(seg_all, position * shard_rows, shard_rows)
    own_hot = (seg_own[:, None] == jnp.arange(slot_count, dtype=jnp.int32)[None, :]).astype(
        jnp.float32
    )
    label_hot = (labels[0][:, None] == jnp.arange(class_count, dtype=jnp.int32)[None, :]).astype(
        jnp.float32
    )
    step_feats = features(timesteps[0].astype(jnp.float32), freq_width)
    condition = jnp.dot(label_hot, class_table, precision=HIGH) + jnp.dot(
        step_feats, time_weight, precision=HIGH
    )
    act_low = jax.nn.silu(condition).astype(jnp.bfloat16)
    mod_part = jnp.dot(act_low, ada_weight, preferred_element_type=jnp.float32)
    modulation = lax.all_gather(mod_part, "tensor", axis=1, tiled=True)
    per_token = jnp.dot(own_hot, modulation, precision=HIGH)
    shift_one, scale_one, gate_one, shift_two, scale_two, gate_two = jnp.split(per_token, 6, axis=1)
    normed_one, inverse_one = normalize(own_tokens)
    modulated_one = (normed_one * (1.0 + scale_one) + shift_one).astype(jnp.bfloat16)
    inputs_one = lax.all_gather(modulated_one, "tensor", axis=0, tiled=True)
    qkv_flat = qkv_weight.reshape(model_width, 3 * local_width)
    qkv = jnp.dot(inputs_one, qkv_flat, preferred_element_type=jnp.float32).astype(jnp.bfloat16)
    qkv_heads = qkv.reshape(pack_rows, 3, head_count, HEAD_DIM).transpose(1, 2, 0, 3)
    queries = qkv_heads[0]
    keys = qkv_heads[1]
    values = qkv_heads[2]
    block = min(512, pack_rows)
    block_count = pack_rows // block
    starts = jnp.arange(block_count, dtype=jnp.int32) * block

    def scores_of(start):
        query_block = lax.dynamic_slice_in_dim(queries, start, block, 1)
        seg_block = lax.dynamic_slice_in_dim(seg_all, start, block)
        raw = (
            jnp.einsum("hqd,hkd->hqk", query_block, keys, preferred_element_type=jnp.float32)
            * scale_factor
        )
        same = (seg_block[:, None] == seg_all[None, :])[None]
        return (jnp.where(same, raw, -1e30), query_block)

    def attend(start):
        scores = scores_of(start)[0]
        top = jnp.max(scores, axis=-1, keepdims=True)
        exps = jnp.exp(scores - top)
        total = jnp.sum(exps, axis=-1, keepdims=True)
        weights = (exps / total).astype(jnp.bfloat16)
        out_block = jnp.einsum("hqk,hkd->hqd", weights, values, preferred_element_type=jnp.float32)
        return (out_block, (top + jnp.log(total))[..., 0])

    out_blocks, lse_blocks = lax.map(attend, starts)
    attended = out_blocks.transpose(0, 2, 1, 3).reshape(pack_rows, local_width).astype(jnp.bfloat16)
    lse_all = lse_blocks.transpose(1, 0, 2).reshape(head_count, pack_rows)
    branch_one = lax.psum_scatter(
        jnp.dot(attended, proj_weight, preferred_element_type=jnp.float32),
        "tensor",
        scatter_dimension=0,
        tiled=True,
    )
    halfway = own_tokens + gate_one * branch_one
    normed_two, inverse_two = normalize(halfway)
    modulated_two = (normed_two * (1.0 + scale_two) + shift_two).astype(jnp.bfloat16)
    inputs_two = lax.all_gather(modulated_two, "tensor", axis=0, tiled=True)
    hidden = jnp.dot(inputs_two, up_weight, preferred_element_type=jnp.float32)
    active = jax.nn.gelu(hidden, approximate=True).astype(jnp.bfloat16)
    branch_two = lax.psum_scatter(
        jnp.dot(active, down_weight, preferred_element_type=jnp.float32).astype(jnp.bfloat16),
        "tensor",
        scatter_dimension=0,
        tiled=True,
    ).astype(jnp.float32)
    result = halfway + gate_two * branch_two
    grad_out = cotangent[0].astype(jnp.float32)
    grad_gate_two = grad_out * branch_two
    grad_branch_two = (grad_out * gate_two).astype(jnp.bfloat16)
    grads_two = lax.all_gather(grad_branch_two, "tensor", axis=0, tiled=True)
    grad_down = contract_rows(active, grads_two)
    grad_active = times_transposed(grads_two, down_weight)
    gelu_back = jax.vjp(lambda inner: jax.nn.gelu(inner, approximate=True), hidden)[1]
    grad_hidden = gelu_back(grad_active)[0].astype(jnp.bfloat16)
    grad_up = contract_rows(inputs_two, grad_hidden)
    grad_mod_two = lax.psum_scatter(
        times_transposed(grad_hidden, up_weight), "tensor", scatter_dimension=0, tiled=True
    )
    grad_halfway = grad_out + norm_back(grad_mod_two * (1.0 + scale_two), normed_two, inverse_two)
    grad_gate_one = grad_halfway * branch_one
    grad_branch_one = (grad_halfway * gate_one).astype(jnp.bfloat16)
    grads_one = lax.all_gather(grad_branch_one, "tensor", axis=0, tiled=True)
    grad_proj = contract_rows(attended, grads_one)
    grad_attended = times_transposed(grads_one, proj_weight).astype(jnp.bfloat16)
    grad_heads = grad_attended.reshape(pack_rows, head_count, HEAD_DIM).transpose(1, 0, 2)

    def attend_back(carry, start):
        grad_keys, grad_values = carry
        scores, query_block = scores_of(start)
        lse_block = lax.dynamic_slice_in_dim(lse_all, start, block, 1)
        probs = jnp.exp(scores - lse_block[..., None])
        grad_block = lax.dynamic_slice_in_dim(grad_heads, start, block, 1)
        grad_probs = jnp.einsum(
            "hqd,hkd->hqk", grad_block, values, preferred_element_type=jnp.float32
        )
        grad_scores = (
            probs * (grad_probs - jnp.sum(probs * grad_probs, axis=-1, keepdims=True))
        ).astype(jnp.bfloat16)
        grad_query = (
            jnp.einsum("hqk,hkd->hqd", grad_scores, keys, preferred_element_type=jnp.float32)
            * scale_factor
        )
        grad_keys = (
            grad_keys
            + jnp.einsum(
                "hqk,hqd->hkd", grad_scores, query_block, preferred_element_type=jnp.float32
            )
            * scale_factor
        )
        grad_values = grad_values + jnp.einsum(
            "hqk,hqd->hkd",
            probs.astype(jnp.bfloat16),
            grad_block,
            preferred_element_type=jnp.float32,
        )
        return ((grad_keys, grad_values), grad_query)

    empty = jnp.zeros((head_count, pack_rows, HEAD_DIM), jnp.float32)
    key_grads, grad_queries = lax.scan(attend_back, (empty, empty), starts)
    query_grads = grad_queries.transpose(1, 0, 2, 3).reshape(head_count, pack_rows, HEAD_DIM)
    grad_stack = jnp.stack([query_grads, key_grads[0], key_grads[1]], axis=0)
    grad_qkv = (
        grad_stack.transpose(2, 0, 1, 3).reshape(pack_rows, 3 * local_width).astype(jnp.bfloat16)
    )
    grad_qkv_weight = contract_rows(inputs_one, grad_qkv).reshape(model_width, 3, local_width)
    grad_mod_one = lax.psum_scatter(
        times_transposed(grad_qkv, qkv_flat).astype(jnp.bfloat16),
        "tensor",
        scatter_dimension=0,
        tiled=True,
    ).astype(jnp.float32)
    grad_input = grad_halfway + norm_back(grad_mod_one * (1.0 + scale_one), normed_one, inverse_one)
    grad_per_token = jnp.concatenate(
        [
            grad_mod_one,
            grad_mod_one * normed_one,
            grad_gate_one,
            grad_mod_two,
            grad_mod_two * normed_two,
            grad_gate_two,
        ],
        axis=1,
    )
    slot_terms = contract_exact(own_hot, grad_per_token)
    grad_modulation = lax.psum_scatter(
        slot_terms.astype(jnp.bfloat16), "tensor", scatter_dimension=1, tiled=True
    )
    grad_ada = contract_rows(act_low, grad_modulation)
    cond_part = times_transposed(grad_modulation, ada_weight)
    grad_activated = lax.psum(cond_part.astype(jnp.bfloat16), "tensor").astype(jnp.float32)
    grad_condition = jax.vjp(jax.nn.silu, condition)[1](grad_activated)[0]
    grad_class = contract_exact(label_hot, grad_condition)
    grad_time = contract_exact(step_feats, grad_condition)
    summed = (
        lax.psum(grad_class.astype(jnp.bfloat16), "dp").astype(jnp.float32),
        lax.psum(grad_time.astype(jnp.bfloat16), "dp").astype(jnp.float32),
        lax.psum(grad_ada.astype(jnp.bfloat16), "dp").astype(jnp.float32),
        lax.psum(grad_qkv_weight.astype(jnp.bfloat16), "dp").astype(jnp.float32),
        lax.psum(grad_proj.astype(jnp.bfloat16), "dp").astype(jnp.float32),
        lax.psum(grad_up.astype(jnp.bfloat16), "dp").astype(jnp.float32),
        lax.psum(grad_down.astype(jnp.bfloat16), "dp").astype(jnp.float32),
    )
    grad_class, grad_time, grad_ada, grad_qkv_weight, grad_proj, grad_up, grad_down = summed
    return (
        result.astype(jnp.bfloat16)[None],
        grad_input.astype(jnp.bfloat16)[None],
        grad_class,
        grad_time,
        grad_ada,
        grad_qkv_weight,
        grad_proj,
        grad_up,
        grad_down,
    )


def solution(mesh):
    pairs = mesh.shape["dp"] == 16 and mesh.shape["tensor"] == 2
    return jax.shard_map(
        pair_body if pairs else any_body,
        mesh=mesh,
        in_specs=(
            P("dp", "tensor", None),
            P("dp", None),
            P("dp", None),
            P("dp", None),
            P(),
            P(),
            P(None, "tensor"),
            P(None, None, "tensor"),
            P("tensor", None),
            P(None, "tensor"),
            P("tensor", None),
            P("dp", "tensor", None),
        ),
        out_specs=(
            P("dp", "tensor", None),
            P("dp", "tensor", None),
            P(),
            P(),
            P(None, "tensor"),
            P(None, None, "tensor"),
            P("tensor", None),
            P(None, "tensor"),
            P("tensor", None),
        ),
        check_vma=False,
    )
```

```python
import functools
import math

import jax
import jax.numpy as jnp
from jax import lax
from jax.experimental import pallas as pl
from jax.experimental.pallas import tpu as pltpu
from jax.sharding import PartitionSpec as P

HEAD_DIM = 72
SHORT = 256
HIGH = lax.Precision.HIGHEST
F32 = jnp.float32
BF16 = jnp.bfloat16
SCALE = 1.0 / math.sqrt(HEAD_DIM)
SCALE_LOG2 = SCALE * math.log2(math.e)


def dot(left, right, left_dim, right_dim, precision=None):
    return lax.dot_general(
        left,
        right,
        (((left_dim,), (right_dim,)), ((), ())),
        precision=precision,
        preferred_element_type=F32,
    )


def features(steps_f, width_total):
    half = width_total // 2
    freqs = jnp.exp(-math.log(10000.0) * jnp.arange(half, dtype=F32) / half)
    angles = steps_f[:, None] * freqs[None, :]
    return jnp.concatenate([jnp.cos(angles), jnp.sin(angles)], axis=1)


def contract_rows(left, right):
    return dot(left, right, 0, 0)


def contract_exact(left, right):
    return dot(left, right, 0, 0, HIGH)


def times_transposed(left, right):
    return dot(left, right, 1, 1)


def normalize(values):
    average = jnp.mean(values, axis=-1, keepdims=True)
    centred = values - average
    inverse = lax.rsqrt(jnp.mean(centred * centred, axis=-1, keepdims=True) + 1e-06)
    return centred * inverse, inverse


def norm_back(grad_normed, normed, inverse):
    first = jnp.mean(grad_normed, axis=-1, keepdims=True)
    second = jnp.mean(grad_normed * normed, axis=-1, keepdims=True)
    return inverse * (grad_normed - first - normed * second)


def gelu_parts(x):
    root = math.sqrt(2.0 / math.pi)
    square = x * x
    bent = jnp.tanh(root * x * (1.0 + 0.044715 * square))
    half = 0.5 * (1.0 + bent)
    slope = half + 0.5 * x * (1.0 - bent * bent) * root * (1.0 + 3 * 0.044715 * square)
    return x * half, slope


def joined(own, other):
    return jnp.concatenate([own[0], other[0]], axis=1)


def attend_kernel(block, q0, q1, k0, k1, v0, v1, bias_ref, hot_ref, o_ref, lse_ref):
    tokens = o_ref.shape[2]
    query = jnp.concatenate([joined(q0, q1), bias_ref[...]], axis=0)
    key = jnp.concatenate([joined(k0, k1), hot_ref[...]], axis=0).T
    value = joined(v0, v1)
    for start in range(0, tokens, block):
        part = slice(start, start + block)
        scores = dot(key, query[:, part], 1, 0)
        top = jnp.max(scores, axis=0, keepdims=True) * SCALE_LOG2
        exps = jnp.exp2(scores * SCALE_LOG2 - top)
        total = jnp.sum(exps, axis=0, keepdims=True)
        out = dot(value, exps.astype(BF16), 1, 0)
        o_ref[0, :, part] = (out / total).astype(BF16)
        lse_ref[0, :, part] = top + jnp.log2(total)


def attend_back_kernel(
    block, q0, q1, k0, k1, v0, v1, bias_ref, hot_ref, o_ref, do0, do1, lse_ref, grad_ref
):
    tokens = o_ref.shape[2]
    query_all, key_all = joined(q0, q1), joined(k0, k1)
    query = jnp.concatenate([query_all, bias_ref[...]], axis=0)
    key = jnp.concatenate([key_all, hot_ref[...]], axis=0).T
    value = joined(v0, v1).T
    query_rows = query_all.T
    grad_out = joined(do0, do1)
    grad_rows = grad_out.T
    delta = jnp.sum(grad_out.astype(F32) * o_ref[0].astype(F32), axis=0, keepdims=True)
    lse = lse_ref[0]
    grad_key = grad_value = None
    for start in range(0, tokens, block):
        part = slice(start, start + block)
        scores = dot(key, query[:, part], 1, 0)
        probs = jnp.exp2(scores * SCALE_LOG2 - lse[:, part])
        grad_probs = dot(value, grad_out[:, part], 1, 0)
        grad_scores = (probs * (grad_probs - delta[:, part])).astype(BF16)
        value_term = dot(probs.astype(BF16), grad_rows[part], 1, 0)
        key_term = dot(grad_scores, query_rows[part], 1, 0)
        grad_value = value_term if grad_value is None else grad_value + value_term
        grad_key = key_term if grad_key is None else grad_key + key_term
        grad_ref[0, 0, :, part] = (dot(key_all, grad_scores, 1, 0) * SCALE).astype(BF16)
    grad_ref[1, 0] = (grad_key * SCALE).astype(BF16).T
    grad_ref[2, 0] = grad_value.astype(BF16).T


def head_spec(tokens, offset):
    return pl.BlockSpec((1, HEAD_DIM, tokens), lambda head: (head + offset, 0, 0))


def whole_spec(shape):
    return pl.BlockSpec(shape, lambda head: (0,) * len(shape))


def row_spec(tokens):
    return pl.BlockSpec((1, 1, tokens), lambda head: (head, 0, 0))


SMALL = pl.CostEstimate(flops=1 << 20, bytes_accessed=1 << 20, transcendentals=0)


def attend(own, other, bias, hot, first, count):
    heads = own.shape[0] // 3
    part = own.shape[2]
    tokens = part + other.shape[2]
    in_specs = [
        head_spec(part, component * heads + first) for component in range(3) for _ in range(2)
    ]
    return pl.pallas_call(
        functools.partial(attend_kernel, min(tokens, (1 << 20) // tokens)),
        grid=(count,),
        in_specs=in_specs + [whole_spec(bias.shape), whole_spec(hot.shape)],
        out_specs=[head_spec(tokens, 0), row_spec(tokens)],
        out_shape=[
            jax.ShapeDtypeStruct((count, HEAD_DIM, tokens), BF16),
            jax.ShapeDtypeStruct((count, 1, tokens), F32),
        ],
        compiler_params=pltpu.CompilerParams(vmem_limit_bytes=18 << 20),
        cost_estimate=SMALL,
    )(own, other, own, other, own, other, bias, hot)


def attend_back(own, other, bias, hot, out, grad_own, grad_other, lse, first, count):
    heads = own.shape[0] // 3
    part = own.shape[2]
    tokens = part + other.shape[2]
    in_specs = [
        head_spec(part, component * heads + first) for component in range(3) for _ in range(2)
    ]
    return pl.pallas_call(
        functools.partial(attend_back_kernel, min(tokens, (1 << 19) // tokens)),
        grid=(count,),
        in_specs=in_specs
        + [
            whole_spec(bias.shape),
            whole_spec(hot.shape),
            head_spec(tokens, 0),
            head_spec(part, first),
            head_spec(part, first),
            row_spec(tokens),
        ],
        out_specs=pl.BlockSpec((3, 1, HEAD_DIM, tokens), lambda head: (0, head, 0, 0)),
        out_shape=jax.ShapeDtypeStruct((3, count, HEAD_DIM, tokens), BF16),
        compiler_params=pltpu.CompilerParams(vmem_limit_bytes=18 << 20),
        cost_estimate=SMALL,
    )(own, other, own, other, own, other, bias, hot, out, grad_own, grad_other, lse)


def write_kernel(place, first, last, aliased, *refs):
    me = lax.axis_index("dp")
    sources = refs[: len(refs) - 3 - aliased]
    out_ref, wide, sems = refs[-3:]
    copies = []
    for group, source in enumerate(sources):
        for block in range(first, last):
            slot = group * (last - first) + block - first
            wide[slot] = source[block].astype(F32)
            copies.append(
                pltpu.make_async_copy(
                    wide.at[slot], place(out_ref, me, group, block), sems.at[slot]
                )
            )
            copies[-1].start()
    for copy in copies:
        copy.wait()


def write_out(groups, place, shape, onto=None, part=None):
    blocks, rows, columns = groups[0].shape
    first, last = (0, blocks) if part is None else part
    count = len(groups) * (last - first)
    anywhere = pl.BlockSpec(memory_space=pl.ANY)
    extra = [] if onto is None else [onto]
    return pl.pallas_call(
        functools.partial(write_kernel, place, first, last, len(extra)),
        in_specs=[pl.BlockSpec(memory_space=pltpu.VMEM)] * len(groups) + [anywhere] * len(extra),
        out_specs=anywhere,
        scratch_shapes=[
            pltpu.VMEM((count, rows, columns), F32),
            pltpu.SemaphoreType.DMA((count,)),
        ],
        out_shape=jax.ShapeDtypeStruct(shape, F32),
        input_output_aliases={} if onto is None else {len(groups): 0},
        compiler_params=pltpu.CompilerParams(vmem_limit_bytes=20 << 20),
        cost_estimate=SMALL,
    )(*groups, *extra)


def hidden_kernel(inputs_ref, weight_ref, active_ref, slope_ref):
    rows = inputs_ref.shape[0] // 4
    for start in range(0, 4 * rows, rows):
        part = slice(start, start + rows)
        active, slope = gelu_parts(dot(inputs_ref[part], weight_ref[...], 1, 0))
        active_ref[part] = active.astype(BF16)
        slope_ref[part] = slope.astype(BF16)


def hidden_units(inputs, weight):
    rows, width = inputs.shape
    units = weight.shape[1]
    block = units // 6
    out_block = pl.BlockSpec((rows, block), lambda i: (0, i))
    return pl.pallas_call(
        hidden_kernel,
        grid=(6,),
        in_specs=[
            pl.BlockSpec((rows, width), lambda i: (0, 0)),
            pl.BlockSpec((width, block), lambda i: (0, i)),
        ],
        out_specs=[out_block] * 2,
        out_shape=[jax.ShapeDtypeStruct((rows, units), BF16)] * 2,
        compiler_params=pltpu.CompilerParams(vmem_limit_bytes=20 << 20),
        cost_estimate=SMALL,
    )(inputs, weight)


def hidden_back_kernel(grad_ref, weight_ref, slope_ref, out_ref):
    rows = grad_ref.shape[0] // 4
    for start in range(0, 4 * rows, rows):
        part = slice(start, start + rows)
        grads = dot(grad_ref[part], weight_ref[...], 1, 1)
        out_ref[part] = (grads * slope_ref[part].astype(F32)).astype(BF16)


def hidden_back(grads, weight, slope):
    rows, width = grads.shape
    units = weight.shape[0]
    block = units // 6
    out_block = pl.BlockSpec((rows, block), lambda i: (0, i))
    return pl.pallas_call(
        hidden_back_kernel,
        grid=(6,),
        in_specs=[
            pl.BlockSpec((rows, width), lambda i: (0, 0)),
            pl.BlockSpec((block, width), lambda i: (i, 0)),
            out_block,
        ],
        out_specs=out_block,
        out_shape=jax.ShapeDtypeStruct((rows, units), BF16),
        compiler_params=pltpu.CompilerParams(vmem_limit_bytes=20 << 20),
        cost_estimate=SMALL,
    )(grads, weight, slope)


def gradient_kernel(left_is_blocked, half_ref, left_ref, right_ref, *refs):
    total = dot(left_ref[...], right_ref[...], 0, 0)
    if len(refs) == 2:
        total = total + refs[0][...].astype(F32)
    refs[-1][...] = total.astype(BF16)


def half_gradient(left, right, half, away, left_is_blocked):
    rows = left.shape[0]
    blocked = left if left_is_blocked else right
    whole = right if left_is_blocked else left
    units = blocked.shape[1] // 2
    block = units // 3
    half_spec = pl.BlockSpec((rows, block), lambda i, half_ref: (0, half_ref[0] * 3 + i))
    whole_block = pl.BlockSpec(whole.shape, lambda i, half_ref: (0, 0))
    if left_is_blocked:
        shape = (units, whole.shape[1])
        out_spec = pl.BlockSpec((block, shape[1]), lambda i, half_ref: (i, 0))
        in_specs = [half_spec, whole_block]
    else:
        shape = (whole.shape[1], units)
        out_spec = pl.BlockSpec((shape[0], block), lambda i, half_ref: (0, i))
        in_specs = [whole_block, half_spec]
    extra = [] if away is None else [away]
    return pl.pallas_call(
        functools.partial(gradient_kernel, left_is_blocked),
        grid_spec=pltpu.PrefetchScalarGridSpec(
            num_scalar_prefetch=1,
            grid=(3,),
            in_specs=in_specs + [out_spec] * len(extra),
            out_specs=out_spec,
        ),
        out_shape=jax.ShapeDtypeStruct(shape, BF16),
        compiler_params=pltpu.CompilerParams(vmem_limit_bytes=22 << 20),
        cost_estimate=SMALL,
    )(half.astype(jnp.int32)[None], left, right, *extra)


def down_gradient(active, grads, half, away=None):
    return half_gradient(active, grads, half, away, True)


def up_gradient(inputs, grads, half, away=None):
    return half_gradient(inputs, grads, half, away, False)


def rows_back_kernel(grad_ref, weight_ref, wide_ref, low_ref):
    total = dot(grad_ref[...], weight_ref[...], 1, 1)
    wide_ref[...] = total
    low_ref[...] = total.astype(BF16)


def rows_back(grads, weight, which):
    rows = grads.shape[0] // 2
    units = grads.shape[1]
    width = weight.shape[0]
    block = width // 3
    out_block = pl.BlockSpec((rows, block), lambda i: (0, i))
    return pl.pallas_call(
        rows_back_kernel,
        grid=(3,),
        in_specs=[
            pl.BlockSpec((rows, units), lambda i: (which, 0)),
            pl.BlockSpec((block, units), lambda i: (i, 0)),
        ],
        out_specs=[out_block] * 2,
        out_shape=[
            jax.ShapeDtypeStruct((rows, width), F32),
            jax.ShapeDtypeStruct((rows, width), BF16),
        ],
        compiler_params=pltpu.CompilerParams(vmem_limit_bytes=20 << 20),
        cost_estimate=SMALL,
    )(grads, weight)


def finish_kernel(
    half_steps,
    halfway_ref,
    own_ref,
    away_ref,
    branch_ref,
    two_ref,
    two_first_ref,
    two_last_ref,
    tokens_ref,
    mods_ref,
    result_ref,
    grad_ref,
):
    values = tokens_ref[...].astype(F32)
    two_away = jnp.where(
        pl.program_id(0) < half_steps, two_first_ref[...].astype(F32), two_last_ref[...].astype(F32)
    )
    two = two_ref[...] + two_away
    halfway = values + mods_ref[0, 2:3] * branch_ref[...]
    result_ref[...] = (halfway + mods_ref[0, 5:6] * two).astype(BF16)
    normed, inverse = normalize(values)
    grad_mod = own_ref[...] + away_ref[...].astype(F32)
    back = norm_back(grad_mod * (1.0 + mods_ref[0, 1:2]), normed, inverse)
    grad_ref[...] = (halfway_ref[...] + back).astype(BF16)


def finish(grad_halfway, own, away, branch, two, two_first, two_last, tokens, mods):
    rows, width = tokens.shape
    chunk = own.shape[0] // mods.shape[0]
    steps = rows // chunk
    half_steps = steps // 2
    row_block = pl.BlockSpec((chunk, width), lambda i: (i, 0))
    return pl.pallas_call(
        functools.partial(finish_kernel, half_steps),
        grid=(steps,),
        in_specs=[
            row_block,
            row_block,
            row_block,
            row_block,
            row_block,
            pl.BlockSpec((chunk, width), lambda i: (jnp.minimum(i, half_steps - 1), 0)),
            pl.BlockSpec((chunk, width), lambda i: (jnp.maximum(i - half_steps, 0), 0)),
            row_block,
            pl.BlockSpec((1, 6, width), lambda i: (i, 0, 0)),
        ],
        out_specs=[row_block, row_block],
        out_shape=[jax.ShapeDtypeStruct((rows, width), BF16)] * 2,
        compiler_params=pltpu.CompilerParams(vmem_limit_bytes=16 << 20),
        cost_estimate=SMALL,
    )(grad_halfway, own, away, branch, two, two_first, two_last, tokens, mods)


def heads_back_kernel(first_ref, second_ref, first_weight, second_weight, wide_ref, low_ref):
    total = dot(first_ref[...], first_weight[...], 0, 0)
    total = total + dot(second_ref[...], second_weight[...], 0, 0)
    wide_ref[...] = total
    low_ref[...] = total.astype(BF16)


def heads_back(first, second, first_weight, second_weight):
    rows = first.shape[1]
    width = first_weight.shape[1]
    block = width // 3
    out_block = pl.BlockSpec((rows, block), lambda i: (0, i))
    return pl.pallas_call(
        heads_back_kernel,
        grid=(3,),
        in_specs=[
            pl.BlockSpec(first.shape, lambda i: (0, 0)),
            pl.BlockSpec(second.shape, lambda i: (0, 0)),
            pl.BlockSpec((first_weight.shape[0], block), lambda i: (0, i)),
            pl.BlockSpec((second.shape[0], block), lambda i: (0, i)),
        ],
        out_specs=[out_block] * 2,
        out_shape=[
            jax.ShapeDtypeStruct((rows, width), F32),
            jax.ShapeDtypeStruct((rows, width), BF16),
        ],
        compiler_params=pltpu.CompilerParams(vmem_limit_bytes=22 << 20),
        cost_estimate=SMALL,
    )(first, second, first_weight, second_weight)


def condition_kernel(grad_ref, weight_ref, out_ref):
    out_ref[...] = dot(grad_ref[...], weight_ref[...], 1, 1).astype(BF16)


def condition_part(grads, weight):
    rows, depth = weight.shape
    block = rows // 3
    return pl.pallas_call(
        condition_kernel,
        grid=(3,),
        in_specs=[
            pl.BlockSpec((grads.shape[0], depth), lambda i: (0, 0)),
            pl.BlockSpec((block, depth), lambda i: (i, 0)),
        ],
        out_specs=pl.BlockSpec((grads.shape[0], block), lambda i: (0, i)),
        out_shape=jax.ShapeDtypeStruct((grads.shape[0], rows), BF16),
        compiler_params=pltpu.CompilerParams(vmem_limit_bytes=14 << 20),
        cost_estimate=SMALL,
    )(grads, weight)


def ada_kernel(act_ref, grad_ref, out_ref):
    out_ref[...] = dot(act_ref[...], grad_ref[...], 0, 0)


def ada_gradient(act, grads, columns):
    block = columns // 9
    return pl.pallas_call(
        ada_kernel,
        grid=(9,),
        in_specs=[
            pl.BlockSpec(act.shape, lambda i: (0, 0)),
            pl.BlockSpec((act.shape[0], block), lambda i: (0, i)),
        ],
        out_specs=pl.BlockSpec((act.shape[1], block), lambda i: (0, i)),
        out_shape=jax.ShapeDtypeStruct((act.shape[1], columns), F32),
        compiler_params=pltpu.CompilerParams(vmem_limit_bytes=14 << 20),
        cost_estimate=SMALL,
    )(act, grads)


def middle_kernel(own_steps, first_ref, heads_ref, weight_ref, own_ref, away_ref, mods_ref, *outs):
    branch_ref, inputs_ref, normed_ref = outs
    branch = first_ref[...] + dot(heads_ref[...], weight_ref[...], 0, 0)
    is_own = pl.program_id(0) < own_steps
    values = jnp.where(is_own, own_ref[...].astype(F32), away_ref[...].astype(F32))
    normed, _ = normalize(values + mods_ref[0, 2:3] * branch)
    branch_ref[...] = branch
    inputs_ref[...] = (normed * (1.0 + mods_ref[0, 4:5]) + mods_ref[0, 3:4]).astype(BF16)
    normed_ref[...] = normed.astype(BF16)


def middle(first, heads_away, weight, own, away, mods):
    rows, width = first.shape
    steps = mods.shape[0]
    chunk = rows // steps
    own_steps = own.shape[0] // chunk
    depth = heads_away.shape[0]
    row_block = pl.BlockSpec((chunk, width), lambda i: (i, 0))
    return pl.pallas_call(
        functools.partial(middle_kernel, own_steps),
        grid=(steps,),
        in_specs=[
            row_block,
            pl.BlockSpec((depth, chunk), lambda i: (0, (i + steps // 2) % steps)),
            pl.BlockSpec((depth, width), lambda i: (1, 0)),
            pl.BlockSpec((chunk, width), lambda i: (jnp.minimum(i, own_steps - 1), 0)),
            pl.BlockSpec((chunk, width), lambda i: (jnp.maximum(i - own_steps, 0), 0)),
            pl.BlockSpec((1, 6, width), lambda i: (i, 0, 0)),
        ],
        out_specs=[row_block] * 3,
        out_shape=[
            jax.ShapeDtypeStruct((rows, width), F32),
            jax.ShapeDtypeStruct((rows, width), BF16),
            jax.ShapeDtypeStruct((rows, width), BF16),
        ],
        compiler_params=pltpu.CompilerParams(vmem_limit_bytes=14 << 20),
        cost_estimate=SMALL,
    )(first, heads_away, weight, own, away, mods)


def middle_back_kernel(
    half_steps, own_ref, first_ref, second_ref, branch_ref, tokens_ref, cot_ref, mods_ref, *outs
):
    grad_ref, low_ref, sums_ref = outs
    arrived = jnp.where(
        pl.program_id(0) < half_steps, first_ref[...].astype(F32), second_ref[...].astype(F32)
    )
    branch = branch_ref[...]
    gate = mods_ref[0, 2:3]
    normed, inverse = normalize(tokens_ref[...].astype(F32) + gate * branch)
    grad_mod = own_ref[...] + arrived
    grad = cot_ref[...].astype(F32) + norm_back(
        grad_mod * (1.0 + mods_ref[0, 4:5]), normed, inverse
    )
    grad_ref[...] = grad
    low_ref[...] = (grad * gate).astype(BF16)
    sums_ref[0] = jnp.sum(grad * branch, axis=0, keepdims=True)


def middle_back(own, first, second, branch, tokens, cot, mods):
    rows, width = own.shape
    chunk = branch.shape[0] // mods.shape[0]
    steps = rows // chunk
    half_steps = steps // 2
    row_block = pl.BlockSpec((chunk, width), lambda i: (i, 0))
    return pl.pallas_call(
        functools.partial(middle_back_kernel, half_steps),
        grid=(steps,),
        in_specs=[
            row_block,
            pl.BlockSpec((chunk, width), lambda i: (jnp.minimum(i, half_steps - 1), 0)),
            pl.BlockSpec((chunk, width), lambda i: (jnp.maximum(i - half_steps, 0), 0)),
            row_block,
            row_block,
            row_block,
            pl.BlockSpec((1, 6, width), lambda i: (i, 0, 0)),
        ],
        out_specs=[row_block, row_block, pl.BlockSpec((1, 1, width), lambda i: (i, 0, 0))],
        out_shape=[
            jax.ShapeDtypeStruct((rows, width), F32),
            jax.ShapeDtypeStruct((rows, width), BF16),
            jax.ShapeDtypeStruct((steps, 1, width), F32),
        ],
        compiler_params=pltpu.CompilerParams(vmem_limit_bytes=14 << 20),
        cost_estimate=SMALL,
    )(own, first, second, branch, tokens, cot, mods)


def pair_body(
    tokens,
    segments,
    labels,
    timesteps,
    class_table,
    time_weight,
    ada_weight,
    qkv_weight,
    proj_weight,
    up_weight,
    down_weight,
    cotangent,
):
    position = lax.axis_index("tensor")
    rank = lax.axis_index("dp")
    dp_size = 16
    core, line, deep = rank % 2, rank // 2 % 2, rank // 4 % 2
    own_low = tokens[0]
    cot_low = cotangent[0]
    shard, width = own_low.shape
    pack = segments.shape[1]
    slot_count = labels.shape[1]
    class_count = class_table.shape[0]
    freq_width = time_weight.shape[0]
    local_width = qkv_weight.shape[2]
    heads = local_width // HEAD_DIM
    half_heads = heads // 2
    half_width = local_width // 2
    hidden_width = up_weight.shape[1]
    chunk = shard * SHORT // pack
    own_chunks = shard // chunk
    CORE, LINE, DEEP, FAR = 1, 2, 4, 8

    def fence(*values):
        return lax.optimization_barrier(values)

    def swap(x):
        return lax.ppermute(x, "tensor", [(0, 1), (1, 0)])

    def trade(x, bits):
        return lax.ppermute(x, "dp", [(i, i ^ bits) for i in range(dp_size)])

    def rows_of(x, index, count):
        size = x.shape[0] // count
        return lax.dynamic_slice_in_dim(x, index * size, size, 0)

    def columns_of(x, index, count):
        size = x.shape[1] // count
        return lax.dynamic_slice_in_dim(x, index * size, size, 1)

    def plus(a, b):
        return (a.astype(F32) + b.astype(F32)).astype(BF16)

    def halve(x, digit, bits):
        return plus(rows_of(x, digit, 2), trade(rows_of(x, 1 - digit, 2), bits))

    def digit(me, bits):
        return me // bits % 2

    def down_place(ref, me, group, block):
        index = (
            (digit(me, CORE) + group) % 2 * 4
            + (digit(me, LINE) + block // 2) % 2 * 2
            + (digit(me, DEEP) + block) % 2
        )
        return ref.at[index]

    def proj_place(ref, me, group, block):
        index = (digit(me, CORE) + group // 2) % 2 * 4 + (digit(me, LINE) + group % 2) % 2 * 2
        return ref.at[index + block - 3]

    def up_place(ref, me, group, block):
        index = (digit(me, LINE) + block // 2) % 2 * 2 + (digit(me, DEEP) + block) % 2
        column = (digit(me, CORE) + group) % 2 * (hidden_width // 2)
        return ref.at[index, :, pl.ds(pl.multiple_of(column, 128), hidden_width // 2)]

    def qkv_place(offset, bits):
        def place(ref, me, group, block):
            unit = (
                (digit(me, CORE) + group // 2) % 2 * 2 + (digit(me, bits) + group % 2) % 2
            ) * 3 + block
            return ref.at[unit // half_heads * heads + unit % half_heads + offset]

        return place

    def chunked(x):
        return x.reshape(x.shape[0] // chunk, chunk, x.shape[1])

    def flat(x):
        return x.reshape(x.shape[0] * chunk, x.shape[2])

    quarter = shard // 2
    tokens_away = swap(own_low)
    ids = jnp.stack([labels[0], timesteps[0]], axis=1)

    seg = segments[0]
    seg = jnp.where(position == 0, seg, jnp.roll(seg, shard))
    slots = jnp.arange(slot_count, dtype=jnp.int32)
    chunk_hot = (seg[::chunk][:, None] == slots[None, :]).astype(F32)
    mask_rows = -(-slot_count // 8) * 8
    same = jnp.arange(mask_rows, dtype=jnp.int32)[:, None] == seg[None, :]
    hot = same.astype(BF16)
    bias = jnp.where(same, 0.0, -1e30).astype(BF16)

    classes = jnp.arange(class_count, dtype=jnp.int32)

    def condition_of(ids):
        label_hot = (ids[:, 0][:, None] == classes[None, :]).astype(F32)
        feats = features(ids[:, 1].astype(F32), freq_width)
        values = dot(label_hot, class_table, 1, 0, HIGH) + dot(feats, time_weight, 1, 0, HIGH)
        return label_hot, feats, values

    def hop(y, bits):
        return jnp.concatenate([y, trade(y, bits)], axis=0)

    condition = condition_of(ids)[2]
    pad = jnp.zeros((slot_count, 124), jnp.int32)
    digits = jnp.concatenate([ids // 32, ids % 32, pad], axis=1).astype(BF16)
    act_low = jax.nn.silu(condition).astype(BF16)
    weight_t = qkv_weight.transpose(1, 2, 0).reshape(3 * local_width, width)
    weight_parts = weight_t.reshape(3, 2, half_width, width)
    weight_a = weight_parts[:, 0].reshape(3 * half_width, width)
    weight_b = weight_parts[:, 1].reshape(3 * half_width, width)
    mod_part, tokens_away, proj_half, weight_a, weight_b = fence(
        dot(act_low, ada_weight, 1, 0),
        tokens_away,
        rows_of(proj_weight, core, 2),
        weight_a,
        weight_b,
    )
    mod_away, tokens_away = fence(swap(mod_part), tokens_away)
    modulation = jnp.where(
        position == 0,
        jnp.concatenate([mod_part, mod_away], axis=1),
        jnp.concatenate([mod_away, mod_part], axis=1),
    )
    proj_half = swap(proj_half)
    per_chunk = dot(chunk_hot, modulation, 1, 0, HIGH)
    mods_own = [m[:, None, :] for m in jnp.split(per_chunk[:own_chunks], 6, axis=1)]
    mods_other = [m[:, None, :] for m in jnp.split(per_chunk[own_chunks:], 6, axis=1)]


    def enter(low, mods):
        values = chunked(low.astype(F32))
        normed, inverse = normalize(values)
        inputs = flat((normed * (1.0 + mods[1]) + mods[0]).astype(BF16))
        return values, normed, inverse, inputs

    def project(inputs):
        return dot(weight_t, inputs, 1, 1).astype(BF16).reshape(3 * heads, HEAD_DIM, shard)

    tokens_own, normed_one, inverse_one, inputs_one_own = enter(own_low, mods_own)
    qkv_own = project(inputs_one_own)
    tokens_other, normed_one_other, _, inputs_one_other = enter(tokens_away, mods_other)
    qkv_other = project(inputs_one_other)
    out_a, lse_a = attend(qkv_own, qkv_other, bias, hot, 0, half_heads)
    chunk_mods = per_chunk.reshape(pack // chunk, 6, width)
    out_a, qkv_own, chunk_mods = fence(out_a, qkv_own, chunk_mods)
    away_a = swap(out_a.reshape(half_width, pack))
    out_b, lse_b = attend(qkv_own, qkv_other, bias, hot, half_heads, half_heads)
    out_b, proj_half, away_a = fence(out_b, proj_half, away_a)
    away_b = swap(out_b.reshape(half_width, pack))
    proj_rest = trade(proj_half, CORE)
    proj_other = jnp.where(
        core == 0,
        jnp.concatenate([proj_half, proj_rest], axis=0),
        jnp.concatenate([proj_rest, proj_half], axis=0),
    )
    out_flat = jnp.concatenate([out_a, out_b], axis=0).reshape(local_width, pack)
    own_part, other_part = slice(0, shard), slice(shard, pack)

    def reordered(away):
        return jnp.concatenate([away[:, other_part], away[:, own_part]], axis=1)

    away_a, proj_other = fence(away_a, proj_other)
    first, _ = heads_back(out_flat, reordered(away_a), proj_weight, proj_other)
    away_b, cot_next, first = fence(away_b, cot_low, first)
    cot_away = swap(cot_next)
    branch_one, inputs_two, normed_two = middle(
        first, away_b, proj_other, own_low, tokens_away, chunk_mods
    )

    active, slope = hidden_units(inputs_two, up_weight)
    active, slope, cot_away = fence(active, slope, cot_away)
    grad_branch_two = jnp.concatenate(
        [
            flat((chunked(cot_low.astype(F32)) * mods_own[5]).astype(BF16)),
            flat((chunked(cot_away.astype(F32)) * mods_other[5]).astype(BF16)),
        ],
        axis=0,
    )

    down_away = trade(down_gradient(active, grad_branch_two, 1 - core), CORE)
    grad_hidden = hidden_back(grad_branch_two, down_weight, slope)
    down_sum = down_gradient(active, grad_branch_two, core, down_away)
    down_sum, grad_hidden = fence(down_sum, grad_hidden)
    down_x = trade(rows_of(down_sum, 1 - line, 2), LINE)
    mod_two_other, mod_two_away = rows_back(grad_hidden, up_weight, 1)
    mod_two_away, grad_hidden = fence(mod_two_away, grad_hidden)

    arrived_a = swap(mod_two_away[:quarter])
    up_away = trade(up_gradient(inputs_two, grad_hidden, 1 - core), CORE)
    mod_two, _ = rows_back(grad_hidden, up_weight, 0)
    arrived_a, up_away, mod_two, mod_two_next, grad_hidden, active = fence(
        arrived_a, up_away, mod_two, mod_two_away[quarter:], grad_hidden, active
    )
    arrived_b = swap(mod_two_next)
    up_sum = up_gradient(inputs_two, grad_hidden, core, up_away)
    up_x = trade(rows_of(up_sum, 1 - line, 2), LINE)
    branch_two_away = dot(active[other_part], down_weight, 1, 0)
    branch_two = dot(active[own_part], down_weight, 1, 0)
    arrived_b, mod_two, branch_two_away, branch_two, down_x = fence(
        arrived_b, mod_two, branch_two_away, branch_two, down_x
    )

    down_sum = plus(rows_of(down_sum, line, 2), down_x)
    down_z = trade(rows_of(down_sum, 1 - deep, 2), DEEP)
    grad_halfway, grad_branch_one, gate_one_sums = middle_back(
        mod_two, arrived_a, arrived_b, branch_one, own_low, cot_low, chunk_mods
    )
    grad_att_away = dot(proj_other, grad_branch_one, 1, 1).astype(BF16)
    grad_att_away, grad_branch_one = fence(grad_att_away, grad_branch_one)

    grad_att_other = swap(grad_att_away)
    grad_att_own = dot(proj_weight, grad_branch_one, 1, 1).astype(BF16)
    def chunk_sums(own, other):
        return jnp.concatenate([jnp.sum(own, axis=1), jnp.sum(other, axis=1)], axis=0)

    normed_two = chunked(normed_two.astype(F32))
    late_terms = jnp.concatenate(
        [
            jnp.concatenate([gate_one_sums[:, 0], jnp.zeros_like(gate_one_sums[:, 0])], axis=0),
            chunk_sums(chunked(mod_two), chunked(mod_two_other)),
            chunk_sums(
                chunked(mod_two) * normed_two[:own_chunks],
                chunked(mod_two_other) * normed_two[own_chunks:],
            ),
            chunk_sums(
                chunked(branch_two) * chunked(cot_low.astype(F32)),
                chunked(branch_two_away) * chunked(cot_away.astype(F32)),
            ),
        ],
        axis=1,
    )
    inputs_one = jnp.concatenate([inputs_one_own, inputs_one_other], axis=0)
    grad_att_other, grad_att_own, down_z, branch_one_next, inputs_one, late_terms = fence(
        grad_att_other, grad_att_own, down_z, grad_branch_one, inputs_one, late_terms
    )
    down_sum = plus(rows_of(down_sum, deep, 2), down_z)
    down_block = down_sum.shape[0] // 2
    down_far_a = trade(down_sum[:down_block], FAR)

    def back(out, lse, first):
        return attend_back(
            qkv_own,
            qkv_other,
            bias,
            hot,
            out,
            grad_att_own.reshape(heads, HEAD_DIM, shard),
            grad_att_other.reshape(heads, HEAD_DIM, shard),
            lse,
            first,
            half_heads,
        ).reshape(3 * half_width, pack)

    def qkv_half(grad):
        return lambda half: dot(rows_of(grad, half, 2), inputs_one, 1, 0)

    grads_one_other = swap(branch_one_next)
    grad_qkv_a = back(out_a, lse_a, 0)
    grad_qkv_a, up_x, down_far_a, down_next = fence(
        grad_qkv_a, up_x, down_far_a, down_sum[down_block:]
    )
    down_far_b = trade(down_next, FAR)
    up_sum = plus(rows_of(up_sum, line, 2), up_x)
    up_z = trade(rows_of(up_sum, 1 - deep, 2), DEEP)
    qkv_make = qkv_half(grad_qkv_a)
    qkv_a_away = trade(qkv_make(1 - core).astype(BF16), CORE)
    qkv_a = plus(qkv_make(core), qkv_a_away)
    qkv_a, grad_att_own = fence(qkv_a, grad_att_own)
    qkv_a_x = trade(rows_of(qkv_a, 1 - line, 2), LINE)
    grad_qkv_b = back(out_b, lse_b, half_heads)
    grad_qkv_b, qkv_a_x, up_z, down_far_b, grads_one_other = fence(
        grad_qkv_b, qkv_a_x, up_z, down_far_b, grads_one_other
    )
    qkv_a = plus(rows_of(qkv_a, line, 2), qkv_a_x)
    up_sum = plus(rows_of(up_sum, deep, 2), up_z)
    down_sum = plus(down_sum, jnp.concatenate([down_far_a, down_far_b], axis=0))
    down_z = trade(down_sum, DEEP)
    down_x = trade(down_sum, LINE)
    block = up_sum.shape[0] // 2
    up_far_a = trade(up_sum[:block], FAR)
    mod_one = dot(grad_qkv_a, weight_a, 0, 0) + dot(grad_qkv_b, weight_b, 0, 0)
    mod_one_own, mod_one_away = chunked(mod_one[own_part]), chunked(mod_one[other_part])
    chunk_terms = jnp.concatenate(
        [
            chunk_sums(mod_one_own, mod_one_away),
            chunk_sums(mod_one_own * normed_one, mod_one_away * normed_one_other),
            late_terms,
        ],
        axis=1,
    )
    slot_terms = dot(chunk_hot, chunk_terms, 0, 0, HIGH).astype(BF16)
    half = slot_terms.shape[1] // 2
    low, high = slot_terms[:, :half], slot_terms[:, half:]
    keep = jnp.where(position == 0, low, high)
    away = jnp.where(position == 0, high, low)
    (
        away,
        keep,
        mod_one_next,
        down_z,
        down_x,
        up_far_a,
        grad_qkv_b,
        up_next,
        qkv_a,
    ) = fence(
        away,
        keep,
        flat(mod_one_away).astype(BF16),
        down_z,
        down_x,
        up_far_a,
        grad_qkv_b,
        up_sum[block:],
        qkv_a,
    )

    gathered = jnp.concatenate([plus(keep, swap(away)), digits], axis=1)[None]
    down_zx = trade(down_z, LINE)
    up_far_b = trade(up_next, FAR)
    qkv_a_z = trade(rows_of(qkv_a, 1 - deep, 2), DEEP)
    qkv_make_b = qkv_half(grad_qkv_b)

    def proj_half_of(half):
        rows = rows_of(out_flat, half, 2)
        return dot(rows[:, own_part], grad_branch_one, 1, 0) + dot(
            rows[:, other_part], grads_one_other, 1, 0
        )

    def packed(qkv, proj, index):
        return jnp.concatenate([rows_of(qkv, index, 2), rows_of(proj, index, 2)], axis=0)

    def unpacked(both):
        cut = both.shape[0] * 3 // 5
        return both[:cut], both[cut:]

    def in_order(digit, own, other):
        return jnp.where(
            digit == 0,
            jnp.concatenate([own, other], axis=0),
            jnp.concatenate([other, own], axis=0),
        )

    rest = trade(
        jnp.concatenate(
            [qkv_make_b(1 - core).astype(BF16), proj_half_of(1 - core).astype(BF16)], axis=0
        ),
        CORE,
    )
    qkv_rows = 3 * half_width // 2
    qkv_b = plus(qkv_make_b(core), rest[:qkv_rows])
    proj_sum = plus(proj_half_of(core), rest[qkv_rows:])
    both_next = packed(qkv_b, proj_sum, 1 - line)
    both = packed(qkv_b, proj_sum, line)
    gathered, up_far_b, down_zx, qkv_a_z, both_next, both, mod_one_next = fence(
        gathered, up_far_b, down_zx, qkv_a_z, both_next, both, mod_one_next
    )

    up_low = plus(up_sum[:block], up_far_a)
    up_high = plus(up_next, up_far_b)
    up_sum = jnp.concatenate([up_low, up_high], axis=0)
    qkv_a = plus(rows_of(qkv_a, deep, 2), qkv_a_z)
    up_sum, qkv_a, both_next, gathered, mod_one_next = fence(
        up_sum, qkv_a, both_next, gathered, mod_one_next
    )
    gathered = hop(gathered, LINE)
    mod_one_other = swap(mod_one_next)
    both_x = trade(both_next, LINE)
    up_z = trade(up_sum, DEEP)
    qkv_a_far = trade(qkv_a, FAR)
    (
        gathered,
        both_x,
        up_z,
        qkv_a_far,
        mod_one_other,
        both,
        down_sum,
        down_z,
        down_x,
        down_zx,
    ) = fence(
        gathered,
        both_x,
        up_z,
        qkv_a_far,
        mod_one_other,
        both,
        down_sum,
        down_z,
        down_x,
        down_zx,
    )
    both = plus(both, both_x)
    both_next = packed(*unpacked(both), 1 - deep)
    qkv_a = plus(qkv_a, qkv_a_far)
    both_next, qkv_a, gathered, up_sum, both, two_low = fence(
        both_next, qkv_a, gathered, up_sum, both, branch_two_away.astype(BF16)
    )
    two_first = swap(two_low[:quarter])
    gathered = hop(gathered, FAR)
    up_x = trade(up_sum, LINE)
    down_blocks = jnp.stack([down_sum, down_z, down_x, down_zx])
    both_z = trade(both_next, DEEP)
    qkv_a_z = trade(qkv_a, DEEP)
    both = packed(*unpacked(both), deep)
    gathered, up_x, both_z, qkv_a_z, both, down_blocks, two_first, two_next = fence(
        gathered, up_x, both_z, qkv_a_z, both, down_blocks, two_first, two_low[quarter:]
    )
    both = plus(both, both_z)
    qkv_a = in_order(deep, qkv_a, qkv_a_z).reshape(3, HEAD_DIM, width)
    both, qkv_a, gathered, up_z, down_blocks, two_next = fence(
        both, qkv_a, gathered, up_z, down_blocks, two_next
    )
    two_last = swap(two_next)
    grad_down = write_out(
        [down_blocks, trade(down_blocks, CORE)], down_place, (8, hidden_width // 8, width)
    )
    gathered = hop(gathered, DEEP)
    up_zx = trade(up_z, LINE)
    both_far = trade(both, FAR)
    up_zx, both_far, gathered, grad_down, two_last = fence(
        up_zx, both_far, gathered, grad_down, two_last
    )
    both = plus(both, both_far)
    both, gathered, qkv_a = fence(both, gathered, qkv_a)
    up_blocks = jnp.stack([up_sum, up_z, up_x, up_zx])
    both_z = trade(both, DEEP)
    qkv_a_x = trade(qkv_a, LINE)
    up_blocks_c = trade(up_blocks, CORE)
    grad_mod_all = hop(gathered, CORE).reshape(dp_size * slot_count, half + 128)
    cond_part = condition_part(grad_mod_all, ada_weight)
    result, grad_input = finish(
        grad_halfway,
        mod_one,
        mod_one_other,
        branch_one,
        branch_two,
        two_first,
        two_last,
        own_low,
        chunk_mods,
    )
    both_z, cond_part, grad_mod_all, up_blocks_c, qkv_a_x, result = fence(
        both_z, cond_part, grad_mod_all, up_blocks_c, qkv_a_x, result
    )
    both = jnp.concatenate(
        [in_order(deep, a, b) for a, b in zip(unpacked(both), unpacked(both_z), strict=True)],
        axis=0,
    ).reshape(5, HEAD_DIM, width)
    both_x = trade(both, LINE)
    both_c = trade(both, CORE)
    grad_act = cond_part.astype(F32) + swap(cond_part).astype(F32)
    qkv_a_c = trade(qkv_a, CORE)
    qkv_a_xc = trade(qkv_a_x, CORE)
    grad_up = write_out([up_blocks, up_blocks_c], up_place, (4, width // 4, hidden_width))
    ids_all = grad_mod_all[:, half : half + 4].astype(jnp.int32)
    label_hot, features_all, condition_all = condition_of(ids_all[:, :2] * 32 + ids_all[:, 2:])
    act_all = jax.nn.silu(condition_all).astype(BF16)
    grad_ada = ada_gradient(act_all, grad_mod_all, ada_weight.shape[1])
    both_x, both_c, grad_up, grad_act, grad_ada, qkv_a_c, qkv_a_xc = fence(
        both_x, both_c, grad_up, grad_act, grad_ada, qkv_a_c, qkv_a_xc
    )
    both_xc = trade(both_x, CORE)
    qkv_shape = (3 * heads, HEAD_DIM, width)
    grad_qkv = write_out([qkv_a, qkv_a_x, qkv_a_c, qkv_a_xc], qkv_place(0, LINE), qkv_shape)

    grad_condition = jax.vjp(jax.nn.silu, condition_all)[1](grad_act)[0]
    grad_class = dot(label_hot.astype(BF16), grad_condition.astype(BF16), 0, 0)
    grad_time = dot(features_all, grad_condition, 0, 0, HIGH)
    groups = [both, both_x, both_c, both_xc]
    grad_qkv = write_out(groups, qkv_place(half_heads, LINE), qkv_shape, grad_qkv, (0, 3))
    grad_proj = write_out(groups, proj_place, (8, HEAD_DIM, width), None, (3, 5))
    return (
        result[None],
        grad_input[None],
        grad_class,
        grad_time,
        grad_ada,
        grad_qkv.reshape(3, local_width, width).transpose(2, 0, 1),
        grad_proj.reshape(local_width, width),
        grad_up.reshape(width, hidden_width),
        grad_down.reshape(hidden_width, width),
    )


def any_body(
    tokens,
    segments,
    labels,
    timesteps,
    class_table,
    time_weight,
    ada_weight,
    qkv_weight,
    proj_weight,
    up_weight,
    down_weight,
    cotangent,
):
    own_tokens = tokens[0].astype(jnp.float32)
    shard_rows = own_tokens.shape[0]
    model_width = own_tokens.shape[1]
    seg_all = segments[0]
    pack_rows = seg_all.shape[0]
    slot_count = labels.shape[1]
    class_count = class_table.shape[0]
    freq_width = time_weight.shape[0]
    local_width = qkv_weight.shape[2]
    head_count = local_width // HEAD_DIM
    scale_factor = 1.0 / math.sqrt(HEAD_DIM)
    position = lax.axis_index("tensor")
    seg_own = lax.dynamic_slice_in_dim(seg_all, position * shard_rows, shard_rows)
    own_hot = (seg_own[:, None] == jnp.arange(slot_count, dtype=jnp.int32)[None, :]).astype(
        jnp.float32
    )
    label_hot = (labels[0][:, None] == jnp.arange(class_count, dtype=jnp.int32)[None, :]).astype(
        jnp.float32
    )
    step_feats = features(timesteps[0].astype(jnp.float32), freq_width)
    condition = jnp.dot(label_hot, class_table, precision=HIGH) + jnp.dot(
        step_feats, time_weight, precision=HIGH
    )
    act_low = jax.nn.silu(condition).astype(jnp.bfloat16)
    mod_part = jnp.dot(act_low, ada_weight, preferred_element_type=jnp.float32)
    modulation = lax.all_gather(mod_part, "tensor", axis=1, tiled=True)
    per_token = jnp.dot(own_hot, modulation, precision=HIGH)
    shift_one, scale_one, gate_one, shift_two, scale_two, gate_two = jnp.split(per_token, 6, axis=1)
    normed_one, inverse_one = normalize(own_tokens)
    modulated_one = (normed_one * (1.0 + scale_one) + shift_one).astype(jnp.bfloat16)
    inputs_one = lax.all_gather(modulated_one, "tensor", axis=0, tiled=True)
    qkv_flat = qkv_weight.reshape(model_width, 3 * local_width)
    qkv = jnp.dot(inputs_one, qkv_flat, preferred_element_type=jnp.float32).astype(jnp.bfloat16)
    qkv_heads = qkv.reshape(pack_rows, 3, head_count, HEAD_DIM).transpose(1, 2, 0, 3)
    queries = qkv_heads[0]
    keys = qkv_heads[1]
    values = qkv_heads[2]
    block = min(512, pack_rows)
    block_count = pack_rows // block
    starts = jnp.arange(block_count, dtype=jnp.int32) * block

    def scores_of(start):
        query_block = lax.dynamic_slice_in_dim(queries, start, block, 1)
        seg_block = lax.dynamic_slice_in_dim(seg_all, start, block)
        raw = (
            jnp.einsum("hqd,hkd->hqk", query_block, keys, preferred_element_type=jnp.float32)
            * scale_factor
        )
        same = (seg_block[:, None] == seg_all[None, :])[None]
        return (jnp.where(same, raw, -1e30), query_block)

    def attend(start):
        scores = scores_of(start)[0]
        top = jnp.max(scores, axis=-1, keepdims=True)
        exps = jnp.exp(scores - top)
        total = jnp.sum(exps, axis=-1, keepdims=True)
        weights = (exps / total).astype(jnp.bfloat16)
        out_block = jnp.einsum("hqk,hkd->hqd", weights, values, preferred_element_type=jnp.float32)
        return (out_block, (top + jnp.log(total))[..., 0])

    out_blocks, lse_blocks = lax.map(attend, starts)
    attended = out_blocks.transpose(0, 2, 1, 3).reshape(pack_rows, local_width).astype(jnp.bfloat16)
    lse_all = lse_blocks.transpose(1, 0, 2).reshape(head_count, pack_rows)
    branch_one = lax.psum_scatter(
        jnp.dot(attended, proj_weight, preferred_element_type=jnp.float32),
        "tensor",
        scatter_dimension=0,
        tiled=True,
    )
    halfway = own_tokens + gate_one * branch_one
    normed_two, inverse_two = normalize(halfway)
    modulated_two = (normed_two * (1.0 + scale_two) + shift_two).astype(jnp.bfloat16)
    inputs_two = lax.all_gather(modulated_two, "tensor", axis=0, tiled=True)
    hidden = jnp.dot(inputs_two, up_weight, preferred_element_type=jnp.float32)
    active = jax.nn.gelu(hidden, approximate=True).astype(jnp.bfloat16)
    branch_two = lax.psum_scatter(
        jnp.dot(active, down_weight, preferred_element_type=jnp.float32).astype(jnp.bfloat16),
        "tensor",
        scatter_dimension=0,
        tiled=True,
    ).astype(jnp.float32)
    result = halfway + gate_two * branch_two
    grad_out = cotangent[0].astype(jnp.float32)
    grad_gate_two = grad_out * branch_two
    grad_branch_two = (grad_out * gate_two).astype(jnp.bfloat16)
    grads_two = lax.all_gather(grad_branch_two, "tensor", axis=0, tiled=True)
    grad_down = contract_rows(active, grads_two)
    grad_active = times_transposed(grads_two, down_weight)
    gelu_back = jax.vjp(lambda inner: jax.nn.gelu(inner, approximate=True), hidden)[1]
    grad_hidden = gelu_back(grad_active)[0].astype(jnp.bfloat16)
    grad_up = contract_rows(inputs_two, grad_hidden)
    grad_mod_two = lax.psum_scatter(
        times_transposed(grad_hidden, up_weight), "tensor", scatter_dimension=0, tiled=True
    )
    grad_halfway = grad_out + norm_back(grad_mod_two * (1.0 + scale_two), normed_two, inverse_two)
    grad_gate_one = grad_halfway * branch_one
    grad_branch_one = (grad_halfway * gate_one).astype(jnp.bfloat16)
    grads_one = lax.all_gather(grad_branch_one, "tensor", axis=0, tiled=True)
    grad_proj = contract_rows(attended, grads_one)
    grad_attended = times_transposed(grads_one, proj_weight).astype(jnp.bfloat16)
    grad_heads = grad_attended.reshape(pack_rows, head_count, HEAD_DIM).transpose(1, 0, 2)

    def attend_back(carry, start):
        grad_keys, grad_values = carry
        scores, query_block = scores_of(start)
        lse_block = lax.dynamic_slice_in_dim(lse_all, start, block, 1)
        probs = jnp.exp(scores - lse_block[..., None])
        grad_block = lax.dynamic_slice_in_dim(grad_heads, start, block, 1)
        grad_probs = jnp.einsum(
            "hqd,hkd->hqk", grad_block, values, preferred_element_type=jnp.float32
        )
        grad_scores = (
            probs * (grad_probs - jnp.sum(probs * grad_probs, axis=-1, keepdims=True))
        ).astype(jnp.bfloat16)
        grad_query = (
            jnp.einsum("hqk,hkd->hqd", grad_scores, keys, preferred_element_type=jnp.float32)
            * scale_factor
        )
        grad_keys = (
            grad_keys
            + jnp.einsum(
                "hqk,hqd->hkd", grad_scores, query_block, preferred_element_type=jnp.float32
            )
            * scale_factor
        )
        grad_values = grad_values + jnp.einsum(
            "hqk,hqd->hkd",
            probs.astype(jnp.bfloat16),
            grad_block,
            preferred_element_type=jnp.float32,
        )
        return ((grad_keys, grad_values), grad_query)

    empty = jnp.zeros((head_count, pack_rows, HEAD_DIM), jnp.float32)
    key_grads, grad_queries = lax.scan(attend_back, (empty, empty), starts)
    query_grads = grad_queries.transpose(1, 0, 2, 3).reshape(head_count, pack_rows, HEAD_DIM)
    grad_stack = jnp.stack([query_grads, key_grads[0], key_grads[1]], axis=0)
    grad_qkv = (
        grad_stack.transpose(2, 0, 1, 3).reshape(pack_rows, 3 * local_width).astype(jnp.bfloat16)
    )
    grad_qkv_weight = contract_rows(inputs_one, grad_qkv).reshape(model_width, 3, local_width)
    grad_mod_one = lax.psum_scatter(
        times_transposed(grad_qkv, qkv_flat).astype(jnp.bfloat16),
        "tensor",
        scatter_dimension=0,
        tiled=True,
    ).astype(jnp.float32)
    grad_input = grad_halfway + norm_back(grad_mod_one * (1.0 + scale_one), normed_one, inverse_one)
    grad_per_token = jnp.concatenate(
        [
            grad_mod_one,
            grad_mod_one * normed_one,
            grad_gate_one,
            grad_mod_two,
            grad_mod_two * normed_two,
            grad_gate_two,
        ],
        axis=1,
    )
    slot_terms = contract_exact(own_hot, grad_per_token)
    grad_modulation = lax.psum_scatter(
        slot_terms.astype(jnp.bfloat16), "tensor", scatter_dimension=1, tiled=True
    )
    grad_ada = contract_rows(act_low, grad_modulation)
    cond_part = times_transposed(grad_modulation, ada_weight)
    grad_activated = lax.psum(cond_part.astype(jnp.bfloat16), "tensor").astype(jnp.float32)
    grad_condition = jax.vjp(jax.nn.silu, condition)[1](grad_activated)[0]
    grad_class = contract_exact(label_hot, grad_condition)
    grad_time = contract_exact(step_feats, grad_condition)
    summed = (
        lax.psum(grad_class.astype(jnp.bfloat16), "dp").astype(jnp.float32),
        lax.psum(grad_time.astype(jnp.bfloat16), "dp").astype(jnp.float32),
        lax.psum(grad_ada.astype(jnp.bfloat16), "dp").astype(jnp.float32),
        lax.psum(grad_qkv_weight.astype(jnp.bfloat16), "dp").astype(jnp.float32),
        lax.psum(grad_proj.astype(jnp.bfloat16), "dp").astype(jnp.float32),
        lax.psum(grad_up.astype(jnp.bfloat16), "dp").astype(jnp.float32),
        lax.psum(grad_down.astype(jnp.bfloat16), "dp").astype(jnp.float32),
    )
    grad_class, grad_time, grad_ada, grad_qkv_weight, grad_proj, grad_up, grad_down = summed
    return (
        result.astype(jnp.bfloat16)[None],
        grad_input.astype(jnp.bfloat16)[None],
        grad_class,
        grad_time,
        grad_ada,
        grad_qkv_weight,
        grad_proj,
        grad_up,
        grad_down,
    )


def solution(mesh):
    pairs = mesh.shape["dp"] == 16 and mesh.shape["tensor"] == 2
    return jax.shard_map(
        pair_body if pairs else any_body,
        mesh=mesh,
        in_specs=(
            P("dp", "tensor", None),
            P("dp", None),
            P("dp", None),
            P("dp", None),
            P(),
            P(),
            P(None, "tensor"),
            P(None, None, "tensor"),
            P("tensor", None),
            P(None, "tensor"),
            P("tensor", None),
            P("dp", "tensor", None),
        ),
        out_specs=(
            P("dp", "tensor", None),
            P("dp", "tensor", None),
            P(),
            P(),
            P(None, "tensor"),
            P(None, None, "tensor"),
            P("tensor", None),
            P(None, "tensor"),
            P("tensor", None),
        ),
        check_vma=False,
    )
```
